128 devices in a mesh: tm: 16 (over x_hi, z, core), space: 8 (over y, x_lo).
Axes of the slice: x: 4 (x_hi: 2, x_lo: 2; x = x_hi * 2 + x_lo), y: 4, z: 4, core: 2. Of those that a mesh axis runs over, the one named last changes fastest.
Arguments:
- startup_condition: float32 [2, 32, 128, 128], P(None, 'space'), may hold values from -3 to 3
- slab_final_guess: float32 [16, 2, 32, 128, 128], P('tm', None, 'space'), may hold values from -4 to 4
- thermal_diffusivity_pair: float32 [2, 32, 128, 128], P(None, 'space'), may hold values from 0.25 to 2
- interphase_exchange_rate: float32 [32, 128, 128], P('space'), may hold values from 0.1 to 1
- inlet_stream_warmth: float32 [128, 128], replicated, may hold values from 1 to 3
Outputs:
- updated_c_points: float32 [16, 2, 32, 128, 128], P('tm', None, 'space')
The draws below stay inside these ranges and needn't reach their ends.
All inputs are finite; a program needn't handle non-finite values.
Results may differ from the reference program's by a relative error of at most 0.00002.
Values sent between devices are 32-bit elements; how exact they have to be, the bound alone decides.
No kernel may reach another device: no remote copies, remote signals or barrier semaphores. Data moves between devices by JAX's collectives and lax.ppermute only.
A program may use at most 64 MiB of HBM per device.

```python
import math
import jax
import jax.numpy as jnp
from jax import lax

MESH_ALONG_MIDDLE = 128
MESH_ALONG_LAST = 128
FINE_STEP_COUNT = 4
SWEEPS = 2
SLABS = 16
NX = 32


def draw_startup_condition(key, part):
    key = jax.random.fold_in(key, 11)
    values = jnp.clip(jax.random.normal(key, (2, NX, MESH_ALONG_MIDDLE, MESH_ALONG_LAST), jnp.float32), -3.0, 3.0)
    return values


def levels(key, shape, shards, low, largest):
    def one(dim, blocks):
        heights = jax.random.uniform(jax.random.fold_in(jax.random.fold_in(key, 6), dim), (blocks,), jnp.float32, low / len(shards), largest / len(shards))
        return jnp.repeat(jnp.exp(heights), shape[dim] // blocks).reshape((-1,) + (1,) * (len(shape) - dim - 1))

    level = one(*shards[0])
    for cut in shards[1:]:
        level = level * one(*cut)
    return level


def centred(rng, extent, width, limit, split=(), held_as=jnp.bfloat16):
    entries = width * jax.random.normal(rng, extent, jnp.float32)
    if split:
        entries = entries * levels(rng, extent, split, -0.22, 0.18)
    return jnp.clip(entries, -limit, limit).astype(held_as)


def setup_inputs(seed: int = 0) -> dict:
    streams_of = jax.random.split(jax.random.key(seed), 6)
    startup_condition = draw_startup_condition(jax.random.fold_in(streams_of[5], 71), 0)
    slab_final_guess = centred(streams_of[1], (SLABS, 2, NX, MESH_ALONG_MIDDLE, MESH_ALONG_LAST), 1.0, 4.0, ((0, 16), (2, 8)), jnp.float32)
    thermal_diffusivity_pair = jnp.clip(jnp.exp(math.log(2.0) - 2.0794415 * jax.random.uniform(streams_of[2], (2, NX, MESH_ALONG_MIDDLE, MESH_ALONG_LAST), jnp.float32) ** levels(streams_of[2], (2, NX, MESH_ALONG_MIDDLE, MESH_ALONG_LAST), ((1, 8),), -0.2, 0.2)), 0.25, 2.0)
    interphase_exchange_rate = jnp.clip(jnp.exp(math.log(1.0) - 2.3025851 * jax.random.uniform(streams_of[3], (NX, MESH_ALONG_MIDDLE, MESH_ALONG_LAST), jnp.float32) ** levels(streams_of[3], (NX, MESH_ALONG_MIDDLE, MESH_ALONG_LAST), ((0, 8),), -0.2, 0.2)), 0.1, 1.0)
    inlet_stream_warmth = jnp.clip(jax.random.uniform(streams_of[4], (MESH_ALONG_MIDDLE, MESH_ALONG_LAST), jnp.float32, 1.0, 3.0), 1.0, 3.0)
    return {"startup_condition": startup_condition, "slab_final_guess": slab_final_guess, "thermal_diffusivity_pair": thermal_diffusivity_pair, "interphase_exchange_rate": interphase_exchange_rate, "inlet_stream_warmth": inlet_stream_warmth}


rate_along = 4.0
rate_across = 0.5
advection = 1.0
damping = 0.8


def face_weights(conductance, coupling_field):
    centre = conductance[:, 1:-1]
    padded = jnp.pad(centre, ((0, 0), (0, 0), (1, 1), (1, 1)))
    upwind = jnp.array([0.0, advection], jnp.float32)[:, None, None, None]
    to_west = rate_along * 0.5 * (centre + conductance[:, :-2]) + upwind
    to_east = rate_along * 0.5 * (centre + conductance[:, 2:])
    to_south = rate_across * 0.5 * (centre + padded[:, :, :-2, 1:-1])
    to_north = rate_across * 0.5 * (centre + padded[:, :, 2:, 1:-1])
    to_below = rate_across * 0.5 * (centre + padded[:, :, 1:-1, :-2])
    to_above = rate_across * 0.5 * (centre + padded[:, :, 1:-1, 2:])
    weights = (to_west, to_east, to_south, to_north, to_below, to_above)
    outflow = to_west + to_east + to_south + to_north + to_below + to_above + coupling_field[None]
    return weights, outflow


def jacobi_sweep(weights, outflow, coupling_field, factor, widened, earlier):
    current = widened[:, 1:-1]
    padded = jnp.pad(widened, ((0, 0), (0, 0), (1, 1), (1, 1)))
    to_west, to_east, to_south, to_north, to_below, to_above = weights
    inflow = (to_west * padded[:, :-2, 1:-1, 1:-1] + to_east * padded[:, 2:, 1:-1, 1:-1]
              + to_south * padded[:, 1:-1, :-2, 1:-1] + to_north * padded[:, 1:-1, 2:, 1:-1]
              + to_below * padded[:, 1:-1, 1:-1, :-2] + to_above * padded[:, 1:-1, 1:-1, 2:])
    inflow = inflow + coupling_field[None] * current[::-1]
    pivot_value = 1.0 + factor * outflow
    defect = earlier + factor * inflow - pivot_value * current
    return current + damping * defect / pivot_value


def reference(startup_condition, slab_final_guess, thermal_diffusivity_pair, interphase_exchange_rate, inlet_stream_warmth):
    conductance = jnp.pad(thermal_diffusivity_pair, ((0, 0), (1, 1), (0, 0), (0, 0)))
    weights, outflow = face_weights(conductance, interphase_exchange_rate)
    upstream_ghost_layer = jnp.stack([jnp.zeros_like(inlet_stream_warmth), inlet_stream_warmth])[:, None]
    right_ghost = jnp.zeros_like(upstream_ghost_layer)
    coarse_factor = float(FINE_STEP_COUNT)

    def advance(earlier, factor):
        current = earlier
        for sweep_index in range(SWEEPS):
            widened = jnp.concatenate([upstream_ghost_layer, current, right_ghost], axis=1)
            current = jacobi_sweep(weights, outflow, interphase_exchange_rate, factor, widened, earlier)
        return current

    def relax_slab(slab_begin):
        fine_state = slab_begin
        for step_index in range(FINE_STEP_COUNT):
            fine_state = advance(fine_state, 1.0)
        return fine_state - advance(slab_begin, coarse_factor)

    slab_begins = jnp.concatenate([startup_condition[None], slab_final_guess[:-1]], axis=0)
    tau_terms = lax.map(relax_slab, slab_begins)

    def coarse_step(current, tau_term):
        following = advance(current, coarse_factor) + tau_term
        return following, following

    final_state, updated_c_points = lax.scan(coarse_step, startup_condition, tau_terms)
    return updated_c_points
```

```python
import jax
import jax.numpy as jnp
from jax import lax
from jax.experimental import pallas as pl
from jax.experimental.pallas import tpu as pltpu
from jax.sharding import Mesh, PartitionSpec as P

SLABS = 16
BRICKS = 8
PLANES = 4
NX = 32
MIDDLE = 128
LAST = 128
STRIP = 16
HALF = 8
REACH = 10
EDGE = 16
ROWS = STRIP + 2 * EDGE
FRAME = HALF + 2 * EDGE
PART = ROWS // 2

RATE_ALONG = 4.0
RATE_ACROSS = 0.5
ADVECTION = 1.0
DAMPING = 0.8
COARSE = 4.0

ORDER = [0, 2, 4, 6, 7, 5, 3, 1]
AXES = ("chip", "core", "space")
MIB = 1 << 20

VMEM = pl.BlockSpec(memory_space=pltpu.VMEM)
SMEM = pl.BlockSpec(memory_space=pltpu.SMEM)
ANY = pl.BlockSpec(memory_space=pl.ANY)
F32 = jnp.float32


def shape(*dims):
    return jax.ShapeDtypeStruct(dims, F32)


def call(body, outs, in_specs, out_specs, scratch, limit, flops=1 << 20):
    return pl.pallas_call(
        body,
        out_shape=outs,
        in_specs=in_specs,
        out_specs=out_specs,
        scratch_shapes=scratch,
        compiler_params=pltpu.CompilerParams(vmem_limit_bytes=limit * MIB),
    )


def pack_kernel(where, guess, startup, conduct, couple, out, padded):
    core, slab = where[0], where[2]
    last = slab == SLABS - 1
    zero = jnp.zeros((EDGE * PLANES, LAST), F32)
    end = (EDGE + MIDDLE) * PLANES
    for i in range(5):
        padded[i, 0 : EDGE * PLANES] = zero
        padded[i, end : end + EDGE * PLANES] = zero
        for plane in range(PLANES):
            for first in range(0, MIDDLE, 8):
                rows = pl.ds(first, 8)
                if i < 2:
                    value = jnp.where(last, startup[i, plane, rows], guess[i, plane, rows])
                elif i < 4:
                    value = conduct[i - 2, plane, rows]
                else:
                    value = couple[plane, rows]
                padded[i, pl.ds((EDGE + first) * PLANES + plane, 8, stride=PLANES), :] = value
    tall, part = (STRIP + 2 * REACH) * PLANES, PART * PLANES
    for b in range(BRICKS):
        s = ORDER[b]
        start = (EDGE + STRIP * b - REACH) * PLANES
        for i in range(2):
            out[s, i * tall : (i + 1) * tall] = padded[i, start : start + tall]
        start = pl.multiple_of(STRIP * b * PLANES + part * core, 32)
        for i in range(3):
            at = 2 * tall + i * part
            out[s, at : at + part] = padded[2 + i, pl.ds(start, part)]


def unpack_kernel(got, state, coefficients):
    low = lax.broadcasted_iota(jnp.int32, (8, LAST), 0) < PLANES

    def widen(out, i, at, rows):
        for y in range(0, rows, 2):
            for t in range(NX // 8):
                a = got[2 * t, at + PLANES * y : at + PLANES * y + 8]
                b = got[2 * t + 1, at + PLANES * y : at + PLANES * y + 8]
                out[i, y, 8 * t : 8 * t + 8] = jnp.where(low, a, pltpu.roll(b, 4, 0))
                out[i, y + 1, 8 * t : 8 * t + 8] = jnp.where(low, pltpu.roll(a, 4, 0), b)

    tall, part = (STRIP + 2 * REACH) * PLANES, PART * PLANES
    for i in range(2):
        widen(state, i, i * tall, STRIP + 2 * REACH)
    for i in range(3):
        widen(coefficients, i, 2 * tall + i * part, PART)


def restore_kernel(got, out):
    for core in range(2):
        for b in range(BRICKS):
            source = core * BRICKS + ORDER[b]
            first = STRIP * b + HALF * core
            for i in range(2):
                for plane in range(PLANES):
                    out[0, i, plane, first : first + HALF] = got[
                        source, pl.ds(i * HALF * PLANES + plane, HALF, stride=PLANES), :
                    ]


def row_sweep(y, state, weights, earlier, opening, source):
    centre = (state[0, y], state[1, y])
    out = []
    for i in range(2):
        v = centre[i]
        w = lambda k: weights[y, 8 * i + k]
        along = w(0) * pltpu.roll(v, 1, 0) + w(1) * pltpu.roll(v, NX - 1, 0)
        middle = w(2) * state[i, y - 1] + w(3) * state[i, y + 1]
        across = w(4) * pltpu.roll(v, 1, 1) + w(5) * pltpu.roll(v, LAST - 1, 1)
        rest = w(6) * centre[1 - i]
        if opening:
            rest = rest + (0.2 + w(7)) * v
        else:
            rest = rest + 0.2 * v + w(7) * earlier[i, y]
        new = (along + middle) + (across + rest)
        if i == 1 and source is not None:
            new = jnp.concatenate([new[:8] + source[y], new[8:]], axis=0)
        out.append(new)
    return out


def sweep(state, weights, earlier, into, low, high, opening, source=None, unroll=4):
    def step(k, carry):
        for u in range(unroll):
            y = low + unroll * k + u
            new = row_sweep(y, state, weights, earlier, opening, source)
            into[0, y] = new[0]
            into[1, y] = new[1]
        return carry

    lax.fori_loop(0, (high - low + unroll - 1) // unroll, step, 0)


def advances(count, e, v, weights, low, high, source=None):
    def step(m, carry):
        sweep(e, weights, None, v, low + 2 * m + 1, high - 2 * m - 1, True, source)
        sweep(v, weights, e, e, low + 2 * m + 2, high - 2 * m - 2, False, source)
        return carry

    lax.fori_loop(0, count, step, 0)


def relax_kernel(where, begin, mine, other, inlet, w_out, base, give, own, c, w1, w4, feed, e, v, e0, sem):
    core, strip, slab = where[0], where[1], where[2]
    c[:, pl.ds(PART * core, PART)] = mine[...]
    c[:, pl.ds(PART - PART * core, PART)] = other[...]
    first = EDGE - REACH
    e[:, first : first + STRIP + 2 * REACH] = begin[...]
    e0[:, first : first + STRIP + 2 * REACH] = begin[...]

    plane = lax.broadcasted_iota(jnp.int32, (NX, LAST), 0)
    column = lax.broadcasted_iota(jnp.int32, (NX, LAST), 1)
    top = lax.broadcasted_iota(jnp.int32, (8, LAST), 0) == 0

    def weigh(r, carry):
        y = strip * STRIP - EDGE + r
        lower = jnp.where(y == 0, 0.0, 1.0).astype(F32)
        upper = jnp.where(y == MIDDLE - 1, 0.0, 1.0).astype(F32)
        exchange = c[2, r]
        warmth = inlet[pl.ds(jnp.clip(y, 0, MIDDLE - 1), 1), :]
        for i in range(2):
            here = c[i, r]
            xm = jnp.where(plane == 0, 0.0, pltpu.roll(here, 1, 0))
            xp = jnp.where(plane == NX - 1, 0.0, pltpu.roll(here, NX - 1, 0))
            zm = jnp.where(column == 0, 0.0, pltpu.roll(here, 1, 1))
            zp = jnp.where(column == LAST - 1, 0.0, pltpu.roll(here, LAST - 1, 1))
            half_along, half_across = 0.5 * RATE_ALONG, 0.5 * RATE_ACROSS
            wxm = half_along * (here + xm)
            if i == 1:
                wxm = wxm + ADVECTION
            wxp = half_along * (here + xp)
            wym = half_across * (here + c[i, r - 1])
            wyp = half_across * (here + c[i, r + 1])
            wzm = half_across * (here + zm)
            wzp = half_across * (here + zp)
            outflow = wxm + wxp + wym + wyp + wzm + wzp + exchange
            inner = (
                jnp.where(plane == 0, 0.0, wxm),
                jnp.where(plane == NX - 1, 0.0, wxp),
                wym * lower,
                wyp * upper,
                jnp.where(column == 0, 0.0, wzm),
                jnp.where(column == LAST - 1, 0.0, wzp),
                exchange,
            )
            for factor, w in ((1.0, w1), (COARSE, w4)):
                q = DAMPING / (1.0 + factor * outflow)
                fq = factor * q if factor != 1.0 else q
                for k in range(7):
                    w[r, 8 * i + k] = fq * inner[k]
                w[r, 8 * i + 7] = q
                if i == 1 and factor == 1.0:
                    feed[r] = jnp.where(top, (fq * wxm)[:8] * warmth, 0.0)
        return carry

    lax.fori_loop(1, ROWS - 1, weigh, 0)
    spill = pltpu.make_async_copy(w4.at[pl.ds(HALF * core, FRAME)], w_out, sem)
    spill.start()

    sweep(e0, w4, None, v, EDGE - 3, EDGE + STRIP + 3, True)
    sweep(v, w4, e0, e0, EDGE - 2, EDGE + STRIP + 2, False)
    advances(4, e, v, w1, first, first + STRIP + 2 * REACH, feed)
    keep = jnp.where(slab == SLABS - 1, 0.0, 1.0).astype(F32)
    rows = pl.ds(EDGE - 2, STRIP + 4)
    e[:, rows] = e[:, rows] - keep * e0[:, rows]
    sweep(e, w4, None, v, EDGE - 1, EDGE + STRIP + 1, True)
    sweep(v, w4, e, e0, EDGE, EDGE + STRIP, False)
    joined = jnp.where(slab == SLABS - 2, 0.0, 1.0).astype(F32)
    near, far = pl.ds(EDGE, HALF), pl.ds(EDGE + HALF, HALF)
    base[...] = jnp.where(core == 0, joined * e0[:, near], e[:, far])
    give[...] = jnp.where(core == 0, joined * e0[:, far], e[:, near])
    own[:, :HALF] = e[:, near]
    own[:, HALF:] = e[:, far]
    spill.wait()


def load_weights(w_hbm, w, low, high, sem):
    copy = pltpu.make_async_copy(w_hbm.at[pl.ds(low, high - low)], w.at[pl.ds(low, high - low)], sem)
    copy.start()
    return copy


def place(core, e, inward, outward, distance):
    e[:, pl.ds(EDGE + distance - 2 * distance * core, HALF)] = inward[...]
    e[:, pl.ds(EDGE - distance + 2 * distance * core, HALF)] = outward[...]


def far_kernel(where, own, near, far, swapped, swapped_near, local, w_hbm, out, w, e, v, sem):
    core = where[0]
    copy = load_weights(w_hbm, w, 0, FRAME, sem)
    e[:, EDGE : EDGE + HALF] = own[...]
    place(core, e, swapped, near, HALF)
    place(core, e, swapped_near, far, 2 * HALF)
    copy.wait()
    advances(8, e, v, w, 0, FRAME)
    out[...] = local[...] + e[:, EDGE : EDGE + HALF]


def mid_kernel(where, own, near, swapped, local, w_hbm, out, inner, outer, w, e, v, sem):
    core = where[0]
    copy = load_weights(w_hbm, w, HALF, FRAME - HALF, sem)
    e[:, EDGE : EDGE + HALF] = own[...]
    place(core, e, swapped, near, HALF)
    copy.wait()
    advances(4, e, v, w, EDGE - 8, EDGE + HALF + 8)
    out[...] = local[...] + e[:, EDGE : EDGE + HALF]
    inner[...] = out[:, pl.ds(6 - 6 * core, 2)]
    outer[...] = out[:, pl.ds(6 * core, 2)]


def last_kernel(where, own, near, swapped, c_own, c_near, c_swapped, g, w_hbm, out, w, e, v, r, sem):
    core = where[0]
    copy = load_weights(w_hbm, w, HALF, FRAME - HALF, sem)
    e[:, EDGE : EDGE + HALF] = own[...]
    place(core, e, swapped, near, HALF)
    r[:, EDGE : EDGE + HALF] = c_own[...]
    r[:, pl.ds(EDGE + HALF - 10 * core, 2)] = c_swapped[...]
    r[:, pl.ds(EDGE - 2 + 10 * core, 2)] = c_near[...]
    copy.wait()
    advances(2, e, v, w, EDGE - 6, EDGE + HALF + 6)
    rows = pl.ds(EDGE - 2, HALF + 4)
    r[:, rows] = r[:, rows] + e[:, rows]
    sweep(r, w, None, v, EDGE - 1, EDGE + HALF + 1, True)
    sweep(v, w, r, e, EDGE, EDGE + HALF, False)
    rows = pl.ds(EDGE, HALF)
    e[:, rows] = e[:, rows] + g[...]
    low = lax.broadcasted_iota(jnp.int32, (8, LAST), 0) < PLANES
    for label, source in ((0, r), (1, e)):
        for i in range(2):
            for y in range(0, HALF, 2):
                at = (i * HALF + y) * PLANES
                for t in range(NX // 8):
                    a = source[i, EDGE + y, 8 * t : 8 * t + 8]
                    b = source[i, EDGE + y + 1, 8 * t : 8 * t + 8]
                    out[label * BRICKS + 2 * t, at : at + 8] = jnp.where(low, a, pltpu.roll(b, 4, 0))
                    out[label * BRICKS + 2 * t + 1, at : at + 8] = jnp.where(low, pltpu.roll(a, 4, 0), b)


def index(chip, core, strip):
    return (chip * 2 + core) * BRICKS + ORDER[strip]


def sent(value, chips, flip, shift):
    pairs = []
    for source, target in chips:
        for core in range(2):
            for strip in range(BRICKS):
                beside = strip + shift * (1 if core == 0 else -1)
                if 0 <= beside < BRICKS:
                    pairs.append((index(source, core ^ flip, strip), index(target, core, beside)))
    return lax.ppermute(value, AXES, pairs)


SAME = [(c, c) for c in range(8)]
LEAP_FOUR = [((c - 4) % 8, c) for c in range(3, 7)]
LEAP_TWO = [((c - 2) % 8, c) for c in range(1, 7)]
HOME = [((c - 1) % 8, c) for c in range(8)]
HOME_ONE = [((c - 2) % 8, c) for c in range(1, 8)]


def swap(value):
    return sent(value, SAME, 1, 0)


def shards(startup, guess, conduct, couple, inlet):
    chip, core, space = (lax.axis_index(a) for a in AXES)
    slab = chip * 2 + core
    strip = jnp.take(jnp.array([ORDER.index(s) for s in range(BRICKS)], jnp.int32), space)
    where = jnp.stack([core, strip, slab]).astype(jnp.int32)

    tall = STRIP + 2 * REACH
    chunk = (2 * tall + 3 * PART) * PLANES
    half = shape(2, HALF, NX, LAST)
    packed = call(
        pack_kernel,
        shape(BRICKS, chunk, LAST),
        [SMEM] + [VMEM] * 4,
        VMEM,
        [pltpu.VMEM((5, (MIDDLE + 2 * EDGE) * PLANES, LAST), F32)],
        16,
    )(where, guess[0], startup, conduct, couple)
    got = lax.all_to_all(packed, "space", 0, 0, tiled=True)
    begin, mine = call(
        unpack_kernel, (shape(2, tall, NX, LAST), shape(3, PART, NX, LAST)), [VMEM], (VMEM, VMEM), [], 16
    )(got)
    other = swap(mine)

    field = pltpu.VMEM((2, ROWS + 4, NX, LAST), F32)
    w_all = pltpu.VMEM((ROWS, 16, NX, LAST), F32)
    weights, base, give, g = call(
        relax_kernel,
        (shape(FRAME, 16, NX, LAST), half, half, shape(2, STRIP, NX, LAST)),
        [SMEM] + [VMEM] * 4,
        (ANY, VMEM, VMEM, VMEM),
        [
            pltpu.VMEM((3, ROWS, NX, LAST), F32),
            w_all,
            w_all,
            pltpu.VMEM((ROWS, 8, LAST), F32),
            field,
            field,
            field,
            pltpu.SemaphoreType.DMA,
        ],
        48,
    )(where, begin, mine, other, inlet)
    u = base + swap(give)
    g_far = sent(g[:, HALF:], SAME, 1, 0)
    g_half = jnp.where(core == 0, g[:, :HALF], g_far)

    frame = pltpu.VMEM((2, FRAME + 4, NX, LAST), F32)
    w_frame = pltpu.VMEM((FRAME + 4, 16, NX, LAST), F32)
    own = sent(u, LEAP_FOUR, 0, 0)
    near = sent(u, LEAP_FOUR, 1, 1)
    far = sent(u, LEAP_FOUR, 0, 1)
    x = call(
        far_kernel,
        half,
        [SMEM] + [VMEM] * 6 + [ANY],
        VMEM,
        [w_frame, frame, frame, pltpu.SemaphoreType.DMA],
        32,
    )(where, own, near, far, swap(own), swap(near), u, weights)

    own = sent(x, LEAP_TWO, 0, 0)
    near = sent(x, LEAP_TWO, 1, 1)
    rim = shape(2, 2, NX, LAST)
    y, inner, outer = call(
        mid_kernel,
        (half, rim, rim),
        [SMEM] + [VMEM] * 4 + [ANY],
        (VMEM,) * 3,
        [w_frame, frame, frame, pltpu.SemaphoreType.DMA],
        32,
    )(where, own, near, swap(own), x, weights)

    own = sent(y, HOME_ONE, 0, 0)
    near = sent(y, HOME_ONE, 1, 1)
    c_own = sent(y, HOME, 0, 0)
    c_near = sent(outer, HOME, 1, 1)
    c_swapped = sent(inner, HOME, 1, 0)
    done = call(
        last_kernel,
        shape(2 * BRICKS, 2 * HALF * PLANES, LAST),
        [SMEM] + [VMEM] * 7 + [ANY],
        VMEM,
        [w_frame, frame, frame, frame, pltpu.SemaphoreType.DMA],
        32,
    )(where, own, near, swap(own), c_own, c_near, c_swapped, g_half, weights)
    back = lax.all_to_all(done, ("core", "space"), 0, 0, tiled=True)
    return call(restore_kernel, shape(1, 2, PLANES, MIDDLE, LAST), [VMEM], VMEM, [], 16)(back)


def solution(mesh):
    fine = Mesh(mesh.devices.reshape(SLABS // 2, 2, BRICKS), AXES)
    slabs = ("chip", "core")
    return jax.shard_map(
        shards,
        mesh=fine,
        in_specs=(
            P(None, "space", None, None),
            P(slabs, None, "space", None, None),
            P(None, "space", None, None),
            P("space", None, None),
            P(),
        ),
        out_specs=P(slabs, None, "space", None, None),
        check_vma=False,
    )
```

```python
import jax
import jax.numpy as jnp
from jax import lax
from jax.experimental import pallas as pl
from jax.experimental.pallas import tpu as pltpu
from jax.sharding import Mesh, PartitionSpec as P

SLABS = 16
BRICKS = 8
PLANES = 4
NX = 32
MIDDLE = 128
LAST = 128
STRIP = 16
HALF = 8
REACH = 10
EDGE = 16
ROWS = STRIP + 2 * EDGE
HELD = ROWS + 4
PART = ROWS // 2

RATE_ALONG = 4.0
RATE_ACROSS = 0.5
ADVECTION = 1.0
DAMPING = 0.8
COARSE = 4.0

ORDER = [0, 2, 4, 6, 7, 5, 3, 1]
AXES = ("chip", "core", "space")
MIB = 1 << 20

VMEM = pl.BlockSpec(memory_space=pltpu.VMEM)
HBM = pl.BlockSpec(memory_space=pltpu.HBM)
F32 = jnp.float32


def shape(*dims):
    return jax.ShapeDtypeStruct(dims, F32)


def call(body, outs, in_specs, out_specs, scratch, limit, flops=0):
    return pl.pallas_call(
        body,
        cost_estimate=pl.CostEstimate(flops=flops, bytes_accessed=1 << 20, transcendentals=0) if flops else None,
        out_shape=outs,
        in_specs=in_specs,
        out_specs=out_specs,
        scratch_shapes=scratch,
        compiler_params=pltpu.CompilerParams(vmem_limit_bytes=limit * MIB),
    )


def position():
    chip, core, space = (lax.axis_index(a) for a in AXES)
    y, odd = space // 2, space % 2
    return core, jnp.where(odd == 0, y, BRICKS - 1 - y), chip * 2 + core


def pack_kernel(startup, guess, conduct, couple, out, padded, state, others, sems):
    core, _, slab = position()
    last = slab == SLABS - 1
    from_startup = [pltpu.make_async_copy(startup.at[i], state.at[i], sems.at[i]) for i in range(2)]
    from_guess = [pltpu.make_async_copy(guess.at[0, i], state.at[i], sems.at[i]) for i in range(2)]
    copies = [pltpu.make_async_copy(conduct.at[i], others.at[i], sems.at[2 + i]) for i in range(2)]
    copies.append(pltpu.make_async_copy(couple, others.at[2], sems.at[4]))

    @pl.when(last)
    def _():
        for copy in from_startup:
            copy.start()

    @pl.when(jnp.logical_not(last))
    def _():
        for copy in from_guess:
            copy.start()

    for copy in copies:
        copy.start()
    zero = jnp.zeros((EDGE * PLANES, LAST), F32)
    end = (EDGE + MIDDLE) * PLANES
    for i in range(5):
        padded[i, 0 : EDGE * PLANES] = zero
        padded[i, end : end + EDGE * PLANES] = zero
        (from_guess + copies)[i].wait()
        for plane in range(PLANES):
            for first in range(0, MIDDLE, 8):
                value = state[i, plane, first : first + 8] if i < 2 else others[i - 2, plane, first : first + 8]
                padded[i, pl.ds((EDGE + first) * PLANES + plane, 8, stride=PLANES), :] = value
    tall, part = (STRIP + 2 * REACH) * PLANES, PART * PLANES
    for b in range(BRICKS):
        s = ORDER[b]
        start = (EDGE + STRIP * b - REACH) * PLANES
        for i in range(2):
            out[s, i * tall : (i + 1) * tall] = padded[i, start : start + tall]
        start = pl.multiple_of(STRIP * b * PLANES + part * core, 32)
        for i in range(3):
            at = 2 * tall + i * part
            out[s, at : at + part] = padded[2 + i, pl.ds(start, part)]


def unpack_kernel(got, state, coefficients):
    low = lax.broadcasted_iota(jnp.int32, (8, LAST), 0) < PLANES

    def widen(out, i, at, rows):
        for y in range(0, rows, 2):
            for t in range(NX // 8):
                a = got[2 * t, at + PLANES * y : at + PLANES * y + 8]
                b = got[2 * t + 1, at + PLANES * y : at + PLANES * y + 8]
                out[i, y, 8 * t : 8 * t + 8] = jnp.where(low, a, pltpu.roll(b, 4, 0))
                out[i, y + 1, 8 * t : 8 * t + 8] = jnp.where(low, pltpu.roll(a, 4, 0), b)

    tall, part = (STRIP + 2 * REACH) * PLANES, PART * PLANES
    for i in range(2):
        widen(state, i, i * tall, STRIP + 2 * REACH)
    for i in range(3):
        widen(coefficients, i, 2 * tall + i * part, PART)


def restore_kernel(got, out):
    core, _, _ = position()
    for part in range(2):
        half = core if part == 0 else 1 - core
        for b in range(BRICKS):
            first = pl.multiple_of(STRIP * b + HALF * half, HALF)
            for i in range(2):
                for plane in range(PLANES):
                    at = (part * 2 + i) * HALF * PLANES + plane
                    out[0, i, plane, pl.ds(first, HALF), :] = got[ORDER[b], pl.ds(at, HALF, stride=PLANES), :]


def row_sweep(y, state, weights, earlier, opening, source):
    centre = (state[0, y], state[1, y])
    out = []
    for i in range(2):
        v = centre[i]
        w = lambda k: weights[y, 8 * i + k]
        along = w(0) * pltpu.roll(v, 1, 0) + w(1) * pltpu.roll(v, NX - 1, 0)
        middle = w(2) * state[i, y - 1] + w(3) * state[i, y + 1]
        across = w(4) * pltpu.roll(v, 1, 1) + w(5) * pltpu.roll(v, LAST - 1, 1)
        rest = w(6) * centre[1 - i]
        if opening:
            rest = rest + (0.2 + w(7)) * v
        else:
            rest = rest + 0.2 * v + w(7) * earlier[i, y]
        new = (along + middle) + (across + rest)
        if i == 1 and source is not None:
            new = jnp.concatenate([new[:8] + source[y], new[8:]], axis=0)
        out.append(new)
    return out


def sweep(state, weights, earlier, into, low, high, opening, source=None, unroll=4):
    def step(k, carry):
        for u in range(unroll):
            y = low + unroll * k + u
            new = row_sweep(y, state, weights, earlier, opening, source)
            into[0, y] = new[0]
            into[1, y] = new[1]
        return carry

    lax.fori_loop(0, (high - low + unroll - 1) // unroll, step, 0)


def advances(count, e, v, weights, low, high, source=None):
    def step(m, carry):
        sweep(e, weights, None, v, low + 2 * m + 1, high - 2 * m - 1, True, source)
        sweep(v, weights, e, e, low + 2 * m + 2, high - 2 * m - 2, False, source)
        return carry

    lax.fori_loop(0, count, step, 0)


def relax_kernel(begin, mine, other, inlet, w4, base, give, own, c, w1, feed, e, v, e0):
    core, strip, slab = position()
    c[:, pl.ds(PART * core, PART)] = mine[...]
    c[:, pl.ds(PART - PART * core, PART)] = other[...]
    first = EDGE - REACH
    e[:, first : first + STRIP + 2 * REACH] = begin[...]
    e0[:, first : first + STRIP + 2 * REACH] = begin[...]

    plane = lax.broadcasted_iota(jnp.int32, (NX, LAST), 0)
    column = lax.broadcasted_iota(jnp.int32, (NX, LAST), 1)
    top = lax.broadcasted_iota(jnp.int32, (8, LAST), 0) == 0

    def weigh(r, carry):
        y = strip * STRIP - EDGE + r
        lower = jnp.where(y == 0, 0.0, 1.0).astype(F32)
        upper = jnp.where(y == MIDDLE - 1, 0.0, 1.0).astype(F32)
        exchange = c[2, r]
        warmth = inlet[pl.ds(jnp.clip(y, 0, MIDDLE - 1), 1), :]
        for i in range(2):
            here = c[i, r]
            xm = jnp.where(plane == 0, 0.0, pltpu.roll(here, 1, 0))
            xp = jnp.where(plane == NX - 1, 0.0, pltpu.roll(here, NX - 1, 0))
            zm = jnp.where(column == 0, 0.0, pltpu.roll(here, 1, 1))
            zp = jnp.where(column == LAST - 1, 0.0, pltpu.roll(here, LAST - 1, 1))
            half_along, half_across = 0.5 * RATE_ALONG, 0.5 * RATE_ACROSS
            wxm = half_along * (here + xm)
            if i == 1:
                wxm = wxm + ADVECTION
            wxp = half_along * (here + xp)
            wym = half_across * (here + c[i, r - 1])
            wyp = half_across * (here + c[i, r + 1])
            wzm = half_across * (here + zm)
            wzp = half_across * (here + zp)
            outflow = wxm + wxp + wym + wyp + wzm + wzp + exchange
            inner = (
                jnp.where(plane == 0, 0.0, wxm),
                jnp.where(plane == NX - 1, 0.0, wxp),
                wym * lower,
                wyp * upper,
                jnp.where(column == 0, 0.0, wzm),
                jnp.where(column == LAST - 1, 0.0, wzp),
                exchange,
            )
            for factor, w in ((1.0, w1), (COARSE, w4)):
                q = DAMPING / (1.0 + factor * outflow)
                fq = factor * q if factor != 1.0 else q
                for k in range(7):
                    w[r, 8 * i + k] = fq * inner[k]
                w[r, 8 * i + 7] = q
                if i == 1 and factor == 1.0:
                    feed[r] = jnp.where(top, (fq * wxm)[:8] * warmth, 0.0)
        return carry

    lax.fori_loop(1, ROWS - 1, weigh, 0)
    sweep(e0, w4, None, v, EDGE - 3, EDGE + STRIP + 3, True)
    sweep(v, w4, e0, e0, EDGE - 2, EDGE + STRIP + 2, False)
    advances(4, e, v, w1, first, first + STRIP + 2 * REACH, feed)
    keep = jnp.where(slab == SLABS - 1, 0.0, 1.0).astype(F32)
    rows = pl.ds(EDGE - 2, STRIP + 4)
    e[:, rows] = e[:, rows] - keep * e0[:, rows]
    sweep(e, w4, None, v, EDGE - 1, EDGE + STRIP + 1, True)
    sweep(v, w4, e, e0, EDGE, EDGE + STRIP, False)
    joined = jnp.where(slab == SLABS - 2, 0.0, 1.0).astype(F32)
    near, far = pl.ds(EDGE, HALF), pl.ds(EDGE + HALF, HALF)
    base[...] = jnp.where(core == 0, joined * e0[:, near], e[:, far])
    give[0:2] = jnp.where(core == 0, joined * e0[:, far], e[:, near])
    give[2:4] = e[:, far]
    own[...] = e[:, near]


def place(core, e, middle, inward, outward, distance):
    step = distance * (1 - 2 * core)
    e[:, pl.ds(middle + step, inward.shape[1])] = inward[...]
    e[:, pl.ds(middle - step, outward.shape[1])] = outward[...]


def far_kernel(own, near, far, swapped, swapped_near, w, out, e, v):
    core, _, _ = position()
    middle = EDGE + HALF * core
    rows = pl.ds(middle, HALF)
    e[:, rows] = own[...]
    place(core, e, middle, swapped, near, HALF)
    place(core, e, middle, swapped_near, far, 2 * HALF)
    advances(8, e, v, w, middle - 16, middle + HALF + 16)
    out[...] = e[:, rows]


def mid_kernel(own, near, swapped, local, w, out, inner, outer, e, v):
    core, _, _ = position()
    middle = EDGE + HALF * core
    rows = pl.ds(middle, HALF)
    e[:, rows] = own[...]
    place(core, e, middle, swapped, near, HALF)
    advances(4, e, v, w, middle - 8, middle + HALF + 8)
    out[...] = local[...] + e[:, rows]
    inner[...] = out[:, pl.ds(6 - 6 * core, 2)]
    outer[...] = out[:, pl.ds(6 * core, 2)]


def last_kernel(own, near, swapped, c_own, c_near, c_swapped, g, taken, w, keep, send, e, v, r):
    core, _, _ = position()
    middle = EDGE + HALF * core
    rows = pl.ds(middle, HALF)
    e[:, rows] = own[...]
    place(core, e, middle, swapped, near, HALF)
    r[:, rows] = c_own[...]
    r[:, pl.ds(middle + HALF - 10 * core, 2)] = c_swapped[...]
    r[:, pl.ds(middle - 2 + 10 * core, 2)] = c_near[...]
    advances(2, e, v, w, middle - 6, middle + HALF + 6)
    wide = pl.ds(middle - 2, HALF + 4)
    r[:, wide] = r[:, wide] + e[:, wide]
    sweep(r, w, None, v, middle - 1, middle + HALF + 1, True)
    sweep(v, w, r, e, middle, middle + HALF, False)
    e[:, rows] = e[:, rows] + jnp.where(core == 0, g[...], taken[2:4])
    low = lax.broadcasted_iota(jnp.int32, (8, LAST), 0) < PLANES
    for out, other in ((keep, 0), (send, 1)):
        pick = lambda *at: jnp.where(core == other, r[at], e[at])
        for i in range(2):
            for y in range(0, HALF, 2):
                at = (i * HALF + y) * PLANES
                for t in range(NX // 8):
                    a = pick(i, middle + y, slice(8 * t, 8 * t + 8))
                    b = pick(i, middle + y + 1, slice(8 * t, 8 * t + 8))
                    out[2 * t, at : at + 8] = jnp.where(low, a, pltpu.roll(b, 4, 0))
                    out[2 * t + 1, at : at + 8] = jnp.where(low, pltpu.roll(a, 4, 0), b)


def index(chip, core, strip):
    return (chip * 2 + core) * BRICKS + ORDER[strip]


def sent(value, chips, flip, shift):
    pairs = []
    for source, target in chips:
        for core in range(2):
            for strip in range(BRICKS):
                beside = strip + shift * (1 if core == 0 else -1)
                if 0 <= beside < BRICKS:
                    pairs.append((index(source, core ^ flip, strip), index(target, core, beside)))
    return lax.ppermute(value, AXES, pairs)


SAME = [(c, c) for c in range(8)]
HOME = [((c - 1) % 8, c) for c in range(8)]
LEAP_FOUR = [((c - 5) % 8, c) for c in range(4, 8)]
LEAP_TWO = [(c - 2, c) for c in range(2, 8)]
LEAP_ONE = [(c - 1, c) for c in range(1, 8)]


def swap(value):
    return sent(value, SAME, 1, 0)


def shards(startup, guess, conduct, couple, inlet):
    tall = STRIP + 2 * REACH
    chunk = (2 * tall + 3 * PART) * PLANES
    half = shape(2, HALF, NX, LAST)
    packed = call(
        pack_kernel,
        shape(BRICKS, chunk, LAST),
        [HBM] * 4,
        VMEM,
        [
            pltpu.VMEM((5, (MIDDLE + 2 * EDGE) * PLANES, LAST), F32),
            pltpu.VMEM((2, PLANES, MIDDLE, LAST), F32),
            pltpu.VMEM((3, PLANES, MIDDLE, LAST), F32),
            pltpu.SemaphoreType.DMA((5,)),
        ],
        16,
    )(startup, guess, conduct, couple)
    got = lax.all_to_all(packed, "space", 0, 0, tiled=True)
    begin, mine = call(
        unpack_kernel, (shape(2, tall, NX, LAST), shape(3, PART, NX, LAST)), [VMEM], (VMEM, VMEM), [], 16
    )(got)
    other = swap(mine)

    field = pltpu.VMEM((2, HELD, NX, LAST), F32)
    weights, base, give, g = call(
        relax_kernel,
        (shape(HELD, 16, NX, LAST), half, shape(4, HALF, NX, LAST), half),
        [VMEM] * 4,
        (VMEM,) * 4,
        [
            pltpu.VMEM((3, ROWS, NX, LAST), F32),
            pltpu.VMEM((HELD, 16, NX, LAST), F32),
            pltpu.VMEM((HELD, 8, LAST), F32),
            field,
            field,
            field,
        ],
        42,
    )(begin, mine, other, inlet)
    taken = swap(give)
    u = base + taken[:2]

    own = sent(u, LEAP_FOUR, 0, 0)
    near = sent(u, LEAP_FOUR, 1, 1)
    far = sent(u, LEAP_FOUR, 0, 1)
    local = sent(u, HOME, 0, 0)
    x = call(far_kernel, half, [VMEM] * 6, VMEM, [field, field], 26, 1 << 27)(
        own, near, far, swap(own), swap(near), weights
    )
    x = x + local

    own = sent(x, LEAP_TWO, 0, 0)
    near = sent(x, LEAP_TWO, 1, 1)
    rim = shape(2, 2, NX, LAST)
    y, inner, outer = call(mid_kernel, (half, rim, rim), [VMEM] * 5, (VMEM,) * 3, [field, field], 26)(
        own, near, swap(own), x, weights
    )

    own = sent(y, LEAP_ONE, 0, 0)
    near = sent(y, LEAP_ONE, 1, 1)
    c_near = sent(outer, SAME, 1, 1)
    parcel = shape(BRICKS, 2 * HALF * PLANES, LAST)
    keep, send = call(last_kernel, (parcel, parcel), [VMEM] * 9, (VMEM,) * 2, [field, field, field], 26)(
        own, near, swap(own), y, c_near, swap(inner), g, taken, weights
    )
    back = lax.all_to_all(jnp.concatenate([keep, swap(send)], axis=1), "space", 0, 0, tiled=True)
    return call(restore_kernel, shape(1, 2, PLANES, MIDDLE, LAST), [VMEM], VMEM, [], 16)(back)


def solution(mesh):
    fine = Mesh(mesh.devices.reshape(SLABS // 2, 2, BRICKS), AXES)
    slabs = ("chip", "core")
    return jax.shard_map(
        shards,
        mesh=fine,
        in_specs=(
            P(None, "space", None, None),
            P(slabs, None, "space", None, None),
            P(None, "space", None, None),
            P("space", None, None),
            P(),
        ),
        out_specs=P(slabs, None, "space", None, None),
        check_vma=False,
    )
```

```python
import functools

import jax
import jax.numpy as jnp
from jax import lax
from jax.experimental import pallas as pl
from jax.experimental.pallas import tpu as pltpu
from jax.sharding import Mesh, PartitionSpec as P

SLABS = 16
BRICKS = 8
PLANES = 4
NX = 32
MIDDLE = 128
LAST = 128
STRIP = 16
HALF = 8
EDGE = 10
ROWS = STRIP + 2 * EDGE
HELD = ROWS + 4
PART = ROWS // 2

RATE_ALONG = 4.0
RATE_ACROSS = 0.5
ADVECTION = 1.0
DAMPING = 0.8
COARSE_FACTOR = 4.0

ORDER = [0, 2, 4, 6, 7, 5, 3, 1]
AXES = ("chip", "core", "space")
MIB = 1 << 20

VMEM = pl.BlockSpec(memory_space=pltpu.VMEM)
HBM = pl.BlockSpec(memory_space=pltpu.HBM)
PAIR = 9
FINE, COARSE = 7, 8
F32 = jnp.float32


def shape(*dims):
    return jax.ShapeDtypeStruct(dims, F32)


def call(body, outs, in_specs, out_specs, scratch, limit, flops=0):
    return pl.pallas_call(
        body,
        cost_estimate=pl.CostEstimate(flops=flops, bytes_accessed=1 << 20, transcendentals=0) if flops else None,
        out_shape=outs,
        in_specs=in_specs,
        out_specs=out_specs,
        scratch_shapes=scratch,
        compiler_params=pltpu.CompilerParams(vmem_limit_bytes=limit * MIB),
    )


def position():
    chip, core, space = (lax.axis_index(a) for a in AXES)
    y, odd = space // 2, space % 2
    return core, jnp.where(odd == 0, y, BRICKS - 1 - y), chip * 2 + core


def pack_kernel(startup, guess, conduct, couple, out, padded, state, others, sems):
    core, _, slab = position()
    last = slab == SLABS - 1
    from_startup = [pltpu.make_async_copy(startup.at[i], state.at[i], sems.at[i]) for i in range(2)]
    from_guess = [pltpu.make_async_copy(guess.at[0, i], state.at[i], sems.at[i]) for i in range(2)]
    copies = [pltpu.make_async_copy(conduct.at[i], others.at[i], sems.at[2 + i]) for i in range(2)]
    copies.append(pltpu.make_async_copy(couple, others.at[2], sems.at[4]))

    @pl.when(last)
    def _():
        for copy in from_startup:
            copy.start()

    @pl.when(jnp.logical_not(last))
    def _():
        for copy in from_guess:
            copy.start()

    for copy in copies:
        copy.start()
    zero = jnp.zeros((EDGE * PLANES, LAST), F32)
    end = (EDGE + MIDDLE) * PLANES
    for i in range(5):
        padded[i, 0 : EDGE * PLANES] = zero
        padded[i, end : end + EDGE * PLANES] = zero
        (from_guess + copies)[i].wait()
        for plane in range(PLANES):
            for first in range(0, MIDDLE, 8):
                value = state[i, plane, first : first + 8] if i < 2 else others[i - 2, plane, first : first + 8]
                padded[i, pl.ds((EDGE + first) * PLANES + plane, 8, stride=PLANES), :] = value
    tall, part = (STRIP + 2 * EDGE) * PLANES, PART * PLANES
    for b in range(BRICKS):
        s = ORDER[b]
        start = (STRIP * b) * PLANES
        for i in range(2):
            out[s, i * tall : (i + 1) * tall] = padded[i, start : start + tall]
        start = pl.multiple_of(STRIP * b * PLANES + part * core, 32)
        for i in range(3):
            at = 2 * tall + i * part
            out[s, at : at + part] = padded[2 + i, pl.ds(start, part)]


def unpack_kernel(got, state, coefficients):
    low = lax.broadcasted_iota(jnp.int32, (8, LAST), 0) < PLANES

    def widen(out, i, at, rows):
        for y in range(0, rows, 2):
            for t in range(NX // 8):
                a = got[2 * t, at + PLANES * y : at + PLANES * y + 8]
                b = got[2 * t + 1, at + PLANES * y : at + PLANES * y + 8]
                out[i, y, 8 * t : 8 * t + 8] = jnp.where(low, a, pltpu.roll(b, 4, 0))
                out[i, y + 1, 8 * t : 8 * t + 8] = jnp.where(low, pltpu.roll(a, 4, 0), b)

    tall, part = (STRIP + 2 * EDGE) * PLANES, PART * PLANES
    for i in range(2):
        widen(state, i, i * tall, STRIP + 2 * EDGE)
    for i in range(3):
        widen(coefficients, i, 2 * tall + i * part, PART)


def restore_kernel(got, out):
    core, _, _ = position()
    for part in range(2):
        half = core if part == 0 else 1 - core
        for b in range(BRICKS):
            first = pl.multiple_of(STRIP * b + HALF * half, HALF)
            for i in range(2):
                for plane in range(PLANES):
                    at = (part * 2 + i) * HALF * PLANES + plane
                    out[0, i, plane, pl.ds(first, HALF), :] = got[ORDER[b], pl.ds(at, HALF, stride=PLANES), :]


def row_sweep(y, state, weights, earlier, step, source):
    centre = (state[0, y], state[1, y])
    out = []
    for i in range(2):
        v = centre[i]
        w = lambda k: weights[y, PAIR * i + k]
        along = w(0) * pltpu.roll(v, 1, 0) + w(1) * pltpu.roll(v, NX - 1, 0)
        middle = w(2) * state[i, y - 1] + w(3) * state[i, y + 1]
        across = w(4) * pltpu.roll(v, 1, 1) + w(5) * pltpu.roll(v, LAST - 1, 1)
        begin = v if earlier is None else earlier[i, y]
        if step == COARSE:
            begin = (1.0 / COARSE_FACTOR) * begin
        gain = (along + middle) + (across + (w(6) * centre[1 - i] + begin))
        if i == 1 and source is not None:
            gain = jnp.concatenate([gain[:8] + source[y], gain[8:]], axis=0)
        out.append((1.0 - DAMPING) * v + w(step) * gain)
    return out


def sweep(state, weights, earlier, into, low, high, step, source=None, unroll=4):
    def rows(k, carry):
        for u in range(unroll):
            y = low + unroll * k + u
            new = row_sweep(y, state, weights, earlier, step, source)
            into[0, y] = new[0]
            into[1, y] = new[1]
        return carry

    lax.fori_loop(0, (high - low + unroll - 1) // unroll, rows, 0)


def advances(count, e, v, weights, low, high, step, source=None):
    def one(m, carry):
        sweep(e, weights, None, v, low + 2 * m + 1, high - 2 * m - 1, step, source)
        sweep(v, weights, e, e, low + 2 * m + 2, high - 2 * m - 2, step, source)
        return carry

    lax.fori_loop(0, count, one, 0)


def relax_kernel(begin, mine, other, inlet, w, base, give, own, c, feed, e, v, e0):
    core, strip, slab = position()
    c[:, pl.ds(PART * core, PART)] = mine[...]
    c[:, pl.ds(PART - PART * core, PART)] = other[...]
    e[:, :ROWS] = begin[...]
    e0[:, :ROWS] = begin[...]

    plane = lax.broadcasted_iota(jnp.int32, (NX, LAST), 0)
    column = lax.broadcasted_iota(jnp.int32, (NX, LAST), 1)
    top = lax.broadcasted_iota(jnp.int32, (8, LAST), 0) == 0

    def weigh(r, carry):
        y = strip * STRIP - EDGE + r
        lower = jnp.where(y == 0, 0.0, 1.0).astype(F32)
        upper = jnp.where(y == MIDDLE - 1, 0.0, 1.0).astype(F32)
        exchange = c[2, r]
        warmth = inlet[pl.ds(jnp.clip(y, 0, MIDDLE - 1), 1), :]
        for i in range(2):
            here = c[i, r]
            xm = jnp.where(plane == 0, 0.0, pltpu.roll(here, 1, 0))
            xp = jnp.where(plane == NX - 1, 0.0, pltpu.roll(here, NX - 1, 0))
            zm = jnp.where(column == 0, 0.0, pltpu.roll(here, 1, 1))
            zp = jnp.where(column == LAST - 1, 0.0, pltpu.roll(here, LAST - 1, 1))
            half_along, half_across = 0.5 * RATE_ALONG, 0.5 * RATE_ACROSS
            wxm = half_along * (here + xm)
            if i == 1:
                wxm = wxm + ADVECTION
            wxp = half_along * (here + xp)
            wym = half_across * (here + c[i, r - 1])
            wyp = half_across * (here + c[i, r + 1])
            wzm = half_across * (here + zm)
            wzp = half_across * (here + zp)
            outflow = wxm + wxp + wym + wyp + wzm + wzp + exchange
            inner = (
                jnp.where(plane == 0, 0.0, wxm),
                jnp.where(plane == NX - 1, 0.0, wxp),
                wym * lower,
                wyp * upper,
                jnp.where(column == 0, 0.0, wzm),
                jnp.where(column == LAST - 1, 0.0, wzp),
                exchange,
            )
            for k in range(7):
                w[r, PAIR * i + k] = inner[k]
            w[r, PAIR * i + FINE] = DAMPING / (1.0 + outflow)
            w[r, PAIR * i + COARSE] = (DAMPING * COARSE_FACTOR) / (1.0 + COARSE_FACTOR * outflow)
            if i == 1:
                feed[r] = jnp.where(top, wxm[:8] * warmth, 0.0)
        return carry

    lax.fori_loop(1, ROWS - 1, weigh, 0)
    sweep(e0, w, None, v, EDGE - 3, EDGE + STRIP + 3, COARSE)
    sweep(v, w, e0, e0, EDGE - 2, EDGE + STRIP + 2, COARSE)
    advances(4, e, v, w, 0, ROWS, FINE, feed)
    keep = jnp.where(slab == SLABS - 1, 0.0, 1.0).astype(F32)
    rows = pl.ds(EDGE - 2, STRIP + 4)
    e[:, rows] = e[:, rows] - keep * e0[:, rows]
    sweep(e, w, None, v, EDGE - 1, EDGE + STRIP + 1, COARSE)
    sweep(v, w, e, e0, EDGE, EDGE + STRIP, COARSE)
    joined = jnp.where(slab == SLABS - 2, 0.0, 1.0).astype(F32)
    near, far = pl.ds(EDGE, HALF), pl.ds(EDGE + HALF, HALF)
    base[...] = jnp.where(core == 0, joined * e0[:, near], e[:, far])
    give[0:2] = jnp.where(core == 0, joined * e0[:, far], e[:, near])
    give[2:4] = e[:, far]
    own[...] = e[:, near]


def place(core, state, middle, inward, outward):
    many, rim = inward.shape[1], outward.shape[1]
    state[:, pl.ds(middle + HALF - (HALF + many) * core, many)] = inward[...]
    state[:, pl.ds(middle - rim + (HALF + rim) * core, rim)] = outward[...]


def leap_kernel(summed, *refs):
    core, _, _ = position()
    middle = EDGE + HALF * core
    rows = pl.ds(middle, HALF)
    own, near, swapped, w = refs[:4]
    local, (out, *rims, e, v) = (refs[4], refs[5:]) if summed else (None, refs[4:])
    e[:, rows] = own[...]
    place(core, e, middle, swapped, near)
    advances(4, e, v, w, middle - HALF, middle + 2 * HALF, COARSE)
    out[...] = local[...] + e[:, rows] if summed else e[:, rows]
    if rims:
        inner, outer, outer_wide = rims
        inner[...] = out[:, pl.ds(6 - 6 * core, 2)]
        outer[...] = out[:, pl.ds(6 * core, 2)]
        outer_wide[...] = out[:, pl.ds(2 * core, 6)]


def last_kernel(own, near, swapped, c_own, c_near, c_swapped, g, taken, w, keep, send, e, v, r):
    core, _, _ = position()
    middle = EDGE + HALF * core
    rows = pl.ds(middle, HALF)
    e[:, rows] = own[...]
    place(core, e, middle, swapped, near)
    r[:, rows] = c_own[...]
    place(core, r, middle, c_swapped, c_near)
    advances(2, e, v, w, middle - 6, middle + HALF + 6, COARSE)
    wide = pl.ds(middle - 2, HALF + 4)
    r[:, wide] = r[:, wide] + e[:, wide]
    sweep(r, w, None, v, middle - 1, middle + HALF + 1, COARSE)
    sweep(v, w, r, e, middle, middle + HALF, COARSE)
    e[:, rows] = e[:, rows] + jnp.where(core == 0, g[...], taken[2:4])
    low = lax.broadcasted_iota(jnp.int32, (8, LAST), 0) < PLANES
    for out, other in ((keep, 0), (send, 1)):
        pick = lambda *at: jnp.where(core == other, r[at], e[at])
        for i in range(2):
            for y in range(0, HALF, 2):
                at = (i * HALF + y) * PLANES
                for t in range(NX // 8):
                    a = pick(i, middle + y, slice(8 * t, 8 * t + 8))
                    b = pick(i, middle + y + 1, slice(8 * t, 8 * t + 8))
                    out[2 * t, at : at + 8] = jnp.where(low, a, pltpu.roll(b, 4, 0))
                    out[2 * t + 1, at : at + 8] = jnp.where(low, pltpu.roll(a, 4, 0), b)


def index(chip, core, strip):
    return (chip * 2 + core) * BRICKS + ORDER[strip]


def sent(value, chips, flip, shift):
    pairs = []
    for source, target in chips:
        for core in range(2):
            for strip in range(BRICKS):
                beside = strip + shift * (1 if core == 0 else -1)
                if 0 <= beside < BRICKS:
                    pairs.append((index(source, core ^ flip, strip), index(target, core, beside)))
    return lax.ppermute(value, AXES, pairs)


SAME = [(c, c) for c in range(8)]
HOME = [((c - 1) % 8, c) for c in range(8)]
UPPER = [(c, c) for c in range(4, 8)]
LEAP_FOUR = [((c - 5) % 8, c) for c in range(4, 8)]
LEAP_TWO = [(c - 2, c) for c in range(2, 8)]
LEAP_ONE = [(c - 1, c) for c in range(1, 8)]


def swap(value):
    return sent(value, SAME, 1, 0)


def shards(startup, guess, conduct, couple, inlet):
    chunk = (2 * ROWS + 3 * PART) * PLANES
    half = shape(2, HALF, NX, LAST)
    arrays = [pltpu.with_memory_space_constraint(a, pltpu.HBM) for a in (startup, guess, conduct, couple)]
    packed = call(
        pack_kernel,
        shape(BRICKS, chunk, LAST),
        [HBM] * 4,
        VMEM,
        [
            pltpu.VMEM((5, (MIDDLE + 2 * EDGE) * PLANES, LAST), F32),
            pltpu.VMEM((2, PLANES, MIDDLE, LAST), F32),
            pltpu.VMEM((3, PLANES, MIDDLE, LAST), F32),
            pltpu.SemaphoreType.DMA((5,)),
        ],
        16,
    )(*arrays)
    got = lax.all_to_all(packed, "space", 0, 0, tiled=True)
    begin, mine = call(
        unpack_kernel, (shape(2, ROWS, NX, LAST), shape(3, PART, NX, LAST)), [VMEM], (VMEM, VMEM), [], 16
    )(got)
    other = swap(mine)

    field = pltpu.VMEM((2, HELD, NX, LAST), F32)
    weights, base, give, g = call(
        relax_kernel,
        (pltpu.VMEM((HELD, 2 * PAIR, NX, LAST), F32), half, shape(4, HALF, NX, LAST), half),
        [VMEM] * 4,
        (VMEM,) * 4,
        [pltpu.VMEM((3, ROWS, NX, LAST), F32), pltpu.VMEM((HELD, 8, LAST), F32), field, field, field],
        24,
    )(begin, mine, other, inlet)
    taken = swap(give)
    u = base + taken[:2]

    def leap(own, near, local=None, rims=()):
        operands = [own, near, swap(own), weights] + ([] if local is None else [local])
        return call(
            functools.partial(leap_kernel, local is not None),
            (half,) + rims,
            [VMEM] * len(operands),
            (VMEM,) * (1 + len(rims)),
            [field, field],
            20,
            1 << 26,
        )(*operands)

    (z,) = leap(sent(u, LEAP_FOUR, 0, 0), sent(u, LEAP_FOUR, 1, 1))
    (x,) = leap(z, sent(z, UPPER, 1, 1), sent(u, HOME, 0, 0))
    rim = shape(2, 2, NX, LAST)
    y, inner, outer, outer_wide = leap(
        sent(x, LEAP_TWO, 0, 0), sent(x, LEAP_TWO, 1, 1), x, (rim, rim, shape(2, 6, NX, LAST))
    )

    c_near, c_swapped = sent(outer, SAME, 1, 1), swap(inner)
    near, own = sent(outer_wide, LEAP_ONE, 1, 1), sent(y, LEAP_ONE, 0, 0)
    own, near, c_near, c_swapped = lax.optimization_barrier((own, near, c_near, c_swapped))
    parcel = shape(BRICKS, 2 * HALF * PLANES, LAST)
    keep, send = call(last_kernel, (parcel, parcel), [VMEM] * 9, (VMEM,) * 2, [field, field, field], 22)(
        own, near, swap(own), y, c_near, c_swapped, g, taken, weights
    )
    back = lax.all_to_all(jnp.concatenate([keep, swap(send)], axis=1), "space", 0, 0, tiled=True)
    return call(restore_kernel, shape(1, 2, PLANES, MIDDLE, LAST), [VMEM], VMEM, [], 16)(back)


def solution(mesh):
    fine = Mesh(mesh.devices.reshape(SLABS // 2, 2, BRICKS), AXES)
    slabs = ("chip", "core")
    return jax.shard_map(
        shards,
        mesh=fine,
        in_specs=(
            P(None, "space", None, None),
            P(slabs, None, "space", None, None),
            P(None, "space", None, None),
            P("space", None, None),
            P(),
        ),
        out_specs=P(slabs, None, "space", None, None),
        check_vma=False,
    )
```

```python
import functools

import jax
import jax.numpy as jnp
from jax import lax
from jax.experimental import pallas as pl
from jax.experimental.pallas import tpu as pltpu
from jax.sharding import Mesh, PartitionSpec as P

SLABS = 16
BRICKS = 8
PLANES = 4
NX = 32
MIDDLE = 128
LAST = 128
STRIP = 16
HALF = 8
EDGE = 10
ROWS = STRIP + 2 * EDGE
HELD = ROWS + 4
PART = ROWS // 2

RATE_ALONG = 4.0
RATE_ACROSS = 0.5
ADVECTION = 1.0
DAMPING = 0.8
COARSE_FACTOR = 4.0

ORDER = [0, 2, 4, 6, 7, 5, 3, 1]
AXES = ("chip", "core", "space")
MIB = 1 << 20

VMEM = pl.BlockSpec(memory_space=pltpu.VMEM)
HBM = pl.BlockSpec(memory_space=pltpu.HBM)
PAIR = 9
FINE, COARSE = 7, 8
F32 = jnp.float32


def shape(*dims):
    return jax.ShapeDtypeStruct(dims, F32)


def call(body, outs, in_specs, out_specs, scratch, limit, flops=0):
    return pl.pallas_call(
        body,
        cost_estimate=pl.CostEstimate(flops=flops, bytes_accessed=1 << 20, transcendentals=0) if flops else None,
        out_shape=outs,
        in_specs=in_specs,
        out_specs=out_specs,
        scratch_shapes=scratch,
        compiler_params=pltpu.CompilerParams(vmem_limit_bytes=limit * MIB),
    )


def position():
    chip, core, space = (lax.axis_index(a) for a in AXES)
    y, odd = space // 2, space % 2
    return core, jnp.where(odd == 0, y, BRICKS - 1 - y), chip * 2 + core


def pack_kernel(startup, guess, conduct, couple, out, padded, state, others, sems):
    core, _, slab = position()
    last = slab == SLABS - 1
    from_startup = [pltpu.make_async_copy(startup.at[i], state.at[i], sems.at[i]) for i in range(2)]
    from_guess = [pltpu.make_async_copy(guess.at[0, i], state.at[i], sems.at[i]) for i in range(2)]
    copies = [pltpu.make_async_copy(conduct.at[i], others.at[i], sems.at[2 + i]) for i in range(2)]
    copies.append(pltpu.make_async_copy(couple, others.at[2], sems.at[4]))

    @pl.when(last)
    def _():
        for copy in from_startup:
            copy.start()

    @pl.when(jnp.logical_not(last))
    def _():
        for copy in from_guess:
            copy.start()

    for copy in copies:
        copy.start()
    zero = jnp.zeros((EDGE * PLANES, LAST), F32)
    end = (EDGE + MIDDLE) * PLANES
    for i in range(5):
        padded[i, 0 : EDGE * PLANES] = zero
        padded[i, end : end + EDGE * PLANES] = zero
        (from_guess + copies)[i].wait()
        for plane in range(PLANES):
            for first in range(0, MIDDLE, 8):
                value = state[i, plane, first : first + 8] if i < 2 else others[i - 2, plane, first : first + 8]
                padded[i, pl.ds((EDGE + first) * PLANES + plane, 8, stride=PLANES), :] = value
    tall, part = (STRIP + 2 * EDGE) * PLANES, PART * PLANES
    for b in range(BRICKS):
        s = ORDER[b]
        start = (STRIP * b) * PLANES
        for i in range(2):
            out[s, i * tall : (i + 1) * tall] = padded[i, start : start + tall]
        start = pl.multiple_of(STRIP * b * PLANES + part * core, 32)
        for i in range(3):
            at = 2 * tall + i * part
            out[s, at : at + part] = padded[2 + i, pl.ds(start, part)]


def unpack_kernel(got, state, coefficients):
    low = lax.broadcasted_iota(jnp.int32, (8, LAST), 0) < PLANES

    def widen(out, i, at, rows):
        for y in range(0, rows, 2):
            for t in range(NX // 8):
                a = got[2 * t, at + PLANES * y : at + PLANES * y + 8]
                b = got[2 * t + 1, at + PLANES * y : at + PLANES * y + 8]
                out[i, y, 8 * t : 8 * t + 8] = jnp.where(low, a, pltpu.roll(b, 4, 0))
                out[i, y + 1, 8 * t : 8 * t + 8] = jnp.where(low, pltpu.roll(a, 4, 0), b)

    tall, part = (STRIP + 2 * EDGE) * PLANES, PART * PLANES
    for i in range(2):
        widen(state, i, i * tall, STRIP + 2 * EDGE)
    for i in range(3):
        widen(coefficients, i, 2 * tall + i * part, PART)


def restore_kernel(got, out):
    core, _, _ = position()
    for part in range(2):
        half = core if part == 0 else 1 - core
        for b in range(BRICKS):
            first = pl.multiple_of(STRIP * b + HALF * half, HALF)
            for i in range(2):
                for plane in range(PLANES):
                    at = (part * 2 + i) * HALF * PLANES + plane
                    out[0, i, plane, pl.ds(first, HALF), :] = got[ORDER[b], pl.ds(at, HALF, stride=PLANES), :]


def row_sweep(y, state, weights, earlier, step, source):
    centre = (state[0, y], state[1, y])
    out = []
    for i in range(2):
        v = centre[i]
        w = lambda k: weights[y, PAIR * i + k]
        along = w(0) * pltpu.roll(v, 1, 0) + w(1) * pltpu.roll(v, NX - 1, 0)
        middle = w(2) * state[i, y - 1] + w(3) * state[i, y + 1]
        across = w(4) * pltpu.roll(v, 1, 1) + w(5) * pltpu.roll(v, LAST - 1, 1)
        begin = v if earlier is None else earlier[i, y]
        if step == COARSE:
            begin = (1.0 / COARSE_FACTOR) * begin
        gain = (along + middle) + (across + (w(6) * centre[1 - i] + begin))
        if i == 1 and source is not None:
            gain = jnp.concatenate([gain[:8] + source[y], gain[8:]], axis=0)
        out.append((1.0 - DAMPING) * v + w(step) * gain)
    return out


def sweep(state, weights, earlier, into, low, high, step, source=None, unroll=4):
    def rows(k, carry):
        for u in range(unroll):
            y = low + unroll * k + u
            new = row_sweep(y, state, weights, earlier, step, source)
            into[0, y] = new[0]
            into[1, y] = new[1]
        return carry

    lax.fori_loop(0, (high - low + unroll - 1) // unroll, rows, 0)


def advances(count, e, v, weights, low, high, step, source=None):
    def one(m, carry):
        sweep(e, weights, None, v, low + 2 * m + 1, high - 2 * m - 1, step, source)
        sweep(v, weights, e, e, low + 2 * m + 2, high - 2 * m - 2, step, source)
        return carry

    lax.fori_loop(0, count, one, 0)


def relax_kernel(begin, mine, other, inlet, w, base, give, own, c, feed, e, v, e0):
    core, strip, slab = position()
    c[:, pl.ds(PART * core, PART)] = mine[...]
    c[:, pl.ds(PART - PART * core, PART)] = other[...]
    e[:, :ROWS] = begin[...]
    e0[:, :ROWS] = begin[...]

    plane = lax.broadcasted_iota(jnp.int32, (NX, LAST), 0)
    column = lax.broadcasted_iota(jnp.int32, (NX, LAST), 1)
    top = lax.broadcasted_iota(jnp.int32, (8, LAST), 0) == 0

    def weigh(r, carry):
        y = strip * STRIP - EDGE + r
        lower = jnp.where(y == 0, 0.0, 1.0).astype(F32)
        upper = jnp.where(y == MIDDLE - 1, 0.0, 1.0).astype(F32)
        exchange = c[2, r]
        warmth = inlet[pl.ds(jnp.clip(y, 0, MIDDLE - 1), 1), :]
        for i in range(2):
            here = c[i, r]
            xm = jnp.where(plane == 0, 0.0, pltpu.roll(here, 1, 0))
            xp = jnp.where(plane == NX - 1, 0.0, pltpu.roll(here, NX - 1, 0))
            zm = jnp.where(column == 0, 0.0, pltpu.roll(here, 1, 1))
            zp = jnp.where(column == LAST - 1, 0.0, pltpu.roll(here, LAST - 1, 1))
            half_along, half_across = 0.5 * RATE_ALONG, 0.5 * RATE_ACROSS
            wxm = half_along * (here + xm)
            if i == 1:
                wxm = wxm + ADVECTION
            wxp = half_along * (here + xp)
            wym = half_across * (here + c[i, r - 1])
            wyp = half_across * (here + c[i, r + 1])
            wzm = half_across * (here + zm)
            wzp = half_across * (here + zp)
            outflow = wxm + wxp + wym + wyp + wzm + wzp + exchange
            inner = (
                jnp.where(plane == 0, 0.0, wxm),
                jnp.where(plane == NX - 1, 0.0, wxp),
                wym * lower,
                wyp * upper,
                jnp.where(column == 0, 0.0, wzm),
                jnp.where(column == LAST - 1, 0.0, wzp),
                exchange,
            )
            for k in range(7):
                w[r, PAIR * i + k] = inner[k]
            w[r, PAIR * i + FINE] = DAMPING / (1.0 + outflow)
            w[r, PAIR * i + COARSE] = (DAMPING * COARSE_FACTOR) / (1.0 + COARSE_FACTOR * outflow)
            if i == 1:
                feed[r] = jnp.where(top, wxm[:8] * warmth, 0.0)
        return carry

    lax.fori_loop(1, ROWS - 1, weigh, 0)
    sweep(e0, w, None, v, EDGE - 3, EDGE + STRIP + 3, COARSE)
    sweep(v, w, e0, e0, EDGE - 2, EDGE + STRIP + 2, COARSE)
    advances(4, e, v, w, 0, ROWS, FINE, feed)
    keep = jnp.where(slab == SLABS - 1, 0.0, 1.0).astype(F32)
    rows = pl.ds(EDGE - 2, STRIP + 4)
    e[:, rows] = e[:, rows] - keep * e0[:, rows]
    sweep(e, w, None, v, EDGE - 1, EDGE + STRIP + 1, COARSE)
    sweep(v, w, e, e0, EDGE, EDGE + STRIP, COARSE)
    joined = jnp.where(slab == SLABS - 2, 0.0, 1.0).astype(F32)
    near, far = pl.ds(EDGE, HALF), pl.ds(EDGE + HALF, HALF)
    base[...] = jnp.where(core == 0, joined * e0[:, near], e[:, far])
    give[0:2] = jnp.where(core == 0, joined * e0[:, far], e[:, near])
    give[2:4] = e[:, far]
    own[...] = e[:, near]


def place(core, state, middle, inward, outward):
    many, rim = inward.shape[1], outward.shape[1]
    state[:, pl.ds(middle + HALF - (HALF + many) * core, many)] = inward[...]
    state[:, pl.ds(middle - rim + (HALF + rim) * core, rim)] = outward[...]


def leap_kernel(own, near, swapped, w, odd, *refs):
    core, _, _ = position()
    middle = EDGE + HALF * core
    rows = pl.ds(middle, HALF)
    *more, e, v = refs
    reach = HALF if more else HALF // 2
    e[:, rows] = own[...]
    place(core, e, middle, swapped, near)
    advances(2, e, v, w, middle - reach, middle + HALF + reach, COARSE)
    odd[...] = e[:, rows]
    if more:
        even, *rims = more
        advances(2, e, v, w, middle - 4, middle + HALF + 4, COARSE)
        even[...] = e[:, rows]
        if rims:
            inner, outer = rims
            inner[...] = even[:, pl.ds(4 - 4 * core, 4)]
            outer[...] = even[:, pl.ds(4 * core, 4)]


def sum_kernel(local, *refs):
    core, _, slab = position()
    *arrived, out, inner, outer = refs
    total = arrived[0][...]
    for ref in arrived[1:]:
        total = total + ref[...]
    out[...] = total + jnp.where(slab // 2 == SLABS // 2 - 1, local[...], 0.0)
    inner[...] = out[:, pl.ds(6 - 6 * core, 2)]
    outer[...] = out[:, pl.ds(6 * core, 2)]


def last_kernel(own, near, swapped, g, taken, w, keep, send, r, v, e):
    core, _, _ = position()
    middle = EDGE + HALF * core
    rows = pl.ds(middle, HALF)
    r[:, rows] = own[...]
    place(core, r, middle, swapped, near)
    sweep(r, w, None, v, middle - 1, middle + HALF + 1, COARSE)
    sweep(v, w, r, e, middle, middle + HALF, COARSE)
    e[:, rows] = e[:, rows] + jnp.where(core == 0, g[...], taken[2:4])
    low = lax.broadcasted_iota(jnp.int32, (8, LAST), 0) < PLANES
    for out, other in ((keep, 0), (send, 1)):
        pick = lambda *at: jnp.where(core == other, r[at], e[at])
        for i in range(2):
            for y in range(0, HALF, 2):
                at = (i * HALF + y) * PLANES
                for t in range(NX // 8):
                    a = pick(i, middle + y, slice(8 * t, 8 * t + 8))
                    b = pick(i, middle + y + 1, slice(8 * t, 8 * t + 8))
                    out[2 * t, at : at + 8] = jnp.where(low, a, pltpu.roll(b, 4, 0))
                    out[2 * t + 1, at : at + 8] = jnp.where(low, pltpu.roll(a, 4, 0), b)


def index(chip, core, strip):
    return (chip * 2 + core) * BRICKS + ORDER[strip]


def sent(value, chips, flip, shift):
    pairs = []
    for source, target in chips:
        for core in range(2):
            for strip in range(BRICKS):
                beside = strip + shift * (1 if core == 0 else -1)
                if 0 <= beside < BRICKS:
                    pairs.append((index(source, core ^ flip, strip), index(target, core, beside)))
    return lax.ppermute(value, AXES, pairs)


CHIPS = SLABS // 2
SAME = [(c, c) for c in range(CHIPS)]


def onward(power):
    return [((j - 1) % CHIPS, j + power) for j in range(CHIPS - power)]


def swap(value):
    return sent(value, SAME, 1, 0)


def shards(startup, guess, conduct, couple, inlet):
    chunk = (2 * ROWS + 3 * PART) * PLANES
    half = shape(2, HALF, NX, LAST)
    arrays = [pltpu.with_memory_space_constraint(a, pltpu.HBM) for a in (startup, guess, conduct, couple)]
    packed = call(
        pack_kernel,
        shape(BRICKS, chunk, LAST),
        [HBM] * 4,
        VMEM,
        [
            pltpu.VMEM((5, (MIDDLE + 2 * EDGE) * PLANES, LAST), F32),
            pltpu.VMEM((2, PLANES, MIDDLE, LAST), F32),
            pltpu.VMEM((3, PLANES, MIDDLE, LAST), F32),
            pltpu.SemaphoreType.DMA((5,)),
        ],
        16,
    )(*arrays)
    got = lax.all_to_all(packed, "space", 0, 0, tiled=True)
    begin, mine = call(
        unpack_kernel, (shape(2, ROWS, NX, LAST), shape(3, PART, NX, LAST)), [VMEM], (VMEM, VMEM), [], 16
    )(got)
    other = swap(mine)

    field = pltpu.VMEM((2, HELD, NX, LAST), F32)
    weights, base, give, g = call(
        relax_kernel,
        (pltpu.VMEM((HELD, 2 * PAIR, NX, LAST), F32), half, shape(4, HALF, NX, LAST), half),
        [VMEM] * 4,
        (VMEM,) * 4,
        [pltpu.VMEM((3, ROWS, NX, LAST), F32), pltpu.VMEM((HELD, 8, LAST), F32), field, field, field],
        24,
    )(begin, mine, other, inlet)
    taken = swap(give)
    u = base + taken[:2]

    def leap(own, near, swapped, *rims, second=True):
        outs = (half,) * (1 + second) + rims
        return call(leap_kernel, outs, [VMEM] * 4, (VMEM,) * len(outs), [field, field], 20, 1 << 26)(
            own, near, swapped, weights
        )

    def beside(value):
        return sent(value, SAME, 1, 1)

    rim4, rim2 = shape(2, 4, NX, LAST), shape(2, 2, NX, LAST)
    u1, u2 = leap(u, beside(u), swap(u))
    u3, u4 = leap(u2, beside(u2), swap(u2))
    u5, u6, inner, outer = leap(u4, beside(u4), swap(u4), rim4, rim4)
    (u7,) = leap(u6, beside(outer), swap(inner), second=False)
    arrived = [sent(power, onward(k), 0, 0) for k, power in enumerate((u, u1, u2, u3, u4, u5, u6))]
    c, inner, outer = call(sum_kernel, (half, rim2, rim2), [VMEM] * 8, (VMEM,) * 3, [], 16)(u7, *arrived)
    parcel = shape(BRICKS, 2 * HALF * PLANES, LAST)
    keep, send = call(last_kernel, (parcel, parcel), [VMEM] * 6, (VMEM,) * 2, [field, field, field], 22)(
        c, beside(outer), swap(inner), g, taken, weights
    )
    back = lax.all_to_all(jnp.concatenate([keep, swap(send)], axis=1), "space", 0, 0, tiled=True)
    return call(restore_kernel, shape(1, 2, PLANES, MIDDLE, LAST), [VMEM], VMEM, [], 16)(back)


def solution(mesh):
    fine = Mesh(mesh.devices.reshape(SLABS // 2, 2, BRICKS), AXES)
    slabs = ("chip", "core")
    return jax.shard_map(
        shards,
        mesh=fine,
        in_specs=(
            P(None, "space", None, None),
            P(slabs, None, "space", None, None),
            P(None, "space", None, None),
            P("space", None, None),
            P(),
        ),
        out_specs=P(slabs, None, "space", None, None),
        check_vma=False,
    )
```

```python
import functools

import jax
import jax.numpy as jnp
from jax import lax
from jax.experimental import pallas as pl
from jax.experimental.pallas import tpu as pltpu
from jax.sharding import Mesh, PartitionSpec as P

SLABS = 16
BRICKS = 8
PLANES = 4
NX = 32
MIDDLE = 128
LAST = 128
STRIP = 16
HALF = 8
EDGE = 10
ROWS = STRIP + 2 * EDGE
HELD = ROWS + 4
PART = ROWS // 2

RATE_ALONG = 4.0
RATE_ACROSS = 0.5
ADVECTION = 1.0
DAMPING = 0.8
COARSE_FACTOR = 4.0

ORDER = [0, 2, 4, 6, 7, 5, 3, 1]
AXES = ("chip", "core", "space")
MIB = 1 << 20

VMEM = pl.BlockSpec(memory_space=pltpu.VMEM)
HBM = pl.BlockSpec(memory_space=pltpu.HBM)
PAIR = 9
FINE, COARSE = 7, 8
F32 = jnp.float32


def shape(*dims):
    return jax.ShapeDtypeStruct(dims, F32)


def call(body, outs, in_specs, out_specs, scratch, limit, us=1):
    return pl.pallas_call(
        body,
        cost_estimate=pl.CostEstimate(flops=0, bytes_accessed=us * (3 << 20), transcendentals=0),
        out_shape=outs,
        in_specs=in_specs,
        out_specs=out_specs,
        scratch_shapes=scratch,
        compiler_params=pltpu.CompilerParams(vmem_limit_bytes=limit * MIB),
    )


def position():
    chip, core, space = (lax.axis_index(a) for a in AXES)
    y, odd = space // 2, space % 2
    return core, jnp.where(odd == 0, y, BRICKS - 1 - y), chip * 2 + core


def pack_kernel(startup, guess, conduct, couple, out, padded, state, others, sems):
    core, _, slab = position()
    last = slab == SLABS - 1
    from_startup = [pltpu.make_async_copy(startup.at[i], state.at[i], sems.at[i]) for i in range(2)]
    from_guess = [pltpu.make_async_copy(guess.at[0, i], state.at[i], sems.at[i]) for i in range(2)]
    copies = [pltpu.make_async_copy(conduct.at[i], others.at[i], sems.at[2 + i]) for i in range(2)]
    copies.append(pltpu.make_async_copy(couple, others.at[2], sems.at[4]))

    @pl.when(last)
    def _():
        for copy in from_startup:
            copy.start()

    @pl.when(jnp.logical_not(last))
    def _():
        for copy in from_guess:
            copy.start()

    for copy in copies:
        copy.start()
    zero = jnp.zeros((EDGE * PLANES, LAST), F32)
    end = (EDGE + MIDDLE) * PLANES
    for i in range(5):
        padded[i, 0 : EDGE * PLANES] = zero
        padded[i, end : end + EDGE * PLANES] = zero
        (from_guess + copies)[i].wait()
        for plane in range(PLANES):
            for first in range(0, MIDDLE, 8):
                value = state[i, plane, first : first + 8] if i < 2 else others[i - 2, plane, first : first + 8]
                padded[i, pl.ds((EDGE + first) * PLANES + plane, 8, stride=PLANES), :] = value
    tall, part = (STRIP + 2 * EDGE) * PLANES, PART * PLANES
    for b in range(BRICKS):
        s = ORDER[b]
        start = (STRIP * b) * PLANES
        for i in range(2):
            out[s, i * tall : (i + 1) * tall] = padded[i, start : start + tall]
        start = pl.multiple_of(STRIP * b * PLANES + part * core, 32)
        for i in range(3):
            at = 2 * tall + i * part
            out[s, at : at + part] = padded[2 + i, pl.ds(start, part)]


def unpack_kernel(got, state, coefficients):
    low = lax.broadcasted_iota(jnp.int32, (8, LAST), 0) < PLANES

    def widen(out, i, at, rows):
        for y in range(0, rows, 2):
            for t in range(NX // 8):
                a = got[2 * t, at + PLANES * y : at + PLANES * y + 8]
                b = got[2 * t + 1, at + PLANES * y : at + PLANES * y + 8]
                out[i, y, 8 * t : 8 * t + 8] = jnp.where(low, a, pltpu.roll(b, 4, 0))
                out[i, y + 1, 8 * t : 8 * t + 8] = jnp.where(low, pltpu.roll(a, 4, 0), b)

    tall, part = (STRIP + 2 * EDGE) * PLANES, PART * PLANES
    for i in range(2):
        widen(state, i, i * tall, STRIP + 2 * EDGE)
    for i in range(3):
        widen(coefficients, i, 2 * tall + i * part, PART)


def restore_kernel(got, out):
    core, _, _ = position()
    for part in range(2):
        half = core if part == 0 else 1 - core
        for b in range(BRICKS):
            first = pl.multiple_of(STRIP * b + HALF * half, HALF)
            for i in range(2):
                for plane in range(PLANES):
                    at = (part * 2 + i) * HALF * PLANES + plane
                    out[0, i, plane, pl.ds(first, HALF), :] = got[ORDER[b], pl.ds(at, HALF, stride=PLANES), :]


def row_sweep(y, state, weights, earlier, step, source):
    centre = (state[0, y], state[1, y])
    out = []
    for i in range(2):
        v = centre[i]
        w = lambda k: weights[y, PAIR * i + k]
        along = w(0) * pltpu.roll(v, 1, 0) + w(1) * pltpu.roll(v, NX - 1, 0)
        middle = w(2) * state[i, y - 1] + w(3) * state[i, y + 1]
        across = w(4) * pltpu.roll(v, 1, 1) + w(5) * pltpu.roll(v, LAST - 1, 1)
        begin = v if earlier is None else earlier[i, y]
        if step == COARSE:
            begin = (1.0 / COARSE_FACTOR) * begin
        gain = (along + middle) + (across + (w(6) * centre[1 - i] + begin))
        if i == 1 and source is not None:
            gain = jnp.concatenate([gain[:8] + source[y], gain[8:]], axis=0)
        out.append((1.0 - DAMPING) * v + w(step) * gain)
    return out


def sweep(state, weights, earlier, into, low, high, step, source=None, unroll=4):
    def rows(k, carry):
        for u in range(unroll):
            y = low + unroll * k + u
            new = row_sweep(y, state, weights, earlier, step, source)
            into[0, y] = new[0]
            into[1, y] = new[1]
        return carry

    lax.fori_loop(0, (high - low + unroll - 1) // unroll, rows, 0)


def advances(count, e, v, weights, low, high, step, source=None):
    def one(m, carry):
        sweep(e, weights, None, v, low + 2 * m + 1, high - 2 * m - 1, step, source)
        sweep(v, weights, e, e, low + 2 * m + 2, high - 2 * m - 2, step, source)
        return carry

    lax.fori_loop(0, count, one, 0)


def relax_kernel(begin, mine, other, inlet, w, base, give, own, c, feed, e, v, e0):
    core, strip, slab = position()
    c[:, pl.ds(PART * core, PART)] = mine[...]
    c[:, pl.ds(PART - PART * core, PART)] = other[...]
    e[:, :ROWS] = begin[...]
    e0[:, :ROWS] = begin[...]

    plane = lax.broadcasted_iota(jnp.int32, (NX, LAST), 0)
    column = lax.broadcasted_iota(jnp.int32, (NX, LAST), 1)
    top = lax.broadcasted_iota(jnp.int32, (8, LAST), 0) == 0

    def weigh(r, carry):
        y = strip * STRIP - EDGE + r
        lower = jnp.where(y == 0, 0.0, 1.0).astype(F32)
        upper = jnp.where(y == MIDDLE - 1, 0.0, 1.0).astype(F32)
        exchange = c[2, r]
        warmth = inlet[pl.ds(jnp.clip(y, 0, MIDDLE - 1), 1), :]
        for i in range(2):
            here = c[i, r]
            xm = jnp.where(plane == 0, 0.0, pltpu.roll(here, 1, 0))
            xp = jnp.where(plane == NX - 1, 0.0, pltpu.roll(here, NX - 1, 0))
            zm = jnp.where(column == 0, 0.0, pltpu.roll(here, 1, 1))
            zp = jnp.where(column == LAST - 1, 0.0, pltpu.roll(here, LAST - 1, 1))
            half_along, half_across = 0.5 * RATE_ALONG, 0.5 * RATE_ACROSS
            wxm = half_along * (here + xm)
            if i == 1:
                wxm = wxm + ADVECTION
            wxp = half_along * (here + xp)
            wym = half_across * (here + c[i, r - 1])
            wyp = half_across * (here + c[i, r + 1])
            wzm = half_across * (here + zm)
            wzp = half_across * (here + zp)
            outflow = wxm + wxp + wym + wyp + wzm + wzp + exchange
            inner = (
                jnp.where(plane == 0, 0.0, wxm),
                jnp.where(plane == NX - 1, 0.0, wxp),
                wym * lower,
                wyp * upper,
                jnp.where(column == 0, 0.0, wzm),
                jnp.where(column == LAST - 1, 0.0, wzp),
                exchange,
            )
            for k in range(7):
                w[r, PAIR * i + k] = inner[k]
            w[r, PAIR * i + FINE] = DAMPING / (1.0 + outflow)
            w[r, PAIR * i + COARSE] = (DAMPING * COARSE_FACTOR) / (1.0 + COARSE_FACTOR * outflow)
            if i == 1:
                feed[r] = jnp.where(top, wxm[:8] * warmth, 0.0)
        return carry

    lax.fori_loop(1, ROWS - 1, weigh, 0)
    sweep(e0, w, None, v, EDGE - 3, EDGE + STRIP + 3, COARSE)
    sweep(v, w, e0, e0, EDGE - 2, EDGE + STRIP + 2, COARSE)
    advances(4, e, v, w, 0, ROWS, FINE, feed)
    keep = jnp.where(slab == SLABS - 1, 0.0, 1.0).astype(F32)
    rows = pl.ds(EDGE - 2, STRIP + 4)
    e[:, rows] = e[:, rows] - keep * e0[:, rows]
    sweep(e, w, None, v, EDGE - 1, EDGE + STRIP + 1, COARSE)
    sweep(v, w, e, e0, EDGE, EDGE + STRIP, COARSE)
    joined = jnp.where(slab == SLABS - 2, 0.0, 1.0).astype(F32)
    near, far = pl.ds(EDGE, HALF), pl.ds(EDGE + HALF, HALF)
    base[...] = jnp.where(core == 0, joined * e0[:, near], e[:, far])
    give[0:2] = jnp.where(core == 0, joined * e0[:, far], e[:, near])
    give[2:4] = e[:, far]
    own[...] = e[:, near]


def place(core, state, middle, inward, outward):
    many, rim = inward.shape[1], outward.shape[1]
    state[:, pl.ds(middle + HALF - (HALF + many) * core, many)] = inward[...]
    state[:, pl.ds(middle - rim + (HALF + rim) * core, rim)] = outward[...]


def leap_kernel(own, near, swapped, w, odd, *refs):
    core, _, _ = position()
    middle = EDGE + HALF * core
    rows = pl.ds(middle, HALF)
    *more, e, v = refs
    reach = HALF if more else HALF // 2
    e[:, rows] = own[...]
    place(core, e, middle, swapped, near)
    advances(2, e, v, w, middle - reach, middle + HALF + reach, COARSE)
    odd[...] = e[:, rows]
    if more:
        even, *rims = more
        advances(2, e, v, w, middle - 4, middle + HALF + 4, COARSE)
        even[...] = e[:, rows]
        if rims:
            inner, outer = rims
            inner[...] = even[:, pl.ds(4 - 4 * core, 4)]
            outer[...] = even[:, pl.ds(4 * core, 4)]


def sum_kernel(local, *refs):
    core, _, slab = position()
    *arrived, out, inner, outer = refs
    total = arrived[0][...]
    for ref in arrived[1:]:
        total = total + ref[...]
    out[...] = total + jnp.where(slab // 2 == SLABS // 2 - 1, local[...], 0.0)
    inner[...] = out[:, pl.ds(6 - 6 * core, 2)]
    outer[...] = out[:, pl.ds(6 * core, 2)]


def last_kernel(own, near, swapped, g, taken, w, keep, send, r, v, e):
    core, _, _ = position()
    middle = EDGE + HALF * core
    rows = pl.ds(middle, HALF)
    r[:, rows] = own[...]
    place(core, r, middle, swapped, near)
    sweep(r, w, None, v, middle - 1, middle + HALF + 1, COARSE)
    sweep(v, w, r, e, middle, middle + HALF, COARSE)
    e[:, rows] = e[:, rows] + jnp.where(core == 0, g[...], taken[2:4])
    low = lax.broadcasted_iota(jnp.int32, (8, LAST), 0) < PLANES
    for out, other in ((keep, 0), (send, 1)):
        pick = lambda *at: jnp.where(core == other, r[at], e[at])
        for i in range(2):
            for y in range(0, HALF, 2):
                at = (i * HALF + y) * PLANES
                for t in range(NX // 8):
                    a = pick(i, middle + y, slice(8 * t, 8 * t + 8))
                    b = pick(i, middle + y + 1, slice(8 * t, 8 * t + 8))
                    out[2 * t, at : at + 8] = jnp.where(low, a, pltpu.roll(b, 4, 0))
                    out[2 * t + 1, at : at + 8] = jnp.where(low, pltpu.roll(a, 4, 0), b)


def index(chip, core, strip):
    return (chip * 2 + core) * BRICKS + ORDER[strip]


def sent(value, chips, flip, shift):
    pairs = []
    for source, target in chips:
        for core in range(2):
            for strip in range(BRICKS):
                beside = strip + shift * (1 if core == 0 else -1)
                if 0 <= beside < BRICKS:
                    pairs.append((index(source, core ^ flip, strip), index(target, core, beside)))
    return lax.ppermute(value, AXES, pairs)


CHIPS = SLABS // 2
SAME = [(c, c) for c in range(CHIPS)]


def onward(power):
    return [((j - 1) % CHIPS, j + power) for j in range(CHIPS - power)]


def swap(value):
    return sent(value, SAME, 1, 0)


def shards(startup, guess, conduct, couple, inlet):
    chunk = (2 * ROWS + 3 * PART) * PLANES
    half = shape(2, HALF, NX, LAST)
    arrays = [pltpu.with_memory_space_constraint(a, pltpu.HBM) for a in (startup, guess, conduct, couple)]
    packed = call(
        pack_kernel,
        shape(BRICKS, chunk, LAST),
        [HBM] * 4,
        VMEM,
        [
            pltpu.VMEM((5, (MIDDLE + 2 * EDGE) * PLANES, LAST), F32),
            pltpu.VMEM((2, PLANES, MIDDLE, LAST), F32),
            pltpu.VMEM((3, PLANES, MIDDLE, LAST), F32),
            pltpu.SemaphoreType.DMA((5,)),
        ],
        16,
    )(*arrays)
    got = lax.all_to_all(packed, "space", 0, 0, tiled=True)
    begin, mine = call(
        unpack_kernel, (shape(2, ROWS, NX, LAST), shape(3, PART, NX, LAST)), [VMEM], (VMEM, VMEM), [], 16
    )(got)
    other = swap(mine)

    field = pltpu.VMEM((2, HELD, NX, LAST), F32)
    weights, base, give, g = call(
        relax_kernel,
        (pltpu.VMEM((HELD, 2 * PAIR, NX, LAST), F32), half, shape(4, HALF, NX, LAST), half),
        [VMEM] * 4,
        (VMEM,) * 4,
        [pltpu.VMEM((3, ROWS, NX, LAST), F32), pltpu.VMEM((HELD, 8, LAST), F32), field, field, field],
        24,
    )(begin, mine, other, inlet)
    taken = swap(give)
    u = base + taken[:2]

    def leap(own, near, swapped, *rims, second=True):
        outs = (half,) * (1 + second) + rims
        return call(leap_kernel, outs, [VMEM] * 4, (VMEM,) * len(outs), [field, field], 20, 2 + 3 * second)(
            own, near, swapped, weights
        )

    def beside(value):
        return sent(value, SAME, 1, 1)

    rim4, rim2 = shape(2, 4, NX, LAST), shape(2, 2, NX, LAST)
    def exchanged(own, inner, outer, *arrived):
        return lax.optimization_barrier((own, beside(outer), swap(inner)) + arrived)

    a0 = sent(u, onward(0), 0, 0)
    u1, u2 = leap(u, beside(u), swap(u))
    a1, a2 = sent(u1, onward(1), 0, 0), sent(u2, onward(2), 0, 0)
    *operands, a0 = exchanged(u2, u2, u2, a0)
    u3, u4 = leap(*operands)
    a3, a4 = sent(u3, onward(3), 0, 0), sent(u4, onward(4), 0, 0)
    *operands, a1, a2 = exchanged(u4, u4, u4, a1, a2)
    u5, u6, inner, outer = leap(*operands, rim4, rim4)
    a5, a6 = sent(u5, onward(5), 0, 0), sent(u6, onward(6), 0, 0)
    *operands, a3, a4 = exchanged(u6, inner, outer, a3, a4)
    (u7,) = leap(*operands, second=False)
    arrived = (a0, a1, a2, a3, a4, a5, a6)
    c, inner, outer = call(sum_kernel, (half, rim2, rim2), [VMEM] * 8, (VMEM,) * 3, [], 16)(u7, *arrived)
    parcel = shape(BRICKS, 2 * HALF * PLANES, LAST)
    keep, send = call(last_kernel, (parcel, parcel), [VMEM] * 6, (VMEM,) * 2, [field, field, field], 22)(
        c, beside(outer), swap(inner), g, taken, weights
    )
    back = lax.all_to_all(jnp.concatenate([keep, swap(send)], axis=1), "space", 0, 0, tiled=True)
    return call(restore_kernel, shape(1, 2, PLANES, MIDDLE, LAST), [VMEM], VMEM, [], 16)(back)


def solution(mesh):
    fine = Mesh(mesh.devices.reshape(SLABS // 2, 2, BRICKS), AXES)
    slabs = ("chip", "core")
    return jax.shard_map(
        shards,
        mesh=fine,
        in_specs=(
            P(None, "space", None, None),
            P(slabs, None, "space", None, None),
            P(None, "space", None, None),
            P("space", None, None),
            P(),
        ),
        out_specs=P(slabs, None, "space", None, None),
        check_vma=False,
    )
```

```python
import functools

import jax
import jax.numpy as jnp
from jax import lax
from jax.experimental import pallas as pl
from jax.experimental.pallas import tpu as pltpu
from jax.sharding import Mesh, PartitionSpec as P

SLABS = 16
BRICKS = 8
PLANES = 4
NX = 32
MIDDLE = 128
LAST = 128
STRIP = 16
CHIPS = SLABS // 2
RING = 4
HALF = 8
EDGE = 10
ROWS = STRIP + 2 * EDGE
HELD = ROWS + 4
PART = ROWS // 2

RATE_ALONG = 4.0
RATE_ACROSS = 0.5
ADVECTION = 1.0
DAMPING = 0.8
COARSE_FACTOR = 4.0

ORDER = [0, 2, 4, 6, 7, 5, 3, 1]
AXES = ("chip", "core", "space")
MIB = 1 << 20

VMEM = pl.BlockSpec(memory_space=pltpu.VMEM)
HBM = pl.BlockSpec(memory_space=pltpu.HBM)
PAIR = 9
FINE, COARSE = 7, 8
F32 = jnp.float32


def shape(*dims):
    return jax.ShapeDtypeStruct(dims, F32)


def call(body, outs, in_specs, out_specs, scratch, limit, us=1):
    return pl.pallas_call(
        body,
        cost_estimate=pl.CostEstimate(flops=0, bytes_accessed=us * (3 << 20), transcendentals=0),
        out_shape=outs,
        in_specs=in_specs,
        out_specs=out_specs,
        scratch_shapes=scratch,
        compiler_params=pltpu.CompilerParams(vmem_limit_bytes=limit * MIB),
    )


def position():
    chip, core, space = (lax.axis_index(a) for a in AXES)
    y, odd = space // 2, space % 2
    return core, jnp.where(odd == 0, y, BRICKS - 1 - y), chip * 2 + core


def pack_kernel(startup, guess, conduct, couple, out, padded, state, others, sems):
    core, _, slab = position()
    last = slab == SLABS - 1
    from_startup = [pltpu.make_async_copy(startup.at[i], state.at[i], sems.at[i]) for i in range(2)]
    from_guess = [pltpu.make_async_copy(guess.at[0, i], state.at[i], sems.at[i]) for i in range(2)]
    copies = [pltpu.make_async_copy(conduct.at[i], others.at[i], sems.at[2 + i]) for i in range(2)]
    copies.append(pltpu.make_async_copy(couple, others.at[2], sems.at[4]))

    @pl.when(last)
    def _():
        for copy in from_startup:
            copy.start()

    @pl.when(jnp.logical_not(last))
    def _():
        for copy in from_guess:
            copy.start()

    for copy in copies:
        copy.start()
    zero = jnp.zeros((EDGE * PLANES, LAST), F32)
    end = (EDGE + MIDDLE) * PLANES
    for i in range(5):
        padded[i, 0 : EDGE * PLANES] = zero
        padded[i, end : end + EDGE * PLANES] = zero
        (from_guess + copies)[i].wait()
        for plane in range(PLANES):
            for first in range(0, MIDDLE, 8):
                value = state[i, plane, first : first + 8] if i < 2 else others[i - 2, plane, first : first + 8]
                padded[i, pl.ds((EDGE + first) * PLANES + plane, 8, stride=PLANES), :] = value
    tall, part = (STRIP + 2 * EDGE) * PLANES, PART * PLANES
    for b in range(BRICKS):
        s = ORDER[b]
        start = (STRIP * b) * PLANES
        for i in range(2):
            out[s, i * tall : (i + 1) * tall] = padded[i, start : start + tall]
        start = pl.multiple_of(STRIP * b * PLANES + part * core, 32)
        for i in range(3):
            at = 2 * tall + i * part
            out[s, at : at + part] = padded[2 + i, pl.ds(start, part)]


def unpack_kernel(got, state, coefficients):
    low = lax.broadcasted_iota(jnp.int32, (8, LAST), 0) < PLANES

    def widen(out, i, at, rows):
        for y in range(0, rows, 2):
            for t in range(NX // 8):
                a = got[2 * t, at + PLANES * y : at + PLANES * y + 8]
                b = got[2 * t + 1, at + PLANES * y : at + PLANES * y + 8]
                out[i, y, 8 * t : 8 * t + 8] = jnp.where(low, a, pltpu.roll(b, 4, 0))
                out[i, y + 1, 8 * t : 8 * t + 8] = jnp.where(low, pltpu.roll(a, 4, 0), b)

    tall, part = (STRIP + 2 * EDGE) * PLANES, PART * PLANES
    for i in range(2):
        widen(state, i, i * tall, STRIP + 2 * EDGE)
    for i in range(3):
        widen(coefficients, i, 2 * tall + i * part, PART)


def restore_kernel(got, out):
    core, _, _ = position()
    for part in range(2):
        half = core if part == 0 else 1 - core
        for b in range(BRICKS):
            first = pl.multiple_of(STRIP * b + HALF * half, HALF)
            for i in range(2):
                for plane in range(PLANES):
                    at = (part * 2 + i) * HALF * PLANES + plane
                    out[0, i, plane, pl.ds(first, HALF), :] = got[ORDER[b], pl.ds(at, HALF, stride=PLANES), :]


def row_sweep(y, state, weights, earlier, step, source):
    centre = (state[0, y], state[1, y])
    out = []
    for i in range(2):
        v = centre[i]
        w = lambda k: weights[y, PAIR * i + k]
        along = w(0) * pltpu.roll(v, 1, 0) + w(1) * pltpu.roll(v, NX - 1, 0)
        middle = w(2) * state[i, y - 1] + w(3) * state[i, y + 1]
        across = w(4) * pltpu.roll(v, 1, 1) + w(5) * pltpu.roll(v, LAST - 1, 1)
        begin = v if earlier is None else earlier[i, y]
        if step == COARSE:
            begin = (1.0 / COARSE_FACTOR) * begin
        gain = (along + middle) + (across + (w(6) * centre[1 - i] + begin))
        if i == 1 and source is not None:
            gain = jnp.concatenate([gain[:8] + source[y], gain[8:]], axis=0)
        out.append((1.0 - DAMPING) * v + w(step) * gain)
    return out


def sweep(state, weights, earlier, into, low, high, step, source=None, unroll=4):
    def rows(k, carry):
        for u in range(unroll):
            y = low + unroll * k + u
            new = row_sweep(y, state, weights, earlier, step, source)
            into[0, y] = new[0]
            into[1, y] = new[1]
        return carry

    lax.fori_loop(0, (high - low + unroll - 1) // unroll, rows, 0)


def advances(count, e, v, weights, low, high, step, source=None):
    def one(m, carry):
        sweep(e, weights, None, v, low + 2 * m + 1, high - 2 * m - 1, step, source)
        sweep(v, weights, e, e, low + 2 * m + 2, high - 2 * m - 2, step, source)
        return carry

    lax.fori_loop(0, count, one, 0)


def relax_kernel(begin, mine, other, inlet, w, base, give, own, c, feed, e, v, e0):
    core, strip, slab = position()
    c[:, pl.ds(PART * core, PART)] = mine[...]
    c[:, pl.ds(PART - PART * core, PART)] = other[...]
    e[:, :ROWS] = begin[...]
    e0[:, :ROWS] = begin[...]

    plane = lax.broadcasted_iota(jnp.int32, (NX, LAST), 0)
    column = lax.broadcasted_iota(jnp.int32, (NX, LAST), 1)
    top = lax.broadcasted_iota(jnp.int32, (8, LAST), 0) == 0

    def weigh(r, carry):
        y = strip * STRIP - EDGE + r
        lower = jnp.where(y == 0, 0.0, 1.0).astype(F32)
        upper = jnp.where(y == MIDDLE - 1, 0.0, 1.0).astype(F32)
        exchange = c[2, r]
        warmth = inlet[pl.ds(jnp.clip(y, 0, MIDDLE - 1), 1), :]
        for i in range(2):
            here = c[i, r]
            xm = jnp.where(plane == 0, 0.0, pltpu.roll(here, 1, 0))
            xp = jnp.where(plane == NX - 1, 0.0, pltpu.roll(here, NX - 1, 0))
            zm = jnp.where(column == 0, 0.0, pltpu.roll(here, 1, 1))
            zp = jnp.where(column == LAST - 1, 0.0, pltpu.roll(here, LAST - 1, 1))
            half_along, half_across = 0.5 * RATE_ALONG, 0.5 * RATE_ACROSS
            wxm = half_along * (here + xm)
            if i == 1:
                wxm = wxm + ADVECTION
            wxp = half_along * (here + xp)
            wym = half_across * (here + c[i, r - 1])
            wyp = half_across * (here + c[i, r + 1])
            wzm = half_across * (here + zm)
            wzp = half_across * (here + zp)
            outflow = wxm + wxp + wym + wyp + wzm + wzp + exchange
            inner = (
                jnp.where(plane == 0, 0.0, wxm),
                jnp.where(plane == NX - 1, 0.0, wxp),
                wym * lower,
                wyp * upper,
                jnp.where(column == 0, 0.0, wzm),
                jnp.where(column == LAST - 1, 0.0, wzp),
                exchange,
            )
            for k in range(7):
                w[r, PAIR * i + k] = inner[k]
            w[r, PAIR * i + FINE] = DAMPING / (1.0 + outflow)
            w[r, PAIR * i + COARSE] = (DAMPING * COARSE_FACTOR) / (1.0 + COARSE_FACTOR * outflow)
            if i == 1:
                feed[r] = jnp.where(top, wxm[:8] * warmth, 0.0)
        return carry

    lax.fori_loop(1, ROWS - 1, weigh, 0)
    sweep(e0, w, None, v, EDGE - 3, EDGE + STRIP + 3, COARSE)
    sweep(v, w, e0, e0, EDGE - 2, EDGE + STRIP + 2, COARSE)
    advances(4, e, v, w, 0, ROWS, FINE, feed)
    keep = jnp.where(slab == SLABS - 1, 0.0, 1.0).astype(F32)
    rows = pl.ds(EDGE - 2, STRIP + 4)
    e[:, rows] = e[:, rows] - keep * e0[:, rows]
    sweep(e, w, None, v, EDGE - 1, EDGE + STRIP + 1, COARSE)
    sweep(v, w, e, e0, EDGE, EDGE + STRIP, COARSE)
    joined = jnp.where(slab == SLABS - 2, 0.0, 1.0).astype(F32)
    near, far = pl.ds(EDGE, HALF), pl.ds(EDGE + HALF, HALF)
    base[...] = jnp.where(core == 0, joined * e0[:, near], e[:, far])
    give[0:2] = jnp.where(core == 0, joined * e0[:, far], e[:, near])
    give[2:4] = e[:, far]
    own[...] = e[:, near]


def place(core, state, middle, inward, outward):
    many, rim = inward.shape[1], outward.shape[1]
    state[:, pl.ds(middle + HALF - (HALF + many) * core, many)] = inward[...]
    state[:, pl.ds(middle - rim + (HALF + rim) * core, rim)] = outward[...]


def leap_kernel(own, near, swapped, w, odd, *refs):
    core, _, _ = position()
    middle = EDGE + HALF * core
    rows = pl.ds(middle, HALF)
    *more, e, v = refs
    reach = HALF if more else HALF // 2
    e[:, rows] = own[...]
    place(core, e, middle, swapped, near)
    advances(2, e, v, w, middle - reach, middle + HALF + reach, COARSE)
    odd[...] = e[:, rows]
    if more:
        even, *rims = more
        advances(2, e, v, w, middle - 4, middle + HALF + 4, COARSE)
        even[...] = e[:, rows]
        if rims:
            inner, outer = rims
            inner[...] = even[:, pl.ds(4 - 4 * core, 4)]
            outer[...] = even[:, pl.ds(4 * core, 4)]


def share_kernel(*refs):
    *arrived, mine, theirs = refs
    _, _, slab = position()
    chip = slab // 2
    half = chip // RING
    ours, other = 0.0, 0.0
    for power, ref in enumerate(arrived):
        source = half * RING + lax.rem(chip + 2 * RING - power - 1, RING)
        target = lax.rem(source + 1, CHIPS) + power
        value = jnp.where(target < CHIPS, ref[...], 0.0)
        at_home = target // RING == half
        ours = ours + jnp.where(at_home, value, 0.0)
        other = other + jnp.where(at_home, 0.0, value)
    mine[...] = ours
    theirs[...] = other


def sum_kernel(local, *refs):
    core, _, slab = position()
    *arrived, out, inner, outer = refs
    total = arrived[0][...]
    for ref in arrived[1:]:
        total = total + ref[...]
    out[...] = total + jnp.where(slab // 2 == CHIPS - 1, local[...], 0.0)
    inner[...] = out[:, pl.ds(6 - 6 * core, 2)]
    outer[...] = out[:, pl.ds(6 * core, 2)]


def last_kernel(own, near, swapped, g, taken, w, keep, send, r, v, e):
    core, _, _ = position()
    middle = EDGE + HALF * core
    rows = pl.ds(middle, HALF)
    r[:, rows] = own[...]
    place(core, r, middle, swapped, near)
    sweep(r, w, None, v, middle - 1, middle + HALF + 1, COARSE)
    sweep(v, w, r, e, middle, middle + HALF, COARSE)
    e[:, rows] = e[:, rows] + jnp.where(core == 0, g[...], taken[2:4])
    low = lax.broadcasted_iota(jnp.int32, (8, LAST), 0) < PLANES
    for out, other in ((keep, 0), (send, 1)):
        pick = lambda *at: jnp.where(core == other, r[at], e[at])
        for i in range(2):
            for y in range(0, HALF, 2):
                at = (i * HALF + y) * PLANES
                for t in range(NX // 8):
                    a = pick(i, middle + y, slice(8 * t, 8 * t + 8))
                    b = pick(i, middle + y + 1, slice(8 * t, 8 * t + 8))
                    out[2 * t, at : at + 8] = jnp.where(low, a, pltpu.roll(b, 4, 0))
                    out[2 * t + 1, at : at + 8] = jnp.where(low, pltpu.roll(a, 4, 0), b)


def index(chip, core, strip):
    return (chip * 2 + core) * BRICKS + ORDER[strip]


def sent(value, chips, flip, shift):
    pairs = []
    for source, target in chips:
        for core in range(2):
            for strip in range(BRICKS):
                beside = strip + shift * (1 if core == 0 else -1)
                if 0 <= beside < BRICKS:
                    pairs.append((index(source, core ^ flip, strip), index(target, core, beside)))
    return lax.ppermute(value, AXES, pairs)


SAME = [(c, c) for c in range(CHIPS)]
ACROSS = [((c + RING) % CHIPS, c) for c in range(CHIPS)]


def onward(power):
    return [((j - 1) % CHIPS, j + power) for j in range(CHIPS - power)]


def ringward(power):
    pairs = []
    for c in range(CHIPS):
        target = (c + 1) % CHIPS + power
        if target < CHIPS:
            pairs.append((c, c // RING * RING + target % RING))
    return pairs


def swap(value):
    return sent(value, SAME, 1, 0)


def shards(startup, guess, conduct, couple, inlet):
    chunk = (2 * ROWS + 3 * PART) * PLANES
    half = shape(2, HALF, NX, LAST)
    arrays = [pltpu.with_memory_space_constraint(a, pltpu.HBM) for a in (startup, guess, conduct, couple)]
    packed = call(
        pack_kernel,
        shape(BRICKS, chunk, LAST),
        [HBM] * 4,
        VMEM,
        [
            pltpu.VMEM((5, (MIDDLE + 2 * EDGE) * PLANES, LAST), F32),
            pltpu.VMEM((2, PLANES, MIDDLE, LAST), F32),
            pltpu.VMEM((3, PLANES, MIDDLE, LAST), F32),
            pltpu.SemaphoreType.DMA((5,)),
        ],
        16,
    )(*arrays)
    got = lax.all_to_all(packed, "space", 0, 0, tiled=True)
    begin, mine = call(
        unpack_kernel, (shape(2, ROWS, NX, LAST), shape(3, PART, NX, LAST)), [VMEM], (VMEM, VMEM), [], 16
    )(got)
    other = swap(mine)

    field = pltpu.VMEM((2, HELD, NX, LAST), F32)
    weights, base, give, g = call(
        relax_kernel,
        (pltpu.VMEM((HELD, 2 * PAIR, NX, LAST), F32), half, shape(4, HALF, NX, LAST), half),
        [VMEM] * 4,
        (VMEM,) * 4,
        [pltpu.VMEM((3, ROWS, NX, LAST), F32), pltpu.VMEM((HELD, 8, LAST), F32), field, field, field],
        24,
    )(begin, mine, other, inlet)
    taken = swap(give)
    u = base + taken[:2]

    def leap(own, near, swapped, *rims, second=True):
        outs = (half,) * (1 + second) + rims
        return call(leap_kernel, outs, [VMEM] * 4, (VMEM,) * len(outs), [field, field], 20, 2 + 3 * second)(
            own, near, swapped, weights
        )

    def beside(value):
        return sent(value, SAME, 1, 1)

    rim4, rim2 = shape(2, 4, NX, LAST), shape(2, 2, NX, LAST)
    def exchanged(own, inner, outer, *arrived):
        return lax.optimization_barrier((own, beside(outer), swap(inner)) + arrived)

    a0 = sent(u, ringward(0), 0, 0)
    u1, u2 = leap(u, beside(u), swap(u))
    a1, a2 = sent(u1, ringward(1), 0, 0), sent(u2, ringward(2), 0, 0)
    *operands, a0 = exchanged(u2, u2, u2, a0)
    u3, u4 = leap(*operands)
    a4 = sent(u4, ringward(4), 0, 0)
    *operands, a1, a2 = exchanged(u4, u4, u4, a1, a2)
    u5, u6, inner, outer = leap(*operands, rim4, rim4)
    a5, a6 = sent(u5, onward(5), 0, 0), sent(u6, onward(6), 0, 0)
    mine, theirs = call(share_kernel, (half, half), [VMEM] * 5, (VMEM,) * 2, [], 16)(a0, a1, a2, u3, a4)
    *operands, mine, theirs = exchanged(u6, inner, outer, mine, theirs)
    (u7,) = leap(*operands, second=False)
    arrived = (mine, sent(theirs, ACROSS, 0, 0), a5, a6)
    c, inner, outer = call(sum_kernel, (half, rim2, rim2), [VMEM] * 5, (VMEM,) * 3, [], 16)(u7, *arrived)
    parcel = shape(BRICKS, 2 * HALF * PLANES, LAST)
    keep, send = call(last_kernel, (parcel, parcel), [VMEM] * 6, (VMEM,) * 2, [field, field, field], 22)(
        c, beside(outer), swap(inner), g, taken, weights
    )
    back = lax.all_to_all(jnp.concatenate([keep, swap(send)], axis=1), "space", 0, 0, tiled=True)
    return call(restore_kernel, shape(1, 2, PLANES, MIDDLE, LAST), [VMEM], VMEM, [], 16)(back)


def solution(mesh):
    fine = Mesh(mesh.devices.reshape(SLABS // 2, 2, BRICKS), AXES)
    slabs = ("chip", "core")
    return jax.shard_map(
        shards,
        mesh=fine,
        in_specs=(
            P(None, "space", None, None),
            P(slabs, None, "space", None, None),
            P(None, "space", None, None),
            P("space", None, None),
            P(),
        ),
        out_specs=P(slabs, None, "space", None, None),
        check_vma=False,
    )
```

```python
import functools

import jax
import jax.numpy as jnp
from jax import lax
from jax.experimental import pallas as pl
from jax.experimental.pallas import tpu as pltpu
from jax.sharding import Mesh, PartitionSpec as P

SLABS = 16
BRICKS = 8
PLANES = 4
NX = 32
MIDDLE = 128
LAST = 128
STRIP = 16
CHIPS = SLABS // 2
RING = 4
HALF = 8
EDGE = 10
ROWS = STRIP + 2 * EDGE
HELD = ROWS + 4
PART = ROWS // 2

RATE_ALONG = 4.0
RATE_ACROSS = 0.5
ADVECTION = 1.0
DAMPING = 0.8
COARSE_FACTOR = 4.0

ORDER = [0, 2, 4, 6, 7, 5, 3, 1]
AXES = ("chip", "core", "space")
MIB = 1 << 20

VMEM = pl.BlockSpec(memory_space=pltpu.VMEM)
HBM = pl.BlockSpec(memory_space=pltpu.HBM)
PAIR = 9
FINE, COARSE = 7, 8
F32 = jnp.float32


def shape(*dims):
    return jax.ShapeDtypeStruct(dims, F32)


def call(body, outs, in_specs, out_specs, scratch, limit, us=1):
    return pl.pallas_call(
        body,
        cost_estimate=pl.CostEstimate(flops=0, bytes_accessed=us * (3 << 20), transcendentals=0),
        out_shape=outs,
        in_specs=in_specs,
        out_specs=out_specs,
        scratch_shapes=scratch,
        compiler_params=pltpu.CompilerParams(vmem_limit_bytes=limit * MIB),
    )


def position():
    chip, core, space = (lax.axis_index(a) for a in AXES)
    y, odd = space // 2, space % 2
    return core, jnp.where(odd == 0, y, BRICKS - 1 - y), chip * 2 + core


def pack_kernel(startup, guess, conduct, couple, out, padded, state, others, sems):
    core, _, slab = position()
    last = slab == SLABS - 1
    from_startup = [pltpu.make_async_copy(startup.at[i], state.at[i], sems.at[i]) for i in range(2)]
    from_guess = [pltpu.make_async_copy(guess.at[0, i], state.at[i], sems.at[i]) for i in range(2)]
    copies = [pltpu.make_async_copy(conduct.at[i], others.at[i], sems.at[2 + i]) for i in range(2)]
    copies.append(pltpu.make_async_copy(couple, others.at[2], sems.at[4]))

    @pl.when(last)
    def _():
        for copy in from_startup:
            copy.start()

    @pl.when(jnp.logical_not(last))
    def _():
        for copy in from_guess:
            copy.start()

    for copy in copies:
        copy.start()
    zero = jnp.zeros((EDGE * PLANES, LAST), F32)
    end = (EDGE + MIDDLE) * PLANES
    for i in range(5):
        padded[i, 0 : EDGE * PLANES] = zero
        padded[i, end : end + EDGE * PLANES] = zero
        (from_guess + copies)[i].wait()
        for plane in range(PLANES):
            for first in range(0, MIDDLE, 8):
                value = state[i, plane, first : first + 8] if i < 2 else others[i - 2, plane, first : first + 8]
                padded[i, pl.ds((EDGE + first) * PLANES + plane, 8, stride=PLANES), :] = value
    tall, part = (STRIP + 2 * EDGE) * PLANES, PART * PLANES
    for b in range(BRICKS):
        s = ORDER[b]
        start = (STRIP * b) * PLANES
        for i in range(2):
            out[s, i * tall : (i + 1) * tall] = padded[i, start : start + tall]
        start = pl.multiple_of(STRIP * b * PLANES + part * core, 32)
        for i in range(3):
            at = 2 * tall + i * part
            out[s, at : at + part] = padded[2 + i, pl.ds(start, part)]


def unpack_kernel(got, state, coefficients):
    low = lax.broadcasted_iota(jnp.int32, (8, LAST), 0) < PLANES

    def widen(out, i, at, rows):
        for y in range(0, rows, 2):
            for t in range(NX // 8):
                a = got[2 * t, at + PLANES * y : at + PLANES * y + 8]
                b = got[2 * t + 1, at + PLANES * y : at + PLANES * y + 8]
                out[i, y, 8 * t : 8 * t + 8] = jnp.where(low, a, pltpu.roll(b, 4, 0))
                out[i, y + 1, 8 * t : 8 * t + 8] = jnp.where(low, pltpu.roll(a, 4, 0), b)

    tall, part = (STRIP + 2 * EDGE) * PLANES, PART * PLANES
    for i in range(2):
        widen(state, i, i * tall, STRIP + 2 * EDGE)
    for i in range(3):
        widen(coefficients, i, 2 * tall + i * part, PART)


def restore_kernel(got, out):
    core, _, _ = position()
    for part in range(2):
        half = core if part == 0 else 1 - core
        for b in range(BRICKS):
            first = pl.multiple_of(STRIP * b + HALF * half, HALF)
            for i in range(2):
                for plane in range(PLANES):
                    at = (part * 2 + i) * HALF * PLANES + plane
                    out[0, i, plane, pl.ds(first, HALF), :] = got[ORDER[b], pl.ds(at, HALF, stride=PLANES), :]


def row_sweep(y, state, weights, earlier, step, source):
    centre = (state[0, y], state[1, y])
    out = []
    for i in range(2):
        v = centre[i]
        w = lambda k: weights[y, PAIR * i + k]
        along = w(0) * pltpu.roll(v, 1, 0) + w(1) * pltpu.roll(v, NX - 1, 0)
        middle = w(2) * state[i, y - 1] + w(3) * state[i, y + 1]
        across = w(4) * pltpu.roll(v, 1, 1) + w(5) * pltpu.roll(v, LAST - 1, 1)
        begin = v if earlier is None else earlier[i, y]
        if step == COARSE:
            begin = (1.0 / COARSE_FACTOR) * begin
        gain = (along + middle) + (across + (w(6) * centre[1 - i] + begin))
        if i == 1 and source is not None:
            gain = jnp.concatenate([gain[:8] + source[y], gain[8:]], axis=0)
        out.append((1.0 - DAMPING) * v + w(step) * gain)
    return out


def sweep(state, weights, earlier, into, low, high, step, source=None, unroll=4):
    def rows(k, carry):
        for u in range(unroll):
            y = low + unroll * k + u
            new = row_sweep(y, state, weights, earlier, step, source)
            into[0, y] = new[0]
            into[1, y] = new[1]
        return carry

    lax.fori_loop(0, (high - low + unroll - 1) // unroll, rows, 0)


def advances(count, e, v, weights, low, high, step, source=None):
    def one(m, carry):
        sweep(e, weights, None, v, low + 2 * m + 1, high - 2 * m - 1, step, source)
        sweep(v, weights, e, e, low + 2 * m + 2, high - 2 * m - 2, step, source)
        return carry

    lax.fori_loop(0, count, one, 0)


def relax_kernel(begin, mine, other, inlet, w, base, give, own, c, feed, e, v, e0):
    core, strip, slab = position()
    c[:, pl.ds(PART * core, PART)] = mine[...]
    c[:, pl.ds(PART - PART * core, PART)] = other[...]
    e[:, :ROWS] = begin[...]
    e0[:, :ROWS] = begin[...]

    plane = lax.broadcasted_iota(jnp.int32, (NX, LAST), 0)
    column = lax.broadcasted_iota(jnp.int32, (NX, LAST), 1)
    top = lax.broadcasted_iota(jnp.int32, (8, LAST), 0) == 0

    def weigh(r, carry):
        y = strip * STRIP - EDGE + r
        lower = jnp.where(y == 0, 0.0, 1.0).astype(F32)
        upper = jnp.where(y == MIDDLE - 1, 0.0, 1.0).astype(F32)
        exchange = c[2, r]
        warmth = inlet[pl.ds(jnp.clip(y, 0, MIDDLE - 1), 1), :]
        for i in range(2):
            here = c[i, r]
            xm = jnp.where(plane == 0, 0.0, pltpu.roll(here, 1, 0))
            xp = jnp.where(plane == NX - 1, 0.0, pltpu.roll(here, NX - 1, 0))
            zm = jnp.where(column == 0, 0.0, pltpu.roll(here, 1, 1))
            zp = jnp.where(column == LAST - 1, 0.0, pltpu.roll(here, LAST - 1, 1))
            half_along, half_across = 0.5 * RATE_ALONG, 0.5 * RATE_ACROSS
            wxm = half_along * (here + xm)
            if i == 1:
                wxm = wxm + ADVECTION
            wxp = half_along * (here + xp)
            wym = half_across * (here + c[i, r - 1])
            wyp = half_across * (here + c[i, r + 1])
            wzm = half_across * (here + zm)
            wzp = half_across * (here + zp)
            outflow = wxm + wxp + wym + wyp + wzm + wzp + exchange
            inner = (
                jnp.where(plane == 0, 0.0, wxm),
                jnp.where(plane == NX - 1, 0.0, wxp),
                wym * lower,
                wyp * upper,
                jnp.where(column == 0, 0.0, wzm),
                jnp.where(column == LAST - 1, 0.0, wzp),
                exchange,
            )
            for k in range(7):
                w[r, PAIR * i + k] = inner[k]
            w[r, PAIR * i + FINE] = DAMPING / (1.0 + outflow)
            w[r, PAIR * i + COARSE] = (DAMPING * COARSE_FACTOR) / (1.0 + COARSE_FACTOR * outflow)
            if i == 1:
                feed[r] = jnp.where(top, wxm[:8] * warmth, 0.0)
        return carry

    lax.fori_loop(1, ROWS - 1, weigh, 0)
    sweep(e0, w, None, v, EDGE - 3, EDGE + STRIP + 3, COARSE)
    sweep(v, w, e0, e0, EDGE - 2, EDGE + STRIP + 2, COARSE)
    advances(4, e, v, w, 0, ROWS, FINE, feed)
    keep = jnp.where(slab == SLABS - 1, 0.0, 1.0).astype(F32)
    rows = pl.ds(EDGE - 2, STRIP + 4)
    e[:, rows] = e[:, rows] - keep * e0[:, rows]
    sweep(e, w, None, v, EDGE - 1, EDGE + STRIP + 1, COARSE)
    sweep(v, w, e, e0, EDGE, EDGE + STRIP, COARSE)
    joined = jnp.where(slab == SLABS - 2, 0.0, 1.0).astype(F32)
    near, far = pl.ds(EDGE, HALF), pl.ds(EDGE + HALF, HALF)
    base[...] = jnp.where(core == 0, joined * e0[:, near], e[:, far])
    give[0:2] = jnp.where(core == 0, joined * e0[:, far], e[:, near])
    give[2:4] = e[:, far]
    own[...] = e[:, near]


def place(core, state, middle, inward, outward):
    many, rim = inward.shape[1], outward.shape[1]
    state[:, pl.ds(middle + HALF - (HALF + many) * core, many)] = inward[...]
    state[:, pl.ds(middle - rim + (HALF + rim) * core, rim)] = outward[...]


def leap_kernel(own, near, swapped, w, odd, *refs):
    core, _, _ = position()
    middle = EDGE + HALF * core
    rows = pl.ds(middle, HALF)
    *more, e, v = refs
    reach = HALF if more else HALF // 2
    e[:, rows] = own[...]
    place(core, e, middle, swapped, near)
    advances(2, e, v, w, middle - reach, middle + HALF + reach, COARSE)
    odd[...] = e[:, rows]
    if more:
        even, *rims = more
        advances(2, e, v, w, middle - 4, middle + HALF + 4, COARSE)
        even[...] = e[:, rows]
        if rims:
            inner, outer = rims
            inner[...] = even[:, pl.ds(4 - 4 * core, 4)]
            outer[...] = even[:, pl.ds(4 * core, 4)]


def share_kernel(*refs):
    *arrived, mine, theirs = refs
    _, _, slab = position()
    chip = slab // 2
    half = chip // RING
    ours, other = 0.0, 0.0
    for power, ref in enumerate(arrived):
        source = half * RING + lax.rem(chip + 2 * RING - power - 1, RING)
        target = lax.rem(source + 1, CHIPS) + power
        value = jnp.where(target < CHIPS, ref[...], 0.0)
        at_home = target // RING == half
        ours = ours + jnp.where(at_home, value, 0.0)
        other = other + jnp.where(at_home, 0.0, value)
    mine[...] = ours
    theirs[...] = other


def sum_kernel(mine, arrived, out, inner, outer):
    core, _, _ = position()
    out[...] = mine[...] + arrived[...]
    inner[...] = out[:, pl.ds(6 - 6 * core, 2)]
    outer[...] = out[:, pl.ds(6 * core, 2)]


def last_kernel(own, near, swapped, g, taken, w, keep, send, r, v, e):
    core, _, _ = position()
    middle = EDGE + HALF * core
    rows = pl.ds(middle, HALF)
    r[:, rows] = own[...]
    place(core, r, middle, swapped, near)
    sweep(r, w, None, v, middle - 1, middle + HALF + 1, COARSE)
    sweep(v, w, r, e, middle, middle + HALF, COARSE)
    e[:, rows] = e[:, rows] + jnp.where(core == 0, g[...], taken[2:4])
    low = lax.broadcasted_iota(jnp.int32, (8, LAST), 0) < PLANES
    for out, other in ((keep, 0), (send, 1)):
        pick = lambda *at: jnp.where(core == other, r[at], e[at])
        for i in range(2):
            for y in range(0, HALF, 2):
                at = (i * HALF + y) * PLANES
                for t in range(NX // 8):
                    a = pick(i, middle + y, slice(8 * t, 8 * t + 8))
                    b = pick(i, middle + y + 1, slice(8 * t, 8 * t + 8))
                    out[2 * t, at : at + 8] = jnp.where(low, a, pltpu.roll(b, 4, 0))
                    out[2 * t + 1, at : at + 8] = jnp.where(low, pltpu.roll(a, 4, 0), b)


def index(chip, core, strip):
    return (chip * 2 + core) * BRICKS + ORDER[strip]


def sent(value, chips, flip, shift):
    pairs = []
    for source, target in chips:
        for core in range(2):
            for strip in range(BRICKS):
                beside = strip + shift * (1 if core == 0 else -1)
                if 0 <= beside < BRICKS:
                    pairs.append((index(source, core ^ flip, strip), index(target, core, beside)))
    return lax.ppermute(value, AXES, pairs)


SAME = [(c, c) for c in range(CHIPS)]
ACROSS = [((c + RING) % CHIPS, c) for c in range(CHIPS)]


def needed(power):
    return [(c, c) for c in range(CHIPS) if (c + 1) % CHIPS + power < CHIPS]


def ringward(power):
    return [(c, c // RING * RING + ((c + 1) % CHIPS + power) % RING) for c, _ in needed(power)]


def swap(value, chips=SAME):
    return sent(value, chips, 1, 0)


def beside(value, chips=SAME):
    return sent(value, chips, 1, 1)


def shards(startup, guess, conduct, couple, inlet):
    chunk = (2 * ROWS + 3 * PART) * PLANES
    half = shape(2, HALF, NX, LAST)
    arrays = [pltpu.with_memory_space_constraint(a, pltpu.HBM) for a in (startup, guess, conduct, couple)]
    packed = call(
        pack_kernel,
        shape(BRICKS, chunk, LAST),
        [HBM] * 4,
        VMEM,
        [
            pltpu.VMEM((5, (MIDDLE + 2 * EDGE) * PLANES, LAST), F32),
            pltpu.VMEM((2, PLANES, MIDDLE, LAST), F32),
            pltpu.VMEM((3, PLANES, MIDDLE, LAST), F32),
            pltpu.SemaphoreType.DMA((5,)),
        ],
        16,
    )(*arrays)
    got = lax.all_to_all(packed, "space", 0, 0, tiled=True)
    begin, mine = call(
        unpack_kernel, (shape(2, ROWS, NX, LAST), shape(3, PART, NX, LAST)), [VMEM], (VMEM, VMEM), [], 16
    )(got)
    other = swap(mine)

    field = pltpu.VMEM((2, HELD, NX, LAST), F32)
    weights, base, give, g = call(
        relax_kernel,
        (pltpu.VMEM((HELD, 2 * PAIR, NX, LAST), F32), half, shape(4, HALF, NX, LAST), half),
        [VMEM] * 4,
        (VMEM,) * 4,
        [pltpu.VMEM((3, ROWS, NX, LAST), F32), pltpu.VMEM((HELD, 8, LAST), F32), field, field, field],
        24,
    )(begin, mine, other, inlet)
    taken = swap(give)
    u = base + taken[:2]

    def leap(own, near, swapped, *rims, second=True):
        outs = (half,) * (1 + second) + rims
        return call(leap_kernel, outs, [VMEM] * 4, (VMEM,) * len(outs), [field, field], 20, 2 + 3 * second)(
            own, near, swapped, weights
        )

    rim4, rim2 = shape(2, 4, NX, LAST), shape(2, 2, NX, LAST)
    def exchanged(power, own, inner, outer, *arrived):
        chips = needed(power)
        return lax.optimization_barrier((own, beside(outer, chips), swap(inner, chips)) + arrived)

    def along(value, power):
        return sent(value, ringward(power), 0, 0)

    a0 = along(u, 0)
    u1, u2 = leap(*exchanged(1, u, u, u))
    a1, a2 = along(u1, 1), along(u2, 2)
    *operands, a0 = exchanged(3, u2, u2, u2, a0)
    u3, u4 = leap(*operands)
    a4 = along(u4, 4)
    *operands, a1, a2 = exchanged(5, u4, u4, u4, a1, a2)
    u5, u6, inner, outer = leap(*operands, rim4, rim4)
    a5, a6 = along(u5, 5), along(u6, 6)
    *operands, a4 = exchanged(7, u6, inner, outer, a4)
    (u7,) = leap(*operands, second=False)
    mine, theirs = call(share_kernel, (half, half), [VMEM] * 8, (VMEM,) * 2, [], 16)(a0, a1, a2, u3, a4, a5, a6, u7)
    c, inner, outer = call(sum_kernel, (half, rim2, rim2), [VMEM] * 2, (VMEM,) * 3, [], 16)(
        mine, sent(theirs, ACROSS, 0, 0)
    )
    parcel = shape(BRICKS, 2 * HALF * PLANES, LAST)
    keep, send = call(last_kernel, (parcel, parcel), [VMEM] * 6, (VMEM,) * 2, [field, field, field], 22)(
        c, beside(outer), swap(inner), g, taken, weights
    )
    back = lax.all_to_all(jnp.concatenate([keep, swap(send)], axis=1), "space", 0, 0, tiled=True)
    return call(restore_kernel, shape(1, 2, PLANES, MIDDLE, LAST), [VMEM], VMEM, [], 16)(back)


def solution(mesh):
    fine = Mesh(mesh.devices.reshape(SLABS // 2, 2, BRICKS), AXES)
    slabs = ("chip", "core")
    return jax.shard_map(
        shards,
        mesh=fine,
        in_specs=(
            P(None, "space", None, None),
            P(slabs, None, "space", None, None),
            P(None, "space", None, None),
            P("space", None, None),
            P(),
        ),
        out_specs=P(slabs, None, "space", None, None),
        check_vma=False,
    )
```

```python
import functools

import jax
import jax.numpy as jnp
from jax import lax
from jax.experimental import pallas as pl
from jax.experimental.pallas import tpu as pltpu
from jax.sharding import Mesh, PartitionSpec as P

SLABS = 16
BRICKS = 8
PLANES = 4
NX = 32
MIDDLE = 128
LAST = 128
STRIP = 16
CHIPS = SLABS // 2
RING = 4
HALF = 8
EDGE = 10
ROWS = STRIP + 2 * EDGE
HELD = ROWS + 4
PART = ROWS // 2

RATE_ALONG = 4.0
RATE_ACROSS = 0.5
ADVECTION = 1.0
DAMPING = 0.8
COARSE_FACTOR = 4.0

ORDER = [0, 2, 4, 6, 7, 5, 3, 1]
AXES = ("chip", "core", "space")
MIB = 1 << 20

VMEM = pl.BlockSpec(memory_space=pltpu.VMEM)
HBM = pl.BlockSpec(memory_space=pltpu.HBM)
PAIR = 9
FINE, COARSE = 7, 8
F32 = jnp.float32


def shape(*dims):
    return jax.ShapeDtypeStruct(dims, F32)


def call(body, outs, in_specs, out_specs, scratch, limit, us=1):
    return pl.pallas_call(
        body,
        cost_estimate=pl.CostEstimate(flops=0, bytes_accessed=us * (3 << 20), transcendentals=0),
        out_shape=outs,
        in_specs=in_specs,
        out_specs=out_specs,
        scratch_shapes=scratch,
        compiler_params=pltpu.CompilerParams(vmem_limit_bytes=limit * MIB),
    )


def position():
    chip, core, space = (lax.axis_index(a) for a in AXES)
    y, odd = space // 2, space % 2
    return core, jnp.where(odd == 0, y, BRICKS - 1 - y), chip * 2 + core


def pack_kernel(startup, guess, conduct, couple, out, padded, state, others, sems):
    core, _, slab = position()
    last = slab == SLABS - 1
    from_startup = [pltpu.make_async_copy(startup.at[i], state.at[i], sems.at[i]) for i in range(2)]
    from_guess = [pltpu.make_async_copy(guess.at[0, i], state.at[i], sems.at[i]) for i in range(2)]
    copies = [pltpu.make_async_copy(conduct.at[i], others.at[i], sems.at[2 + i]) for i in range(2)]
    copies.append(pltpu.make_async_copy(couple, others.at[2], sems.at[4]))

    @pl.when(last)
    def _():
        for copy in from_startup:
            copy.start()

    @pl.when(jnp.logical_not(last))
    def _():
        for copy in from_guess:
            copy.start()

    for copy in copies:
        copy.start()
    zero = jnp.zeros((EDGE * PLANES, LAST), F32)
    end = (EDGE + MIDDLE) * PLANES
    for i in range(5):
        padded[i, 0 : EDGE * PLANES] = zero
        padded[i, end : end + EDGE * PLANES] = zero
        (from_guess + copies)[i].wait()
        for plane in range(PLANES):
            for first in range(0, MIDDLE, 8):
                value = state[i, plane, first : first + 8] if i < 2 else others[i - 2, plane, first : first + 8]
                padded[i, pl.ds((EDGE + first) * PLANES + plane, 8, stride=PLANES), :] = value
    tall, part = (STRIP + 2 * EDGE) * PLANES, PART * PLANES
    for b in range(BRICKS):
        s = ORDER[b]
        start = (STRIP * b) * PLANES
        for i in range(2):
            out[s, i * tall : (i + 1) * tall] = padded[i, start : start + tall]
        start = pl.multiple_of(STRIP * b * PLANES + part * core, 32)
        for i in range(3):
            at = 2 * tall + i * part
            out[s, at : at + part] = padded[2 + i, pl.ds(start, part)]


def unpack_kernel(got, state, coefficients):
    low = lax.broadcasted_iota(jnp.int32, (8, LAST), 0) < PLANES

    def widen(out, i, at, rows):
        for y in range(0, rows, 2):
            for t in range(NX // 8):
                a = got[2 * t, at + PLANES * y : at + PLANES * y + 8]
                b = got[2 * t + 1, at + PLANES * y : at + PLANES * y + 8]
                out[i, y, 8 * t : 8 * t + 8] = jnp.where(low, a, pltpu.roll(b, 4, 0))
                out[i, y + 1, 8 * t : 8 * t + 8] = jnp.where(low, pltpu.roll(a, 4, 0), b)

    tall, part = (STRIP + 2 * EDGE) * PLANES, PART * PLANES
    for i in range(2):
        widen(state, i, i * tall, STRIP + 2 * EDGE)
    for i in range(3):
        widen(coefficients, i, 2 * tall + i * part, PART)


def restore_kernel(got, out):
    core, _, _ = position()
    for part in range(2):
        half = core if part == 0 else 1 - core
        for b in range(BRICKS):
            first = pl.multiple_of(STRIP * b + HALF * half, HALF)
            for i in range(2):
                for plane in range(PLANES):
                    at = (part * 2 + i) * HALF * PLANES + plane
                    out[0, i, plane, pl.ds(first, HALF), :] = got[ORDER[b], pl.ds(at, HALF, stride=PLANES), :]


def row_sweep(y, state, weights, earlier, step, source):
    centre = (state[0, y], state[1, y])
    out = []
    for i in range(2):
        v = centre[i]
        w = lambda k: weights[y, PAIR * i + k]
        along = w(0) * pltpu.roll(v, 1, 0) + w(1) * pltpu.roll(v, NX - 1, 0)
        middle = w(2) * state[i, y - 1] + w(3) * state[i, y + 1]
        across = w(4) * pltpu.roll(v, 1, 1) + w(5) * pltpu.roll(v, LAST - 1, 1)
        begin = v if earlier is None else earlier[i, y]
        if step == COARSE:
            begin = (1.0 / COARSE_FACTOR) * begin
        gain = (along + middle) + (across + (w(6) * centre[1 - i] + begin))
        if i == 1 and source is not None:
            gain = jnp.concatenate([gain[:8] + source[y], gain[8:]], axis=0)
        out.append((1.0 - DAMPING) * v + w(step) * gain)
    return out


def sweep(state, weights, earlier, into, low, high, step, source=None, unroll=4):
    def rows(k, carry):
        for u in range(unroll):
            y = low + unroll * k + u
            new = row_sweep(y, state, weights, earlier, step, source)
            into[0, y] = new[0]
            into[1, y] = new[1]
        return carry

    lax.fori_loop(0, (high - low + unroll - 1) // unroll, rows, 0)


def advances(count, e, v, weights, low, high, step, source=None):
    def one(m, carry):
        sweep(e, weights, None, v, low + 2 * m + 1, high - 2 * m - 1, step, source)
        sweep(v, weights, e, e, low + 2 * m + 2, high - 2 * m - 2, step, source)
        return carry

    lax.fori_loop(0, count, one, 0)


def relax_kernel(begin, mine, other, inlet, w, base, give, own, c, feed, e, v, e0):
    core, strip, slab = position()
    c[:, pl.ds(PART * core, PART)] = mine[...]
    c[:, pl.ds(PART - PART * core, PART)] = other[...]
    e[:, :ROWS] = begin[...]
    e0[:, :ROWS] = begin[...]

    plane = lax.broadcasted_iota(jnp.int32, (NX, LAST), 0)
    column = lax.broadcasted_iota(jnp.int32, (NX, LAST), 1)
    top = lax.broadcasted_iota(jnp.int32, (8, LAST), 0) == 0

    def weigh(r, carry):
        y = strip * STRIP - EDGE + r
        lower = jnp.where(y == 0, 0.0, 1.0).astype(F32)
        upper = jnp.where(y == MIDDLE - 1, 0.0, 1.0).astype(F32)
        exchange = c[2, r]
        warmth = inlet[pl.ds(jnp.clip(y, 0, MIDDLE - 1), 1), :]
        for i in range(2):
            here = c[i, r]
            xm = jnp.where(plane == 0, 0.0, pltpu.roll(here, 1, 0))
            xp = jnp.where(plane == NX - 1, 0.0, pltpu.roll(here, NX - 1, 0))
            zm = jnp.where(column == 0, 0.0, pltpu.roll(here, 1, 1))
            zp = jnp.where(column == LAST - 1, 0.0, pltpu.roll(here, LAST - 1, 1))
            half_along, half_across = 0.5 * RATE_ALONG, 0.5 * RATE_ACROSS
            wxm = half_along * (here + xm)
            if i == 1:
                wxm = wxm + ADVECTION
            wxp = half_along * (here + xp)
            wym = half_across * (here + c[i, r - 1])
            wyp = half_across * (here + c[i, r + 1])
            wzm = half_across * (here + zm)
            wzp = half_across * (here + zp)
            outflow = wxm + wxp + wym + wyp + wzm + wzp + exchange
            inner = (
                jnp.where(plane == 0, 0.0, wxm),
                jnp.where(plane == NX - 1, 0.0, wxp),
                wym * lower,
                wyp * upper,
                jnp.where(column == 0, 0.0, wzm),
                jnp.where(column == LAST - 1, 0.0, wzp),
                exchange,
            )
            for k in range(7):
                w[r, PAIR * i + k] = inner[k]
            w[r, PAIR * i + FINE] = DAMPING / (1.0 + outflow)
            w[r, PAIR * i + COARSE] = (DAMPING * COARSE_FACTOR) / (1.0 + COARSE_FACTOR * outflow)
            if i == 1:
                feed[r] = jnp.where(top, wxm[:8] * warmth, 0.0)
        return carry

    lax.fori_loop(1, ROWS - 1, weigh, 0)
    sweep(e0, w, None, v, EDGE - 3, EDGE + STRIP + 3, COARSE)
    sweep(v, w, e0, e0, EDGE - 2, EDGE + STRIP + 2, COARSE)
    advances(4, e, v, w, 0, ROWS, FINE, feed)
    keep = jnp.where(slab == SLABS - 1, 0.0, 1.0).astype(F32)
    rows = pl.ds(EDGE - 2, STRIP + 4)
    e[:, rows] = e[:, rows] - keep * e0[:, rows]
    sweep(e, w, None, v, EDGE - 1, EDGE + STRIP + 1, COARSE)
    sweep(v, w, e, e0, EDGE, EDGE + STRIP, COARSE)
    joined = jnp.where(slab == SLABS - 2, 0.0, 1.0).astype(F32)
    near, far = pl.ds(EDGE, HALF), pl.ds(EDGE + HALF, HALF)
    base[...] = jnp.where(core == 0, joined * e0[:, near], e[:, far])
    give[0:2] = jnp.where(core == 0, joined * e0[:, far], e[:, near])
    give[2:4] = e[:, far]
    own[...] = e[:, near]


def place(core, state, middle, inward, outward):
    many, rim = inward.shape[1], outward.shape[1]
    state[:, pl.ds(middle + HALF - (HALF + many) * core, many)] = inward[...]
    state[:, pl.ds(middle - rim + (HALF + rim) * core, rim)] = outward[...]


def leap_kernel(joined, own, near, swapped, w, *refs):
    high, (odd, *refs) = (refs[0], refs[1:]) if joined else (None, refs)
    core, _, _ = position()
    middle = EDGE + HALF * core
    rows = pl.ds(middle, HALF)
    *more, e, v = refs
    reach = HALF if more else HALF // 2
    e[:, rows] = own[...]
    place(core, e, middle, swapped, near)
    advances(2, e, v, w, middle - reach, middle + HALF + reach, COARSE)
    odd[...] = e[:, rows]
    if more:
        even, *rims = more
        advances(2, e, v, w, middle - 4, middle + HALF + 4, COARSE)
        even[...] = e[:, rows] + high[...] if joined else e[:, rows]
        if rims:
            inner, outer = rims
            inner[...] = even[:, pl.ds(4 - 4 * core, 4)]
            outer[...] = even[:, pl.ds(4 * core, 4)]


def share_kernel(*refs):
    *arrived, out, inner, outer = refs
    core, _, slab = position()
    chip = slab // 2
    late = chip // RING
    total = 0.0
    for power, ref in enumerate(arrived):
        target = lax.rem(chip + 2 * RING - power, RING) + power
        total = total + jnp.where((target // RING == late) & (target < 2 * RING), ref[...], 0.0)
    out[...] = total
    inner[...] = out[:, pl.ds(6 - 6 * core, 2)]
    outer[...] = out[:, pl.ds(6 * core, 2)]


def last_kernel(own, near, swapped, g, taken, w, keep, send, r, v, e):
    core, _, _ = position()
    middle = EDGE + HALF * core
    rows = pl.ds(middle, HALF)
    r[:, rows] = own[...]
    place(core, r, middle, swapped, near)
    sweep(r, w, None, v, middle - 1, middle + HALF + 1, COARSE)
    sweep(v, w, r, e, middle, middle + HALF, COARSE)
    e[:, rows] = e[:, rows] + jnp.where(core == 0, g[...], taken[2:4])
    low = lax.broadcasted_iota(jnp.int32, (8, LAST), 0) < PLANES
    for out, other in ((keep, 0), (send, 1)):
        pick = lambda *at: jnp.where(core == other, r[at], e[at])
        for i in range(2):
            for y in range(0, HALF, 2):
                at = (i * HALF + y) * PLANES
                for t in range(NX // 8):
                    a = pick(i, middle + y, slice(8 * t, 8 * t + 8))
                    b = pick(i, middle + y + 1, slice(8 * t, 8 * t + 8))
                    out[2 * t, at : at + 8] = jnp.where(low, a, pltpu.roll(b, 4, 0))
                    out[2 * t + 1, at : at + 8] = jnp.where(low, pltpu.roll(a, 4, 0), b)


def index(chip, core, strip):
    return (chip * 2 + core) * BRICKS + ORDER[strip]


def sent(value, chips, flip, shift):
    pairs = []
    for source, target in chips:
        for core in range(2):
            for strip in range(BRICKS):
                beside = (strip + shift * (1 if core == 0 else -1)) % BRICKS
                pairs.append((index(source, core ^ flip, strip), index(target, core, beside)))
    return lax.ppermute(value, AXES, pairs)


SAME = [(c, c) for c in range(CHIPS)]
ACROSS = [((c + RING) % CHIPS, c) for c in range(CHIPS)]


def along(value, power):
    pairs = [(c, c // RING * RING + (c + 1 + power) % RING) for c in range(CHIPS)]
    return sent(value, pairs, 0, 0)


def swap(value):
    return sent(value, SAME, 1, 0)


def beside(value):
    return sent(value, SAME, 1, 1)


def exchanged(own, inner, outer, *arrived):
    return lax.optimization_barrier((own, beside(outer), swap(inner)) + arrived)


def shards(startup, guess, conduct, couple, inlet):
    chunk = (2 * ROWS + 3 * PART) * PLANES
    half = shape(2, HALF, NX, LAST)
    arrays = [pltpu.with_memory_space_constraint(a, pltpu.HBM) for a in (startup, guess, conduct, couple)]
    packed = call(
        pack_kernel,
        shape(BRICKS, chunk, LAST),
        [HBM] * 4,
        VMEM,
        [
            pltpu.VMEM((5, (MIDDLE + 2 * EDGE) * PLANES, LAST), F32),
            pltpu.VMEM((2, PLANES, MIDDLE, LAST), F32),
            pltpu.VMEM((3, PLANES, MIDDLE, LAST), F32),
            pltpu.SemaphoreType.DMA((5,)),
        ],
        16,
    )(*arrays)
    got = lax.all_to_all(packed, "space", 0, 0, tiled=True)
    begin, mine = call(
        unpack_kernel, (shape(2, ROWS, NX, LAST), shape(3, PART, NX, LAST)), [VMEM], (VMEM, VMEM), [], 16
    )(got)
    other = swap(mine)

    field = pltpu.VMEM((2, HELD, NX, LAST), F32)
    weights, base, give, g = call(
        relax_kernel,
        (pltpu.VMEM((HELD, 2 * PAIR, NX, LAST), F32), half, shape(4, HALF, NX, LAST), half),
        [VMEM] * 4,
        (VMEM,) * 4,
        [pltpu.VMEM((3, ROWS, NX, LAST), F32), pltpu.VMEM((HELD, 8, LAST), F32), field, field, field],
        24,
    )(begin, mine, other, inlet)
    taken = swap(give)
    u = base + taken[:2]

    def leap(own, near, swapped, *rims, second=True, high=None):
        outs = (half,) * (1 + second) + rims
        operands = [own, near, swapped, weights] + ([] if high is None else [high])
        body = functools.partial(leap_kernel, high is not None)
        return call(body, outs, [VMEM] * len(operands), (VMEM,) * len(outs), [field, field], 20, 2 + 3 * second)(*operands)

    chip = lax.axis_index("chip")
    across = sent(u, ACROSS, 0, 0)
    stays = (chip < RING - 1) | (chip == CHIPS - 1)
    low, high = jnp.where(stays, u, across), jnp.where(stays, across, u)

    rim4, rim2 = shape(2, 4, NX, LAST), shape(2, 2, NX, LAST)
    a0 = along(low, 0)
    u1, u2 = leap(*exchanged(low, low, low))
    a1, a2 = along(u1, 1), along(u2, 2)
    *operands, a0 = exchanged(u2, u2, u2, a0)
    u3, u4 = leap(*operands, high=high)
    a4 = along(u4, 4)
    *operands, a1, a2 = exchanged(u4, u4, u4, a1, a2)
    u5, u6, inner, outer = leap(*operands, rim4, rim4)
    a5, a6 = along(u5, 5), along(u6, 6)
    *operands, a4 = exchanged(u6, inner, outer, a4)
    (u7,) = leap(*operands, second=False)
    c, inner, outer = call(share_kernel, (half, rim2, rim2), [VMEM] * 8, (VMEM,) * 3, [], 16)(
        a0, a1, a2, u3, a4, a5, a6, u7
    )
    parcel = shape(BRICKS, 2 * HALF * PLANES, LAST)
    keep, send = call(last_kernel, (parcel, parcel), [VMEM] * 6, (VMEM,) * 2, [field, field, field], 22)(
        c, beside(outer), swap(inner), g, taken, weights
    )
    back = lax.all_to_all(jnp.concatenate([keep, swap(send)], axis=1), "space", 0, 0, tiled=True)
    return call(restore_kernel, shape(1, 2, PLANES, MIDDLE, LAST), [VMEM], VMEM, [], 16)(back)


def solution(mesh):
    fine = Mesh(mesh.devices.reshape(SLABS // 2, 2, BRICKS), AXES)
    slabs = ("chip", "core")
    return jax.shard_map(
        shards,
        mesh=fine,
        in_specs=(
            P(None, "space", None, None),
            P(slabs, None, "space", None, None),
            P(None, "space", None, None),
            P("space", None, None),
            P(),
        ),
        out_specs=P(slabs, None, "space", None, None),
        check_vma=False,
    )
```

```python
import functools

import jax
import jax.numpy as jnp
from jax import lax
from jax.experimental import pallas as pl
from jax.experimental.pallas import tpu as pltpu
from jax.sharding import Mesh, PartitionSpec as P

SLABS = 16
BRICKS = 8
PLANES = 4
NX = 32
MIDDLE = 128
LAST = 128
STRIP = 16
CHIPS = SLABS // 2
RING = 4
HALF = 8
EDGE = 10
ROWS = STRIP + 2 * EDGE
HELD = ROWS + 4
PART = ROWS // 2

RATE_ALONG = 4.0
RATE_ACROSS = 0.5
ADVECTION = 1.0
DAMPING = 0.8
COARSE_FACTOR = 4.0

ORDER = [0, 2, 4, 6, 7, 5, 3, 1]
AXES = ("chip", "core", "space")
MIB = 1 << 20

VMEM = pl.BlockSpec(memory_space=pltpu.VMEM)
HBM = pl.BlockSpec(memory_space=pltpu.HBM)
PAIR = 9
FINE, COARSE = 7, 8
F32 = jnp.float32


def shape(*dims):
    return jax.ShapeDtypeStruct(dims, F32)


def call(body, outs, in_specs, out_specs, scratch, limit, us=1):
    return pl.pallas_call(
        body,
        cost_estimate=pl.CostEstimate(flops=0, bytes_accessed=us * (3 << 20), transcendentals=0),
        out_shape=outs,
        in_specs=in_specs,
        out_specs=out_specs,
        scratch_shapes=scratch,
        compiler_params=pltpu.CompilerParams(vmem_limit_bytes=limit * MIB),
    )


def position():
    chip, core, space = (lax.axis_index(a) for a in AXES)
    y, odd = space // 2, space % 2
    return core, jnp.where(odd == 0, y, BRICKS - 1 - y), chip * 2 + core


def pack_kernel(startup, guess, conduct, couple, out, padded, state, others, sems):
    core, _, slab = position()
    last = slab == SLABS - 1
    from_startup = [pltpu.make_async_copy(startup.at[i], state.at[i], sems.at[i]) for i in range(2)]
    from_guess = [pltpu.make_async_copy(guess.at[0, i], state.at[i], sems.at[i]) for i in range(2)]
    copies = [pltpu.make_async_copy(conduct.at[i], others.at[i], sems.at[2 + i]) for i in range(2)]
    copies.append(pltpu.make_async_copy(couple, others.at[2], sems.at[4]))

    @pl.when(last)
    def _():
        for copy in from_startup:
            copy.start()

    @pl.when(jnp.logical_not(last))
    def _():
        for copy in from_guess:
            copy.start()

    for copy in copies:
        copy.start()
    zero = jnp.zeros((EDGE * PLANES, LAST), F32)
    end = (EDGE + MIDDLE) * PLANES
    for i in range(5):
        padded[i, 0 : EDGE * PLANES] = zero
        padded[i, end : end + EDGE * PLANES] = zero
        (from_guess + copies)[i].wait()
        for plane in range(PLANES):
            for first in range(0, MIDDLE, 8):
                value = state[i, plane, first : first + 8] if i < 2 else others[i - 2, plane, first : first + 8]
                padded[i, pl.ds((EDGE + first) * PLANES + plane, 8, stride=PLANES), :] = value
    tall, part = (STRIP + 2 * EDGE) * PLANES, PART * PLANES
    for b in range(BRICKS):
        s = ORDER[b]
        start = (STRIP * b) * PLANES
        for i in range(2):
            out[s, i * tall : (i + 1) * tall] = padded[i, start : start + tall]
        start = pl.multiple_of(STRIP * b * PLANES + part * core, 32)
        for i in range(3):
            at = 2 * tall + i * part
            out[s, at : at + part] = padded[2 + i, pl.ds(start, part)]


def unpack_kernel(got, state, coefficients):
    low = lax.broadcasted_iota(jnp.int32, (8, LAST), 0) < PLANES

    def widen(out, i, at, rows):
        for y in range(0, rows, 2):
            for t in range(NX // 8):
                a = got[2 * t, at + PLANES * y : at + PLANES * y + 8]
                b = got[2 * t + 1, at + PLANES * y : at + PLANES * y + 8]
                out[i, y, 8 * t : 8 * t + 8] = jnp.where(low, a, pltpu.roll(b, 4, 0))
                out[i, y + 1, 8 * t : 8 * t + 8] = jnp.where(low, pltpu.roll(a, 4, 0), b)

    tall, part = (STRIP + 2 * EDGE) * PLANES, PART * PLANES
    for i in range(2):
        widen(state, i, i * tall, STRIP + 2 * EDGE)
    for i in range(3):
        widen(coefficients, i, 2 * tall + i * part, PART)


def restore_kernel(got, out):
    core, _, _ = position()
    for part in range(2):
        half = core if part == 0 else 1 - core
        for b in range(BRICKS):
            first = pl.multiple_of(STRIP * b + HALF * half, HALF)
            for i in range(2):
                for plane in range(PLANES):
                    at = (part * 2 + i) * HALF * PLANES + plane
                    out[0, i, plane, pl.ds(first, HALF), :] = got[ORDER[b], pl.ds(at, HALF, stride=PLANES), :]


def row_sweep(y, state, weights, earlier, step, source):
    centre = (state[0, y], state[1, y])
    out = []
    for i in range(2):
        v = centre[i]
        w = lambda k: weights[y, PAIR * i + k]
        along = w(0) * pltpu.roll(v, 1, 0) + w(1) * pltpu.roll(v, NX - 1, 0)
        middle = w(2) * state[i, y - 1] + w(3) * state[i, y + 1]
        across = w(4) * pltpu.roll(v, 1, 1) + w(5) * pltpu.roll(v, LAST - 1, 1)
        begin = v if earlier is None else earlier[i, y]
        if step == COARSE:
            begin = (1.0 / COARSE_FACTOR) * begin
        gain = (along + middle) + (across + (w(6) * centre[1 - i] + begin))
        if i == 1 and source is not None:
            gain = jnp.concatenate([gain[:8] + source[y], gain[8:]], axis=0)
        out.append((1.0 - DAMPING) * v + w(step) * gain)
    return out


def sweep(state, weights, earlier, into, low, high, step, source=None, unroll=4):
    def rows(k, carry):
        for u in range(unroll):
            y = low + unroll * k + u
            new = row_sweep(y, state, weights, earlier, step, source)
            into[0, y] = new[0]
            into[1, y] = new[1]
        return carry

    lax.fori_loop(0, (high - low + unroll - 1) // unroll, rows, 0)


def advances(count, e, v, weights, low, high, step, source=None):
    def one(m, carry):
        sweep(e, weights, None, v, low + 2 * m + 1, high - 2 * m - 1, step, source)
        sweep(v, weights, e, e, low + 2 * m + 2, high - 2 * m - 2, step, source)
        return carry

    lax.fori_loop(0, count, one, 0)


def relax_kernel(begin, mine, other, inlet, w, base, give, own, c, feed, e, v, e0):
    core, strip, slab = position()
    c[:, pl.ds(PART * core, PART)] = mine[...]
    c[:, pl.ds(PART - PART * core, PART)] = other[...]
    e[:, :ROWS] = begin[...]
    e0[:, :ROWS] = begin[...]

    plane = lax.broadcasted_iota(jnp.int32, (NX, LAST), 0)
    column = lax.broadcasted_iota(jnp.int32, (NX, LAST), 1)
    top = lax.broadcasted_iota(jnp.int32, (8, LAST), 0) == 0

    def weigh(r, carry):
        y = strip * STRIP - EDGE + r
        lower = jnp.where(y == 0, 0.0, 1.0).astype(F32)
        upper = jnp.where(y == MIDDLE - 1, 0.0, 1.0).astype(F32)
        exchange = c[2, r]
        warmth = inlet[pl.ds(jnp.clip(y, 0, MIDDLE - 1), 1), :]
        for i in range(2):
            here = c[i, r]
            xm = jnp.where(plane == 0, 0.0, pltpu.roll(here, 1, 0))
            xp = jnp.where(plane == NX - 1, 0.0, pltpu.roll(here, NX - 1, 0))
            zm = jnp.where(column == 0, 0.0, pltpu.roll(here, 1, 1))
            zp = jnp.where(column == LAST - 1, 0.0, pltpu.roll(here, LAST - 1, 1))
            half_along, half_across = 0.5 * RATE_ALONG, 0.5 * RATE_ACROSS
            wxm = half_along * (here + xm)
            if i == 1:
                wxm = wxm + ADVECTION
            wxp = half_along * (here + xp)
            wym = half_across * (here + c[i, r - 1])
            wyp = half_across * (here + c[i, r + 1])
            wzm = half_across * (here + zm)
            wzp = half_across * (here + zp)
            outflow = wxm + wxp + wym + wyp + wzm + wzp + exchange
            inner = (
                jnp.where(plane == 0, 0.0, wxm),
                jnp.where(plane == NX - 1, 0.0, wxp),
                wym * lower,
                wyp * upper,
                jnp.where(column == 0, 0.0, wzm),
                jnp.where(column == LAST - 1, 0.0, wzp),
                exchange,
            )
            for k in range(7):
                w[r, PAIR * i + k] = inner[k]
            w[r, PAIR * i + FINE] = DAMPING / (1.0 + outflow)
            w[r, PAIR * i + COARSE] = (DAMPING * COARSE_FACTOR) / (1.0 + COARSE_FACTOR * outflow)
            if i == 1:
                feed[r] = jnp.where(top, wxm[:8] * warmth, 0.0)
        return carry

    lax.fori_loop(1, ROWS - 1, weigh, 0)
    sweep(e0, w, None, v, EDGE - 3, EDGE + STRIP + 3, COARSE)
    sweep(v, w, e0, e0, EDGE - 2, EDGE + STRIP + 2, COARSE)
    advances(4, e, v, w, 0, ROWS, FINE, feed)
    keep = jnp.where(slab == SLABS - 1, 0.0, 1.0).astype(F32)
    rows = pl.ds(EDGE - 2, STRIP + 4)
    e[:, rows] = e[:, rows] - keep * e0[:, rows]
    sweep(e, w, None, v, EDGE - 1, EDGE + STRIP + 1, COARSE)
    sweep(v, w, e, e0, EDGE, EDGE + STRIP, COARSE)
    joined = jnp.where(slab == SLABS - 2, 0.0, 1.0).astype(F32)
    near, far = pl.ds(EDGE, HALF), pl.ds(EDGE + HALF, HALF)
    base[...] = jnp.where(core == 0, joined * e0[:, near], e[:, far])
    give[0:2] = jnp.where(core == 0, joined * e0[:, far], e[:, near])
    give[2:4] = e[:, far]
    own[...] = e[:, near]


def place(core, state, middle, inward, outward):
    many, rim = inward.shape[1], outward.shape[1]
    state[:, pl.ds(middle + HALF - (HALF + many) * core, many)] = inward[...]
    state[:, pl.ds(middle - rim + (HALF + rim) * core, rim)] = outward[...]


def leap_kernel(joined, own, near, swapped, w, *refs):
    high, (odd, *refs) = (refs[0], refs[1:]) if joined else (None, refs)
    core, _, _ = position()
    middle = EDGE + HALF * core
    rows = pl.ds(middle, HALF)
    *more, e, v = refs
    reach = HALF if more else HALF // 2
    e[:, rows] = own[...]
    place(core, e, middle, swapped, near)
    advances(2, e, v, w, middle - reach, middle + HALF + reach, COARSE)
    odd[...] = e[:, rows]
    if more:
        even, *rims = more
        advances(2, e, v, w, middle - 4, middle + HALF + 4, COARSE)
        even[...] = e[:, rows] + high[...] if joined else e[:, rows]
        if rims:
            inner, outer = rims
            inner[...] = even[:, pl.ds(4 - 4 * core, 4)]
            outer[...] = even[:, pl.ds(4 * core, 4)]


def choose_kernel(ours, across, low, high):
    _, _, slab = position()
    chip = slab // 2
    stays = (chip < RING - 1) | (chip == CHIPS - 1)
    low[...] = jnp.where(stays, ours[...], across[...])
    high[...] = jnp.where(stays, across[...], ours[...])


def share_kernel(*refs):
    *arrived, out, inner, outer = refs
    core, _, slab = position()
    chip = slab // 2
    late = chip // RING
    total = 0.0
    for power, ref in enumerate(arrived):
        target = lax.rem(chip + 2 * RING - power, RING) + power
        total = total + jnp.where((target // RING == late) & (target < 2 * RING), ref[...], 0.0)
    out[...] = total
    inner[...] = out[:, pl.ds(6 - 6 * core, 2)]
    outer[...] = out[:, pl.ds(6 * core, 2)]


def last_kernel(own, near, swapped, g, taken, w, keep, send, r, v, e):
    core, _, _ = position()
    middle = EDGE + HALF * core
    rows = pl.ds(middle, HALF)
    r[:, rows] = own[...]
    place(core, r, middle, swapped, near)
    sweep(r, w, None, v, middle - 1, middle + HALF + 1, COARSE)
    sweep(v, w, r, e, middle, middle + HALF, COARSE)
    e[:, rows] = e[:, rows] + jnp.where(core == 0, g[...], taken[2:4])
    low = lax.broadcasted_iota(jnp.int32, (8, LAST), 0) < PLANES
    for out, other in ((keep, 0), (send, 1)):
        pick = lambda *at: jnp.where(core == other, r[at], e[at])
        for i in range(2):
            for y in range(0, HALF, 2):
                at = (i * HALF + y) * PLANES
                for t in range(NX // 8):
                    a = pick(i, middle + y, slice(8 * t, 8 * t + 8))
                    b = pick(i, middle + y + 1, slice(8 * t, 8 * t + 8))
                    out[2 * t, at : at + 8] = jnp.where(low, a, pltpu.roll(b, 4, 0))
                    out[2 * t + 1, at : at + 8] = jnp.where(low, pltpu.roll(a, 4, 0), b)


def index(chip, core, strip):
    return (chip * 2 + core) * BRICKS + ORDER[strip]


def sent(value, chips, flip, shift):
    pairs = []
    for source, target in chips:
        for core in range(2):
            for strip in range(BRICKS):
                beside = (strip + shift * (1 if core == 0 else -1)) % BRICKS
                pairs.append((index(source, core ^ flip, strip), index(target, core, beside)))
    return lax.ppermute(value, AXES, pairs)


SAME = [(c, c) for c in range(CHIPS)]
ACROSS = [((c + RING) % CHIPS, c) for c in range(CHIPS)]


def along(value, power):
    pairs = [(c, c // RING * RING + (c + 1 + power) % RING) for c in range(CHIPS)]
    return sent(value, pairs, 0, 0)


def swap(value):
    return sent(value, SAME, 1, 0)


def beside(value):
    return sent(value, SAME, 1, 1)


def exchanged(own, inner, outer, *arrived):
    return lax.optimization_barrier((own, beside(outer), swap(inner)) + arrived)


def shards(startup, guess, conduct, couple, inlet):
    chunk = (2 * ROWS + 3 * PART) * PLANES
    half = shape(2, HALF, NX, LAST)
    arrays = [pltpu.with_memory_space_constraint(a, pltpu.HBM) for a in (startup, guess, conduct, couple)]
    packed = call(
        pack_kernel,
        shape(BRICKS, chunk, LAST),
        [HBM] * 4,
        VMEM,
        [
            pltpu.VMEM((5, (MIDDLE + 2 * EDGE) * PLANES, LAST), F32),
            pltpu.VMEM((2, PLANES, MIDDLE, LAST), F32),
            pltpu.VMEM((3, PLANES, MIDDLE, LAST), F32),
            pltpu.SemaphoreType.DMA((5,)),
        ],
        16,
    )(*arrays)
    got = lax.all_to_all(packed, "space", 0, 0, tiled=True)
    begin, mine = call(
        unpack_kernel, (shape(2, ROWS, NX, LAST), shape(3, PART, NX, LAST)), [VMEM], (VMEM, VMEM), [], 16
    )(got)
    other = swap(mine)

    field = pltpu.VMEM((2, HELD, NX, LAST), F32)
    weights, base, give, g = call(
        relax_kernel,
        (pltpu.VMEM((HELD, 2 * PAIR, NX, LAST), F32), half, shape(4, HALF, NX, LAST), half),
        [VMEM] * 4,
        (VMEM,) * 4,
        [pltpu.VMEM((3, ROWS, NX, LAST), F32), pltpu.VMEM((HELD, 8, LAST), F32), field, field, field],
        24,
    )(begin, mine, other, inlet)
    taken = swap(give)
    u = base + taken[:2]

    def leap(own, near, swapped, *rims, second=True, high=None):
        outs = (half,) * (1 + second) + rims
        operands = [own, near, swapped, weights] + ([] if high is None else [high])
        body = functools.partial(leap_kernel, high is not None)
        return call(body, outs, [VMEM] * len(operands), (VMEM,) * len(outs), [field, field], 20, 2 + 3 * second)(*operands)

    low, high = call(choose_kernel, (half, half), [VMEM] * 2, (VMEM,) * 2, [], 8)(u, sent(u, ACROSS, 0, 0))
    rim4, rim2 = shape(2, 4, NX, LAST), shape(2, 2, NX, LAST)
    a0 = along(low, 0)
    u1, u2 = leap(*exchanged(low, low, low))
    a1, a2 = along(u1, 1), along(u2, 2)
    *operands, a0 = exchanged(u2, u2, u2, a0)
    u3, u4 = leap(*operands, high=high)
    a4 = along(u4, 4)
    *operands, a1, a2 = exchanged(u4, u4, u4, a1, a2)
    u5, u6, inner, outer = leap(*operands, rim4, rim4)
    a5, a6 = along(u5, 5), along(u6, 6)
    *operands, a4 = exchanged(u6, inner, outer, a4)
    (u7,) = leap(*operands, second=False)
    c, inner, outer = call(share_kernel, (half, rim2, rim2), [VMEM] * 8, (VMEM,) * 3, [], 16)(
        a0, a1, a2, u3, a4, a5, a6, u7
    )
    parcel = shape(BRICKS, 2 * HALF * PLANES, LAST)
    keep, send = call(last_kernel, (parcel, parcel), [VMEM] * 6, (VMEM,) * 2, [field, field, field], 22)(
        c, beside(outer), swap(inner), g, taken, weights
    )
    back = lax.all_to_all(jnp.concatenate([keep, swap(send)], axis=1), "space", 0, 0, tiled=True)
    return call(restore_kernel, shape(1, 2, PLANES, MIDDLE, LAST), [VMEM], VMEM, [], 16)(back)


def solution(mesh):
    fine = Mesh(mesh.devices.reshape(SLABS // 2, 2, BRICKS), AXES)
    slabs = ("chip", "core")
    return jax.shard_map(
        shards,
        mesh=fine,
        in_specs=(
            P(None, "space", None, None),
            P(slabs, None, "space", None, None),
            P(None, "space", None, None),
            P("space", None, None),
            P(),
        ),
        out_specs=P(slabs, None, "space", None, None),
        check_vma=False,
    )
```

```python
import functools

import jax
import jax.numpy as jnp
from jax import lax
from jax.experimental import pallas as pl
from jax.experimental.pallas import tpu as pltpu
from jax.sharding import Mesh, PartitionSpec as P

SLABS = 16
BRICKS = 8
PLANES = 4
NX = 32
MIDDLE = 128
LAST = 128
STRIP = 16
CHIPS = SLABS // 2
RING = 4
HALF = 8
EDGE = 10
ROWS = STRIP + 2 * EDGE
LONGEST = 12
PART = ROWS // 2

RATE_ALONG = 4.0
RATE_ACROSS = 0.5
ADVECTION = 1.0
DAMPING = 0.8
COARSE_FACTOR = 4.0

ORDER = [0, 2, 4, 6, 7, 5, 3, 1]
AXES = ("chip", "core", "space")
MIB = 1 << 20

VMEM = pl.BlockSpec(memory_space=pltpu.VMEM)
HBM = pl.BlockSpec(memory_space=pltpu.HBM)
PAIR = 9
FINE, COARSE = 7, 8
F32 = jnp.float32


def shape(*dims):
    return jax.ShapeDtypeStruct(dims, F32)


def call(body, outs, in_specs, out_specs, scratch, limit, us=1):
    return pl.pallas_call(
        body,
        cost_estimate=pl.CostEstimate(flops=0, bytes_accessed=us * (3 << 20), transcendentals=0),
        out_shape=outs,
        in_specs=in_specs,
        out_specs=out_specs,
        scratch_shapes=scratch,
        compiler_params=pltpu.CompilerParams(vmem_limit_bytes=limit * MIB),
    )


def position():
    chip, core, space = (lax.axis_index(a) for a in AXES)
    y, odd = space // 2, space % 2
    return core, jnp.where(odd == 0, y, BRICKS - 1 - y), chip * 2 + core


def pack_kernel(startup, guess, conduct, couple, out, padded, state, others, sems):
    core, _, slab = position()
    last = slab == SLABS - 1
    from_startup = [pltpu.make_async_copy(startup.at[i], state.at[i], sems.at[i]) for i in range(2)]
    from_guess = [pltpu.make_async_copy(guess.at[0, i], state.at[i], sems.at[i]) for i in range(2)]
    copies = [pltpu.make_async_copy(conduct.at[i], others.at[i], sems.at[2 + i]) for i in range(2)]
    copies.append(pltpu.make_async_copy(couple, others.at[2], sems.at[4]))

    @pl.when(last)
    def _():
        for copy in from_startup:
            copy.start()

    @pl.when(jnp.logical_not(last))
    def _():
        for copy in from_guess:
            copy.start()

    for copy in copies:
        copy.start()
    zero = jnp.zeros((EDGE * PLANES, LAST), F32)
    end = (EDGE + MIDDLE) * PLANES
    for i in range(5):
        padded[i, 0 : EDGE * PLANES] = zero
        padded[i, end : end + EDGE * PLANES] = zero
        (from_guess + copies)[i].wait()
        for plane in range(PLANES):
            for first in range(0, MIDDLE, 8):
                value = state[i, plane, first : first + 8] if i < 2 else others[i - 2, plane, first : first + 8]
                padded[i, pl.ds((EDGE + first) * PLANES + plane, 8, stride=PLANES), :] = value
    tall, part = (STRIP + 2 * EDGE) * PLANES, PART * PLANES
    for b in range(BRICKS):
        s = ORDER[b]
        start = (STRIP * b) * PLANES
        for i in range(2):
            out[s, i * tall : (i + 1) * tall] = padded[i, start : start + tall]
        start = pl.multiple_of(STRIP * b * PLANES + part * core, 32)
        for i in range(3):
            at = 2 * tall + i * part
            out[s, at : at + part] = padded[2 + i, pl.ds(start, part)]


def unpack_kernel(got, state, coefficients):
    low = lax.broadcasted_iota(jnp.int32, (8, LAST), 0) < PLANES

    def widen(out, i, at, rows):
        for y in range(0, rows, 2):
            for t in range(NX // 8):
                a = got[2 * t, at + PLANES * y : at + PLANES * y + 8]
                b = got[2 * t + 1, at + PLANES * y : at + PLANES * y + 8]
                out[i, y, 8 * t : 8 * t + 8] = jnp.where(low, a, pltpu.roll(b, 4, 0))
                out[i, y + 1, 8 * t : 8 * t + 8] = jnp.where(low, pltpu.roll(a, 4, 0), b)

    tall, part = (STRIP + 2 * EDGE) * PLANES, PART * PLANES
    for i in range(2):
        widen(state, i, i * tall, STRIP + 2 * EDGE)
    for i in range(3):
        widen(coefficients, i, 2 * tall + i * part, PART)


def restore_kernel(got, out):
    core, _, _ = position()
    for part in range(2):
        half = core if part == 0 else 1 - core
        for b in range(BRICKS):
            first = pl.multiple_of(STRIP * b + HALF * half, HALF)
            for i in range(2):
                for plane in range(PLANES):
                    at = (part * 2 + i) * HALF * PLANES + plane
                    out[0, i, plane, pl.ds(first, HALF), :] = got[ORDER[b], pl.ds(at, HALF, stride=PLANES), :]


def sweep_rows(first, count, state, weights, earlier, into, step, source):
    centres = [[state[i, first - 1 + k] for k in range(count + 2)] for i in range(2)]
    for u in range(count):
        y = first + u
        for i in range(2):
            v = centres[i][u + 1]
            w = lambda k: weights[y, PAIR * i + k]
            along = w(0) * pltpu.roll(v, 1, 0) + w(1) * pltpu.roll(v, NX - 1, 0)
            middle = w(2) * centres[i][u] + w(3) * centres[i][u + 2]
            across = w(4) * pltpu.roll(v, 1, 1) + w(5) * pltpu.roll(v, LAST - 1, 1)
            begin = v if earlier is None else earlier[i, y]
            if step == COARSE:
                begin = (1.0 / COARSE_FACTOR) * begin
            gain = (along + middle) + (across + (w(6) * centres[1 - i][u + 1] + begin))
            if i == 1 and source is not None:
                gain = jnp.concatenate([gain[:8] + source[y], gain[8:]], axis=0)
            into[i, y] = (1.0 - DAMPING) * v + w(step) * gain


def sweep(state, weights, earlier, into, low, count, step, source=None):
    pieces = -(-count // LONGEST)
    size = -(-count // pieces)
    whole = count // size

    def piece(first, rows):
        sweep_rows(first, rows, state, weights, earlier, into, step, source)

    if whole > 1:

        def one(k, carry):
            piece(low + k * size, size)
            return carry

        lax.fori_loop(0, whole, one, 0)
    else:
        piece(low, size)
    if count > whole * size:
        piece(low + whole * size, count - whole * size)


def advances(many, e, v, weights, low, count, step, source=None):
    for m in range(many):
        sweep(e, weights, None, v, low + 2 * m + 1, count - 4 * m - 2, step, source)
        sweep(v, weights, e, e, low + 2 * m + 2, count - 4 * m - 4, step, source)


def relax_kernel(begin, mine, other, inlet, w, base, give, own, c, feed, e, v, e0):
    core, strip, slab = position()
    c[:, pl.ds(PART * core, PART)] = mine[...]
    c[:, pl.ds(PART - PART * core, PART)] = other[...]
    e[:, :ROWS] = begin[...]
    e0[:, :ROWS] = begin[...]

    plane = lax.broadcasted_iota(jnp.int32, (NX, LAST), 0)
    column = lax.broadcasted_iota(jnp.int32, (NX, LAST), 1)
    top = lax.broadcasted_iota(jnp.int32, (8, LAST), 0) == 0

    def weigh(r):
        y = strip * STRIP - EDGE + r
        lower = jnp.where(y == 0, 0.0, 1.0).astype(F32)
        upper = jnp.where(y == MIDDLE - 1, 0.0, 1.0).astype(F32)
        exchange = c[2, r]
        warmth = inlet[pl.ds(jnp.clip(y, 0, MIDDLE - 1), 1), :]
        for i in range(2):
            here = c[i, r]
            xm = jnp.where(plane == 0, 0.0, pltpu.roll(here, 1, 0))
            xp = jnp.where(plane == NX - 1, 0.0, pltpu.roll(here, NX - 1, 0))
            zm = jnp.where(column == 0, 0.0, pltpu.roll(here, 1, 1))
            zp = jnp.where(column == LAST - 1, 0.0, pltpu.roll(here, LAST - 1, 1))
            half_along, half_across = 0.5 * RATE_ALONG, 0.5 * RATE_ACROSS
            wxm = half_along * (here + xm)
            if i == 1:
                wxm = wxm + ADVECTION
            wxp = half_along * (here + xp)
            wym = half_across * (here + c[i, r - 1])
            wyp = half_across * (here + c[i, r + 1])
            wzm = half_across * (here + zm)
            wzp = half_across * (here + zp)
            outflow = wxm + wxp + wym + wyp + wzm + wzp + exchange
            inner = (
                jnp.where(plane == 0, 0.0, wxm),
                jnp.where(plane == NX - 1, 0.0, wxp),
                wym * lower,
                wyp * upper,
                jnp.where(column == 0, 0.0, wzm),
                jnp.where(column == LAST - 1, 0.0, wzp),
                exchange,
            )
            for k in range(7):
                w[r, PAIR * i + k] = inner[k]
            w[r, PAIR * i + FINE] = DAMPING / (1.0 + outflow)
            w[r, PAIR * i + COARSE] = (DAMPING * COARSE_FACTOR) / (1.0 + COARSE_FACTOR * outflow)
            if i == 1:
                feed[r] = jnp.where(top, wxm[:8] * warmth, 0.0)

    def weigh_two(k, carry):
        weigh(1 + 2 * k)
        weigh(2 + 2 * k)
        return carry

    lax.fori_loop(0, (ROWS - 2) // 2, weigh_two, 0)
    sweep(e0, w, None, v, EDGE - 3, STRIP + 6, COARSE)
    sweep(v, w, e0, e0, EDGE - 2, STRIP + 4, COARSE)
    advances(4, e, v, w, 0, ROWS, FINE, feed)
    keep = jnp.where(slab == SLABS - 1, 0.0, 1.0).astype(F32)
    rows = pl.ds(EDGE - 2, STRIP + 4)
    e[:, rows] = e[:, rows] - keep * e0[:, rows]
    sweep(e, w, None, v, EDGE - 1, STRIP + 2, COARSE)
    sweep(v, w, e, e0, EDGE, STRIP, COARSE)
    joined = jnp.where(slab == SLABS - 2, 0.0, 1.0).astype(F32)
    near, far = pl.ds(EDGE, HALF), pl.ds(EDGE + HALF, HALF)
    base[...] = jnp.where(core == 0, joined * e0[:, near], e[:, far])
    give[0:2] = jnp.where(core == 0, joined * e0[:, far], e[:, near])
    give[2:4] = e[:, far]
    own[...] = e[:, near]


def place(core, state, middle, inward, outward):
    many, rim = inward.shape[1], outward.shape[1]
    state[:, pl.ds(middle + HALF - (HALF + many) * core, many)] = inward[...]
    state[:, pl.ds(middle - rim + (HALF + rim) * core, rim)] = outward[...]


def leap_kernel(joined, own, near, swapped, w, *refs):
    high, (odd, *refs) = (refs[0], refs[1:]) if joined else (None, refs)
    core, _, _ = position()
    middle = EDGE + HALF * core
    rows = pl.ds(middle, HALF)
    *more, e, v = refs
    reach = HALF if more else HALF // 2
    e[:, rows] = own[...]
    place(core, e, middle, swapped, near)
    advances(2, e, v, w, middle - reach, HALF + 2 * reach, COARSE)
    odd[...] = e[:, rows]
    if more:
        even, *rims = more
        advances(2, e, v, w, middle - 4, HALF + 8, COARSE)
        even[...] = e[:, rows] + high[...] if joined else e[:, rows]
        if rims:
            inner, outer = rims
            inner[...] = even[:, pl.ds(4 - 4 * core, 4)]
            outer[...] = even[:, pl.ds(4 * core, 4)]


def choose_kernel(ours, across, low, high):
    _, _, slab = position()
    chip = slab // 2
    stays = (chip < RING - 1) | (chip == CHIPS - 1)
    low[...] = jnp.where(stays, ours[...], across[...])
    high[...] = jnp.where(stays, across[...], ours[...])


def share_kernel(*refs):
    *arrived, out, inner, outer = refs
    core, _, slab = position()
    chip = slab // 2
    late = chip // RING
    total = 0.0
    for power, ref in enumerate(arrived):
        target = lax.rem(chip + 2 * RING - power, RING) + power
        total = total + jnp.where((target // RING == late) & (target < 2 * RING), ref[...], 0.0)
    out[...] = total
    inner[...] = out[:, pl.ds(6 - 6 * core, 2)]
    outer[...] = out[:, pl.ds(6 * core, 2)]


def last_kernel(own, near, swapped, g, taken, w, keep, send, r, v, e):
    core, _, _ = position()
    middle = EDGE + HALF * core
    rows = pl.ds(middle, HALF)
    r[:, rows] = own[...]
    place(core, r, middle, swapped, near)
    sweep(r, w, None, v, middle - 1, HALF + 2, COARSE)
    sweep(v, w, r, e, middle, HALF, COARSE)
    e[:, rows] = e[:, rows] + jnp.where(core == 0, g[...], taken[2:4])
    low = lax.broadcasted_iota(jnp.int32, (8, LAST), 0) < PLANES
    for out, other in ((keep, 0), (send, 1)):
        pick = lambda *at: jnp.where(core == other, r[at], e[at])
        for i in range(2):
            for y in range(0, HALF, 2):
                at = (i * HALF + y) * PLANES
                for t in range(NX // 8):
                    a = pick(i, middle + y, slice(8 * t, 8 * t + 8))
                    b = pick(i, middle + y + 1, slice(8 * t, 8 * t + 8))
                    out[2 * t, at : at + 8] = jnp.where(low, a, pltpu.roll(b, 4, 0))
                    out[2 * t + 1, at : at + 8] = jnp.where(low, pltpu.roll(a, 4, 0), b)


def index(chip, core, strip):
    return (chip * 2 + core) * BRICKS + ORDER[strip]


def sent(value, chips, flip, shift):
    pairs = []
    for source, target in chips:
        for core in range(2):
            for strip in range(BRICKS):
                beside = (strip + shift * (1 if core == 0 else -1)) % BRICKS
                pairs.append((index(source, core ^ flip, strip), index(target, core, beside)))
    return lax.ppermute(value, AXES, pairs)


SAME = [(c, c) for c in range(CHIPS)]
ACROSS = [((c + RING) % CHIPS, c) for c in range(CHIPS)]


def along(value, power):
    pairs = [(c, c // RING * RING + (c + 1 + power) % RING) for c in range(CHIPS)]
    return sent(value, pairs, 0, 0)


def swap(value):
    return sent(value, SAME, 1, 0)


def beside(value):
    return sent(value, SAME, 1, 1)


def exchanged(own, inner, outer, *arrived):
    return lax.optimization_barrier((own, beside(outer), swap(inner)) + arrived)


def shards(startup, guess, conduct, couple, inlet):
    chunk = (2 * ROWS + 3 * PART) * PLANES
    half = shape(2, HALF, NX, LAST)
    arrays = [pltpu.with_memory_space_constraint(a, pltpu.HBM) for a in (startup, guess, conduct, couple)]
    packed = call(
        pack_kernel,
        shape(BRICKS, chunk, LAST),
        [HBM] * 4,
        VMEM,
        [
            pltpu.VMEM((5, (MIDDLE + 2 * EDGE) * PLANES, LAST), F32),
            pltpu.VMEM((2, PLANES, MIDDLE, LAST), F32),
            pltpu.VMEM((3, PLANES, MIDDLE, LAST), F32),
            pltpu.SemaphoreType.DMA((5,)),
        ],
        16,
    )(*arrays)
    got = lax.all_to_all(packed, "space", 0, 0, tiled=True)
    begin, mine = call(
        unpack_kernel, (shape(2, ROWS, NX, LAST), shape(3, PART, NX, LAST)), [VMEM], (VMEM, VMEM), [], 16
    )(got)
    other = swap(mine)

    field = pltpu.VMEM((2, ROWS, NX, LAST), F32)
    weights, base, give, g = call(
        relax_kernel,
        (pltpu.VMEM((ROWS, 2 * PAIR, NX, LAST), F32), half, shape(4, HALF, NX, LAST), half),
        [VMEM] * 4,
        (VMEM,) * 4,
        [pltpu.VMEM((3, ROWS, NX, LAST), F32), pltpu.VMEM((ROWS, 8, LAST), F32), field, field, field],
        24,
    )(begin, mine, other, inlet)
    taken = swap(give)
    u = base + taken[:2]

    def leap(own, near, swapped, *rims, second=True, high=None):
        outs = (half,) * (1 + second) + rims
        operands = [own, near, swapped, weights] + ([] if high is None else [high])
        body = functools.partial(leap_kernel, high is not None)
        return call(body, outs, [VMEM] * len(operands), (VMEM,) * len(outs), [field, field], 20, 2 + 3 * second)(*operands)

    low, high = call(choose_kernel, (half, half), [VMEM] * 2, (VMEM,) * 2, [], 8)(u, sent(u, ACROSS, 0, 0))
    rim4, rim2 = shape(2, 4, NX, LAST), shape(2, 2, NX, LAST)
    a0 = along(low, 0)
    u1, u2 = leap(*exchanged(low, low, low))
    a1, a2 = along(u1, 1), along(u2, 2)
    *operands, a0 = exchanged(u2, u2, u2, a0)
    u3, u4 = leap(*operands, high=high)
    a4 = along(u4, 4)
    *operands, a1, a2 = exchanged(u4, u4, u4, a1, a2)
    u5, u6, inner, outer = leap(*operands, rim4, rim4)
    a5, a6 = along(u5, 5), along(u6, 6)
    *operands, a4 = exchanged(u6, inner, outer, a4)
    (u7,) = leap(*operands, second=False)
    c, inner, outer = call(share_kernel, (half, rim2, rim2), [VMEM] * 8, (VMEM,) * 3, [], 16)(
        a0, a1, a2, u3, a4, a5, a6, u7
    )
    parcel = shape(BRICKS, 2 * HALF * PLANES, LAST)
    keep, send = call(last_kernel, (parcel, parcel), [VMEM] * 6, (VMEM,) * 2, [field, field, field], 22)(
        c, beside(outer), swap(inner), g, taken, weights
    )
    back = lax.all_to_all(jnp.concatenate([keep, swap(send)], axis=1), "space", 0, 0, tiled=True)
    return call(restore_kernel, shape(1, 2, PLANES, MIDDLE, LAST), [VMEM], VMEM, [], 16)(back)


def solution(mesh):
    fine = Mesh(mesh.devices.reshape(SLABS // 2, 2, BRICKS), AXES)
    slabs = ("chip", "core")
    return jax.shard_map(
        shards,
        mesh=fine,
        in_specs=(
            P(None, "space", None, None),
            P(slabs, None, "space", None, None),
            P(None, "space", None, None),
            P("space", None, None),
            P(),
        ),
        out_specs=P(slabs, None, "space", None, None),
        check_vma=False,
    )
```

```python
import functools

import jax
import jax.numpy as jnp
from jax import lax
from jax.experimental import pallas as pl
from jax.experimental.pallas import tpu as pltpu
from jax.sharding import Mesh, PartitionSpec as P

SLABS = 16
BRICKS = 8
PLANES = 4
NX = 32
MIDDLE = 128
LAST = 128
STRIP = 16
CHIPS = SLABS // 2
RING = 4
HALF = 8
EDGE = 10
ROWS = STRIP + 2 * EDGE
LONGEST = 12
PART = ROWS // 2

RATE_ALONG = 4.0
RATE_ACROSS = 0.5
ADVECTION = 1.0
DAMPING = 0.8
COARSE_FACTOR = 4.0

ORDER = [0, 2, 4, 6, 7, 5, 3, 1]
AXES = ("chip", "core", "space")
MIB = 1 << 20

VMEM = pl.BlockSpec(memory_space=pltpu.VMEM)
HBM = pl.BlockSpec(memory_space=pltpu.HBM)
PAIR = 9
FINE, COARSE = 7, 8
F32 = jnp.float32


def shape(*dims):
    return jax.ShapeDtypeStruct(dims, F32)


def call(body, outs, in_specs, out_specs, scratch, limit, us=1):
    return pl.pallas_call(
        body,
        cost_estimate=pl.CostEstimate(flops=0, bytes_accessed=us * (3 << 20), transcendentals=0),
        out_shape=outs,
        in_specs=in_specs,
        out_specs=out_specs,
        scratch_shapes=scratch,
        compiler_params=pltpu.CompilerParams(vmem_limit_bytes=limit * MIB),
    )


def position():
    chip, core, space = (lax.axis_index(a) for a in AXES)
    y, odd = space // 2, space % 2
    return core, placed(jnp.where(odd == 0, y, BRICKS - 1 - y), chip), chip * 2 + core


def placed(place, chip):
    return jnp.where(chip < RING, place, BRICKS - 1 - place)


def pack_kernel(startup, guess, conduct, couple, out, padded, state, others, sems):
    core, _, slab = position()
    last = slab == SLABS - 1
    from_startup = [pltpu.make_async_copy(startup.at[i], state.at[i], sems.at[i]) for i in range(2)]
    from_guess = [pltpu.make_async_copy(guess.at[0, i], state.at[i], sems.at[i]) for i in range(2)]
    copies = [pltpu.make_async_copy(conduct.at[i], others.at[i], sems.at[2 + i]) for i in range(2)]
    copies.append(pltpu.make_async_copy(couple, others.at[2], sems.at[4]))

    @pl.when(last)
    def _():
        for copy in from_startup:
            copy.start()

    @pl.when(jnp.logical_not(last))
    def _():
        for copy in from_guess:
            copy.start()

    for copy in copies:
        copy.start()
    zero = jnp.zeros((EDGE * PLANES, LAST), F32)
    end = (EDGE + MIDDLE) * PLANES
    for i in range(5):
        padded[i, 0 : EDGE * PLANES] = zero
        padded[i, end : end + EDGE * PLANES] = zero
        (from_guess + copies)[i].wait()
        for plane in range(PLANES):
            for first in range(0, MIDDLE, 8):
                value = state[i, plane, first : first + 8] if i < 2 else others[i - 2, plane, first : first + 8]
                padded[i, pl.ds((EDGE + first) * PLANES + plane, 8, stride=PLANES), :] = value
    tall, part = (STRIP + 2 * EDGE) * PLANES, PART * PLANES
    for place in range(BRICKS):
        s = ORDER[place]
        start = pl.multiple_of(STRIP * PLANES * placed(place, slab // 2), 64)
        for i in range(2):
            out[s, i * tall : (i + 1) * tall] = padded[i, pl.ds(start, tall)]
        start = pl.multiple_of(start + part * core, 8)
        for i in range(3):
            at = 2 * tall + i * part
            out[s, at : at + part] = padded[2 + i, pl.ds(start, part)]


def unpack_kernel(got, state, coefficients):
    low = lax.broadcasted_iota(jnp.int32, (8, LAST), 0) < PLANES

    def widen(out, i, at, rows):
        for y in range(0, rows, 2):
            for t in range(NX // 8):
                a = got[2 * t, at + PLANES * y : at + PLANES * y + 8]
                b = got[2 * t + 1, at + PLANES * y : at + PLANES * y + 8]
                out[i, y, 8 * t : 8 * t + 8] = jnp.where(low, a, pltpu.roll(b, 4, 0))
                out[i, y + 1, 8 * t : 8 * t + 8] = jnp.where(low, pltpu.roll(a, 4, 0), b)

    tall, part = (STRIP + 2 * EDGE) * PLANES, PART * PLANES
    for i in range(2):
        widen(state, i, i * tall, STRIP + 2 * EDGE)
    for i in range(3):
        widen(coefficients, i, 2 * tall + i * part, PART)


def restore_kernel(got, out):
    core, _, slab = position()
    for part in range(2):
        half = core if part == 0 else 1 - core
        for place in range(BRICKS):
            first = pl.multiple_of(STRIP * placed(place, slab // 2) + HALF * half, HALF)
            for i in range(2):
                for plane in range(PLANES):
                    at = (part * 2 + i) * HALF * PLANES + plane
                    out[0, i, plane, pl.ds(first, HALF), :] = got[ORDER[place], pl.ds(at, HALF, stride=PLANES), :]


def sweep_rows(first, count, state, weights, earlier, into, step, source):
    centres = [[state[i, first - 1 + k] for k in range(count + 2)] for i in range(2)]
    for u in range(count):
        y = first + u
        for i in range(2):
            v = centres[i][u + 1]
            w = lambda k: weights[y, PAIR * i + k]
            along = w(0) * pltpu.roll(v, 1, 0) + w(1) * pltpu.roll(v, NX - 1, 0)
            middle = w(2) * centres[i][u] + w(3) * centres[i][u + 2]
            across = w(4) * pltpu.roll(v, 1, 1) + w(5) * pltpu.roll(v, LAST - 1, 1)
            begin = v if earlier is None else earlier[i, y]
            if step == COARSE:
                begin = (1.0 / COARSE_FACTOR) * begin
            gain = (along + middle) + (across + (w(6) * centres[1 - i][u + 1] + begin))
            if i == 1 and source is not None:
                gain = jnp.concatenate([gain[:8] + source[y], gain[8:]], axis=0)
            into[i, y] = (1.0 - DAMPING) * v + w(step) * gain


def sweep(state, weights, earlier, into, low, count, step, source=None):
    pieces = -(-count // LONGEST)
    size = -(-count // pieces)
    whole = count // size

    def piece(first, rows):
        sweep_rows(first, rows, state, weights, earlier, into, step, source)

    if whole > 1:

        def one(k, carry):
            piece(low + k * size, size)
            return carry

        lax.fori_loop(0, whole, one, 0)
    else:
        piece(low, size)
    if count > whole * size:
        piece(low + whole * size, count - whole * size)


def advances(many, e, v, weights, low, count, step, source=None):
    for m in range(many):
        sweep(e, weights, None, v, low + 2 * m + 1, count - 4 * m - 2, step, source)
        sweep(v, weights, e, e, low + 2 * m + 2, count - 4 * m - 4, step, source)


def relax_kernel(begin, mine, other, inlet, w, base, give, own, c, feed, e, v, e0):
    core, strip, slab = position()
    c[:, pl.ds(PART * core, PART)] = mine[...]
    c[:, pl.ds(PART - PART * core, PART)] = other[...]
    e[:, :ROWS] = begin[...]
    e0[:, :ROWS] = begin[...]

    plane = lax.broadcasted_iota(jnp.int32, (NX, LAST), 0)
    column = lax.broadcasted_iota(jnp.int32, (NX, LAST), 1)
    top = lax.broadcasted_iota(jnp.int32, (8, LAST), 0) == 0

    def weigh(r):
        y = strip * STRIP - EDGE + r
        lower = jnp.where(y == 0, 0.0, 1.0).astype(F32)
        upper = jnp.where(y == MIDDLE - 1, 0.0, 1.0).astype(F32)
        exchange = c[2, r]
        warmth = inlet[pl.ds(jnp.clip(y, 0, MIDDLE - 1), 1), :]
        for i in range(2):
            here = c[i, r]
            xm = jnp.where(plane == 0, 0.0, pltpu.roll(here, 1, 0))
            xp = jnp.where(plane == NX - 1, 0.0, pltpu.roll(here, NX - 1, 0))
            zm = jnp.where(column == 0, 0.0, pltpu.roll(here, 1, 1))
            zp = jnp.where(column == LAST - 1, 0.0, pltpu.roll(here, LAST - 1, 1))
            half_along, half_across = 0.5 * RATE_ALONG, 0.5 * RATE_ACROSS
            wxm = half_along * (here + xm)
            if i == 1:
                wxm = wxm + ADVECTION
            wxp = half_along * (here + xp)
            wym = half_across * (here + c[i, r - 1])
            wyp = half_across * (here + c[i, r + 1])
            wzm = half_across * (here + zm)
            wzp = half_across * (here + zp)
            outflow = wxm + wxp + wym + wyp + wzm + wzp + exchange
            inner = (
                jnp.where(plane == 0, 0.0, wxm),
                jnp.where(plane == NX - 1, 0.0, wxp),
                wym * lower,
                wyp * upper,
                jnp.where(column == 0, 0.0, wzm),
                jnp.where(column == LAST - 1, 0.0, wzp),
                exchange,
            )
            for k in range(7):
                w[r, PAIR * i + k] = inner[k]
            w[r, PAIR * i + FINE] = DAMPING / (1.0 + outflow)
            w[r, PAIR * i + COARSE] = (DAMPING * COARSE_FACTOR) / (1.0 + COARSE_FACTOR * outflow)
            if i == 1:
                feed[r] = jnp.where(top, wxm[:8] * warmth, 0.0)

    def weigh_two(k, carry):
        weigh(1 + 2 * k)
        weigh(2 + 2 * k)
        return carry

    lax.fori_loop(0, (ROWS - 2) // 2, weigh_two, 0)
    sweep(e0, w, None, v, EDGE - 3, STRIP + 6, COARSE)
    sweep(v, w, e0, e0, EDGE - 2, STRIP + 4, COARSE)
    advances(4, e, v, w, 0, ROWS, FINE, feed)
    keep = jnp.where(slab == SLABS - 1, 0.0, 1.0).astype(F32)
    rows = pl.ds(EDGE - 2, STRIP + 4)
    e[:, rows] = e[:, rows] - keep * e0[:, rows]
    sweep(e, w, None, v, EDGE - 1, STRIP + 2, COARSE)
    sweep(v, w, e, e0, EDGE, STRIP, COARSE)
    joined = jnp.where(slab == SLABS - 2, 0.0, 1.0).astype(F32)
    near, far = pl.ds(EDGE, HALF), pl.ds(EDGE + HALF, HALF)
    base[...] = jnp.where(core == 0, joined * e0[:, near], e[:, far])
    give[0:2] = jnp.where(core == 0, joined * e0[:, far], e[:, near])
    give[2:4] = e[:, far]
    own[...] = e[:, near]


def place(core, state, middle, inward, outward):
    many, rim = inward.shape[1], outward.shape[1]
    state[:, pl.ds(middle + HALF - (HALF + many) * core, many)] = inward[...]
    state[:, pl.ds(middle - rim + (HALF + rim) * core, rim)] = outward[...]


def leap_kernel(joined, own, near, swapped, w, *refs):
    high, (odd, *refs) = (refs[0], refs[1:]) if joined else (None, refs)
    core, _, _ = position()
    middle = EDGE + HALF * core
    rows = pl.ds(middle, HALF)
    *more, e, v = refs
    reach = HALF if more else HALF // 2
    e[:, rows] = own[...]
    place(core, e, middle, swapped, near)
    advances(2, e, v, w, middle - reach, HALF + 2 * reach, COARSE)
    odd[...] = e[:, rows]
    if more:
        even, *rims = more
        advances(2, e, v, w, middle - 4, HALF + 8, COARSE)
        even[...] = e[:, rows] + high[...] if joined else e[:, rows]
        if rims:
            inner, outer = rims
            inner[...] = even[:, pl.ds(4 - 4 * core, 4)]
            outer[...] = even[:, pl.ds(4 * core, 4)]


def choose_kernel(ours, across, low, high):
    _, _, slab = position()
    chip = slab // 2
    stays = (chip < RING - 1) | (chip == CHIPS - 1)
    low[...] = jnp.where(stays, ours[...], across[...])
    high[...] = jnp.where(stays, across[...], ours[...])


def share_kernel(*refs):
    *arrived, out, inner, outer = refs
    core, _, slab = position()
    chip = slab // 2
    late = chip // RING
    total = 0.0
    for power, ref in enumerate(arrived):
        target = lax.rem(chip + 2 * RING - power, RING) + power
        total = total + jnp.where((target // RING == late) & (target < 2 * RING), ref[...], 0.0)
    out[...] = total
    inner[...] = out[:, pl.ds(6 - 6 * core, 2)]
    outer[...] = out[:, pl.ds(6 * core, 2)]


def last_kernel(own, near, swapped, g, taken, w, keep, send, r, v, e):
    core, _, _ = position()
    middle = EDGE + HALF * core
    rows = pl.ds(middle, HALF)
    r[:, rows] = own[...]
    place(core, r, middle, swapped, near)
    sweep(r, w, None, v, middle - 1, HALF + 2, COARSE)
    sweep(v, w, r, e, middle, HALF, COARSE)
    e[:, rows] = e[:, rows] + jnp.where(core == 0, g[...], taken[2:4])
    low = lax.broadcasted_iota(jnp.int32, (8, LAST), 0) < PLANES
    for out, other in ((keep, 0), (send, 1)):
        pick = lambda *at: jnp.where(core == other, r[at], e[at])
        for i in range(2):
            for y in range(0, HALF, 2):
                at = (i * HALF + y) * PLANES
                for t in range(NX // 8):
                    a = pick(i, middle + y, slice(8 * t, 8 * t + 8))
                    b = pick(i, middle + y + 1, slice(8 * t, 8 * t + 8))
                    out[2 * t, at : at + 8] = jnp.where(low, a, pltpu.roll(b, 4, 0))
                    out[2 * t + 1, at : at + 8] = jnp.where(low, pltpu.roll(a, 4, 0), b)


def index(chip, core, strip):
    return (chip * 2 + core) * BRICKS + ORDER[strip if chip < RING else BRICKS - 1 - strip]


def sent(value, chips, flip, shift):
    pairs = []
    for source, target in chips:
        for core in range(2):
            for strip in range(BRICKS):
                beside = (strip + shift * (1 if core == 0 else -1)) % BRICKS
                pairs.append((index(source, core ^ flip, strip), index(target, core, beside)))
    return lax.ppermute(value, AXES, pairs)


SAME = [(c, c) for c in range(CHIPS)]
ACROSS = [((c + RING) % CHIPS, c) for c in range(CHIPS)]


def along(value, power):
    pairs = [(c, c // RING * RING + (c + 1 + power) % RING) for c in range(CHIPS)]
    return sent(value, pairs, 0, 0)


def swap(value):
    return sent(value, SAME, 1, 0)


def beside(value):
    return sent(value, SAME, 1, 1)


def exchanged(own, inner, outer, *arrived):
    return lax.optimization_barrier((own, beside(outer), swap(inner)) + arrived)


def shards(startup, guess, conduct, couple, inlet):
    chunk = (2 * ROWS + 3 * PART) * PLANES
    half = shape(2, HALF, NX, LAST)
    arrays = [pltpu.with_memory_space_constraint(a, pltpu.HBM) for a in (startup, guess, conduct, couple)]
    packed = call(
        pack_kernel,
        shape(BRICKS, chunk, LAST),
        [HBM] * 4,
        VMEM,
        [
            pltpu.VMEM((5, (MIDDLE + 2 * EDGE) * PLANES, LAST), F32),
            pltpu.VMEM((2, PLANES, MIDDLE, LAST), F32),
            pltpu.VMEM((3, PLANES, MIDDLE, LAST), F32),
            pltpu.SemaphoreType.DMA((5,)),
        ],
        16,
    )(*arrays)
    got = lax.all_to_all(packed, "space", 0, 0, tiled=True)
    begin, mine = call(
        unpack_kernel, (shape(2, ROWS, NX, LAST), shape(3, PART, NX, LAST)), [VMEM], (VMEM, VMEM), [], 16
    )(got)
    other = swap(mine)

    field = pltpu.VMEM((2, ROWS, NX, LAST), F32)
    weights, base, give, g = call(
        relax_kernel,
        (pltpu.VMEM((ROWS, 2 * PAIR, NX, LAST), F32), half, shape(4, HALF, NX, LAST), half),
        [VMEM] * 4,
        (VMEM,) * 4,
        [pltpu.VMEM((3, ROWS, NX, LAST), F32), pltpu.VMEM((ROWS, 8, LAST), F32), field, field, field],
        24,
    )(begin, mine, other, inlet)
    taken = swap(give)
    u = base + taken[:2]

    def leap(own, near, swapped, *rims, second=True, high=None):
        outs = (half,) * (1 + second) + rims
        operands = [own, near, swapped, weights] + ([] if high is None else [high])
        body = functools.partial(leap_kernel, high is not None)
        return call(body, outs, [VMEM] * len(operands), (VMEM,) * len(outs), [field, field], 20, 2 + 3 * second)(*operands)

    low, high = call(choose_kernel, (half, half), [VMEM] * 2, (VMEM,) * 2, [], 8)(u, sent(u, ACROSS, 0, 0))
    rim4, rim2 = shape(2, 4, NX, LAST), shape(2, 2, NX, LAST)
    a0 = along(low, 0)
    u1, u2 = leap(*exchanged(low, low, low))
    a1, a2 = along(u1, 1), along(u2, 2)
    *operands, a0 = exchanged(u2, u2, u2, a0)
    u3, u4 = leap(*operands, high=high)
    a4 = along(u4, 4)
    *operands, a1, a2 = exchanged(u4, u4, u4, a1, a2)
    u5, u6, inner, outer = leap(*operands, rim4, rim4)
    a5, a6 = along(u5, 5), along(u6, 6)
    *operands, a4 = exchanged(u6, inner, outer, a4)
    (u7,) = leap(*operands, second=False)
    c, inner, outer = call(share_kernel, (half, rim2, rim2), [VMEM] * 8, (VMEM,) * 3, [], 16)(
        a0, a1, a2, u3, a4, a5, a6, u7
    )
    parcel = shape(BRICKS, 2 * HALF * PLANES, LAST)
    keep, send = call(last_kernel, (parcel, parcel), [VMEM] * 6, (VMEM,) * 2, [field, field, field], 22)(
        c, beside(outer), swap(inner), g, taken, weights
    )
    back = lax.all_to_all(jnp.concatenate([keep, swap(send)], axis=1), "space", 0, 0, tiled=True)
    return call(restore_kernel, shape(1, 2, PLANES, MIDDLE, LAST), [VMEM], VMEM, [], 16)(back)


def solution(mesh):
    fine = Mesh(mesh.devices.reshape(SLABS // 2, 2, BRICKS), AXES)
    slabs = ("chip", "core")
    return jax.shard_map(
        shards,
        mesh=fine,
        in_specs=(
            P(None, "space", None, None),
            P(slabs, None, "space", None, None),
            P(None, "space", None, None),
            P("space", None, None),
            P(),
        ),
        out_specs=P(slabs, None, "space", None, None),
        check_vma=False,
    )
```

```python
import functools

import jax
import jax.numpy as jnp
from jax import lax
from jax.experimental import pallas as pl
from jax.experimental.pallas import tpu as pltpu
from jax.sharding import Mesh, PartitionSpec as P

SLABS = 16
BRICKS = 8
PLANES = 4
NX = 32
MIDDLE = 128
LAST = 128
STRIP = 16
CHIPS = SLABS // 2
RING = 4
HALF = 8
EDGE = 10
ROWS = STRIP + 2 * EDGE
LONGEST = 22
PART = ROWS // 2

RATE_ALONG = 4.0
RATE_ACROSS = 0.5
ADVECTION = 1.0
DAMPING = 0.8
COARSE_FACTOR = 4.0

ORDER = [0, 2, 4, 6, 7, 5, 3, 1]
AXES = ("chip", "core", "space")
MIB = 1 << 20

VMEM = pl.BlockSpec(memory_space=pltpu.VMEM)
HBM = pl.BlockSpec(memory_space=pltpu.HBM)
PAIR = 9
FINE, COARSE = 7, 8
F32 = jnp.float32


def shape(*dims):
    return jax.ShapeDtypeStruct(dims, F32)


def call(body, outs, in_specs, out_specs, scratch, limit, us=1, aliases={}):
    return pl.pallas_call(
        body,
        input_output_aliases=aliases,
        cost_estimate=pl.CostEstimate(flops=0, bytes_accessed=us * (3 << 20), transcendentals=0),
        out_shape=outs,
        in_specs=in_specs,
        out_specs=out_specs,
        scratch_shapes=scratch,
        compiler_params=pltpu.CompilerParams(vmem_limit_bytes=limit * MIB),
    )


def position():
    chip, core, space = (lax.axis_index(a) for a in AXES)
    y, odd = space // 2, space % 2
    return core, placed(jnp.where(odd == 0, y, BRICKS - 1 - y), chip), chip * 2 + core


def placed(place, chip):
    return jnp.where(chip < RING, place, BRICKS - 1 - place)


def pack_kernel(startup, guess, conduct, couple, out, padded, state, others, sems):
    core, _, slab = position()
    last = slab == SLABS - 1
    from_startup = [pltpu.make_async_copy(startup.at[i], state.at[i], sems.at[i]) for i in range(2)]
    from_guess = [pltpu.make_async_copy(guess.at[0, i], state.at[i], sems.at[i]) for i in range(2)]
    copies = [pltpu.make_async_copy(conduct.at[i], others.at[i], sems.at[2 + i]) for i in range(2)]
    copies.append(pltpu.make_async_copy(couple, others.at[2], sems.at[4]))

    @pl.when(last)
    def _():
        for copy in from_startup:
            copy.start()

    @pl.when(jnp.logical_not(last))
    def _():
        for copy in from_guess:
            copy.start()

    for copy in copies:
        copy.start()
    zero = jnp.zeros((EDGE * PLANES, LAST), F32)
    end = (EDGE + MIDDLE) * PLANES
    for i in range(5):
        padded[i, 0 : EDGE * PLANES] = zero
        padded[i, end : end + EDGE * PLANES] = zero
        (from_guess + copies)[i].wait()
        for plane in range(PLANES):
            for first in range(0, MIDDLE, 8):
                value = state[i, plane, first : first + 8] if i < 2 else others[i - 2, plane, first : first + 8]
                padded[i, pl.ds((EDGE + first) * PLANES + plane, 8, stride=PLANES), :] = value
    tall, part = (STRIP + 2 * EDGE) * PLANES, PART * PLANES
    for place in range(BRICKS):
        s = ORDER[place]
        start = pl.multiple_of(STRIP * PLANES * placed(place, slab // 2), 64)
        for i in range(2):
            out[s, i * tall : (i + 1) * tall] = padded[i, pl.ds(start, tall)]
        start = pl.multiple_of(start + part * core, 8)
        for i in range(3):
            at = 2 * tall + i * part
            out[s, at : at + part] = padded[2 + i, pl.ds(start, part)]


def unpack_kernel(got, state, coefficients):
    low = lax.broadcasted_iota(jnp.int32, (8, LAST), 0) < PLANES

    def widen(out, i, at, rows):
        for y in range(0, rows, 2):
            for t in range(NX // 8):
                a = got[2 * t, at + PLANES * y : at + PLANES * y + 8]
                b = got[2 * t + 1, at + PLANES * y : at + PLANES * y + 8]
                out[i, y, 8 * t : 8 * t + 8] = jnp.where(low, a, pltpu.roll(b, 4, 0))
                out[i, y + 1, 8 * t : 8 * t + 8] = jnp.where(low, pltpu.roll(a, 4, 0), b)

    tall, part = (STRIP + 2 * EDGE) * PLANES, PART * PLANES
    for i in range(2):
        widen(state, i, i * tall, STRIP + 2 * EDGE)
    for i in range(3):
        widen(coefficients, i, 2 * tall + i * part, PART)


def restore_kernel(got, out):
    core, _, slab = position()
    for part in range(2):
        half = core if part == 0 else 1 - core
        for place in range(BRICKS):
            first = pl.multiple_of(STRIP * placed(place, slab // 2) + HALF * half, HALF)
            for i in range(2):
                for plane in range(PLANES):
                    at = (part * 2 + i) * HALF * PLANES + plane
                    out[0, i, plane, pl.ds(first, HALF), :] = got[ORDER[place], pl.ds(at, HALF, stride=PLANES), :]


def sweep_rows(first, count, state, weights, earlier, into, step, source):
    centres = [[state[i, first - 1 + k] for k in range(count + 2)] for i in range(2)]
    for u in range(count):
        y = first + u
        for i in range(2):
            v = centres[i][u + 1]
            w = lambda k: weights[y, PAIR * i + k]
            along = w(0) * pltpu.roll(v, 1, 0) + w(1) * pltpu.roll(v, NX - 1, 0)
            middle = w(2) * centres[i][u] + w(3) * centres[i][u + 2]
            across = w(4) * pltpu.roll(v, 1, 1) + w(5) * pltpu.roll(v, LAST - 1, 1)
            begin = v if earlier is None else earlier[i, y]
            if step == COARSE:
                begin = (1.0 / COARSE_FACTOR) * begin
            gain = (along + middle) + (across + (w(6) * centres[1 - i][u + 1] + begin))
            if i == 1 and source is not None:
                gain = jnp.concatenate([gain[:8] + source[y], gain[8:]], axis=0)
            into[i, y] = (1.0 - DAMPING) * v + w(step) * gain


def sweep(state, weights, earlier, into, low, count, step, source=None):
    pieces = -(-count // LONGEST)
    size = -(-count // pieces)
    whole = count // size

    def piece(first, rows):
        sweep_rows(first, rows, state, weights, earlier, into, step, source)

    if whole > 1:

        def one(k, carry):
            piece(low + k * size, size)
            return carry

        lax.fori_loop(0, whole, one, 0)
    else:
        piece(low, size)
    if count > whole * size:
        piece(low + whole * size, count - whole * size)


def advances(many, e, v, weights, low, count, step, source=None):
    for m in range(many):
        sweep(e, weights, None, v, low + 2 * m + 1, count - 4 * m - 2, step, source)
        sweep(v, weights, e, e, low + 2 * m + 2, count - 4 * m - 4, step, source)


def weigh(first, count, c, offset, inlet, w, feed):
    _, strip, _ = position()
    plane = lax.broadcasted_iota(jnp.int32, (NX, LAST), 0)
    column = lax.broadcasted_iota(jnp.int32, (NX, LAST), 1)
    top = lax.broadcasted_iota(jnp.int32, (8, LAST), 0) == 0

    def row(r):
        at = r - offset
        y = strip * STRIP - EDGE + r
        lower = jnp.where(y == 0, 0.0, 1.0).astype(F32)
        upper = jnp.where(y == MIDDLE - 1, 0.0, 1.0).astype(F32)
        exchange = c[2, at]
        warmth = inlet[pl.ds(jnp.clip(y, 0, MIDDLE - 1), 1), :]
        for i in range(2):
            here = c[i, at]
            xm = jnp.where(plane == 0, 0.0, pltpu.roll(here, 1, 0))
            xp = jnp.where(plane == NX - 1, 0.0, pltpu.roll(here, NX - 1, 0))
            zm = jnp.where(column == 0, 0.0, pltpu.roll(here, 1, 1))
            zp = jnp.where(column == LAST - 1, 0.0, pltpu.roll(here, LAST - 1, 1))
            half_along, half_across = 0.5 * RATE_ALONG, 0.5 * RATE_ACROSS
            wxm = half_along * (here + xm)
            if i == 1:
                wxm = wxm + ADVECTION
            wxp = half_along * (here + xp)
            wym = half_across * (here + c[i, at - 1])
            wyp = half_across * (here + c[i, at + 1])
            wzm = half_across * (here + zm)
            wzp = half_across * (here + zp)
            outflow = wxm + wxp + wym + wyp + wzm + wzp + exchange
            inner = (
                jnp.where(plane == 0, 0.0, wxm),
                jnp.where(plane == NX - 1, 0.0, wxp),
                wym * lower,
                wyp * upper,
                jnp.where(column == 0, 0.0, wzm),
                jnp.where(column == LAST - 1, 0.0, wzp),
                exchange,
            )
            for k in range(7):
                w[r, PAIR * i + k] = inner[k]
            w[r, PAIR * i + FINE] = DAMPING / (1.0 + outflow)
            w[r, PAIR * i + COARSE] = (DAMPING * COARSE_FACTOR) / (1.0 + COARSE_FACTOR * outflow)
            if i == 1:
                feed[r] = jnp.where(top, wxm[:8] * warmth, 0.0)

    def two(k, carry):
        row(first + 2 * k)
        row(first + 2 * k + 1)
        return carry

    lax.fori_loop(0, count // 2, two, 0)


def weigh_kernel(mine, inlet, w, feed):
    core, _, _ = position()
    weigh(PART * core + 1, PART - 2, mine, PART * core, inlet, w, feed)


def relax_kernel(begin, mine, other, inlet, w_mine, feed_mine, w, base, give, own, beyond, c, feed, e, v, e0):
    core, _, slab = position()
    c[:, pl.ds(PART * core, PART)] = mine[...]
    c[:, pl.ds(PART - PART * core, PART)] = other[...]
    e[...] = begin[...]
    e0[...] = begin[...]
    ready = pl.ds(PART * core + 1, PART - 2)
    feed[ready] = feed_mine[ready]
    weigh(PART - 1 - (PART - 2) * core, PART, c, 0, inlet, w, feed)

    sweep(e0, w, None, v, EDGE - 3, STRIP + 6, COARSE)
    sweep(v, w, e0, e0, EDGE - 2, STRIP + 4, COARSE)
    advances(4, e, v, w, 0, ROWS, FINE, feed)
    keep = jnp.where(slab == SLABS - 1, 0.0, 1.0).astype(F32)
    rows = pl.ds(EDGE - 2, STRIP + 4)
    e[:, rows] = e[:, rows] - keep * e0[:, rows]
    sweep(e, w, None, v, EDGE - 1, STRIP + 2, COARSE)
    sweep(v, w, e, e0, EDGE, STRIP, COARSE)
    joined = jnp.where(slab == SLABS - 2, 0.0, 1.0).astype(F32)
    near, far = pl.ds(EDGE, HALF), pl.ds(EDGE + HALF, HALF)
    base[...] = jnp.where(core == 0, joined * e0[:, near], e[:, far])
    give[...] = jnp.where(core == 0, joined * e0[:, far], e[:, near])
    own[...] = e[:, near]
    beyond[...] = e[:, far]


def place(core, state, middle, inward, outward):
    many, rim = inward.shape[1], outward.shape[1]
    state[:, pl.ds(middle + HALF - (HALF + many) * core, many)] = inward[...]
    state[:, pl.ds(middle - rim + (HALF + rim) * core, rim)] = outward[...]


def leap_kernel(joined, own, near, swapped, w, *refs):
    high, (odd, *refs) = (refs[0], refs[1:]) if joined else (None, refs)
    core, _, _ = position()
    middle = EDGE + HALF * core
    rows = pl.ds(middle, HALF)
    *more, e, v = refs
    reach = HALF if more else HALF // 2
    e[:, rows] = own[...]
    place(core, e, middle, swapped, near)
    advances(2, e, v, w, middle - reach, HALF + 2 * reach, COARSE)
    odd[...] = e[:, rows]
    if more:
        even, *rims = more
        advances(2, e, v, w, middle - 4, HALF + 8, COARSE)
        even[...] = e[:, rows] + high[...] if joined else e[:, rows]
        if rims:
            inner, outer = rims
            inner[...] = even[:, pl.ds(4 - 4 * core, 4)]
            outer[...] = even[:, pl.ds(4 * core, 4)]


def choose_kernel(ours, across, low, high):
    _, _, slab = position()
    chip = slab // 2
    stays = (chip < RING - 1) | (chip == CHIPS - 1)
    low[...] = jnp.where(stays, ours[...], across[...])
    high[...] = jnp.where(stays, across[...], ours[...])


def share_kernel(*refs):
    *arrived, out, inner, outer = refs
    core, _, slab = position()
    chip = slab // 2
    late = chip // RING
    total = 0.0
    for power, ref in enumerate(arrived):
        target = lax.rem(chip + 2 * RING - power, RING) + power
        total = total + jnp.where((target // RING == late) & (target < 2 * RING), ref[...], 0.0)
    out[...] = total
    inner[...] = out[:, pl.ds(6 - 6 * core, 2)]
    outer[...] = out[:, pl.ds(6 * core, 2)]


def last_kernel(own, near, swapped, g, taken, w, keep, send, r, v, e):
    core, _, _ = position()
    middle = EDGE + HALF * core
    rows = pl.ds(middle, HALF)
    r[:, rows] = own[...]
    place(core, r, middle, swapped, near)
    sweep(r, w, None, v, middle - 1, HALF + 2, COARSE)
    sweep(v, w, r, e, middle, HALF, COARSE)
    e[:, rows] = e[:, rows] + jnp.where(core == 0, g[...], taken[...])
    low = lax.broadcasted_iota(jnp.int32, (8, LAST), 0) < PLANES
    for out, other in ((keep, 0), (send, 1)):
        pick = lambda *at: jnp.where(core == other, r[at], e[at])
        for i in range(2):
            for y in range(0, HALF, 2):
                at = (i * HALF + y) * PLANES
                for t in range(NX // 8):
                    a = pick(i, middle + y, slice(8 * t, 8 * t + 8))
                    b = pick(i, middle + y + 1, slice(8 * t, 8 * t + 8))
                    out[2 * t, at : at + 8] = jnp.where(low, a, pltpu.roll(b, 4, 0))
                    out[2 * t + 1, at : at + 8] = jnp.where(low, pltpu.roll(a, 4, 0), b)


def index(chip, core, strip):
    return (chip * 2 + core) * BRICKS + ORDER[strip if chip < RING else BRICKS - 1 - strip]


def sent(value, chips, flip, shift):
    pairs = []
    for source, target in chips:
        for core in range(2):
            for strip in range(BRICKS):
                beside = (strip + shift * (1 if core == 0 else -1)) % BRICKS
                pairs.append((index(source, core ^ flip, strip), index(target, core, beside)))
    return lax.ppermute(value, AXES, pairs)


SAME = [(c, c) for c in range(CHIPS)]
ACROSS = [((c + RING) % CHIPS, c) for c in range(CHIPS)]


def along(value, power):
    pairs = [(c, c // RING * RING + (c + 1 + power) % RING) for c in range(CHIPS)]
    return sent(value, pairs, 0, 0)


def swap(value):
    return sent(value, SAME, 1, 0)


def beside(value):
    return sent(value, SAME, 1, 1)


def exchanged(own, inner, outer, *arrived):
    return lax.optimization_barrier((own, beside(outer), swap(inner)) + arrived)


def shards(startup, guess, conduct, couple, inlet):
    chunk = (2 * ROWS + 3 * PART) * PLANES
    half = shape(2, HALF, NX, LAST)
    arrays = [pltpu.with_memory_space_constraint(a, pltpu.HBM) for a in (startup, guess, conduct, couple)]
    packed = call(
        pack_kernel,
        shape(BRICKS, chunk, LAST),
        [HBM] * 4,
        VMEM,
        [
            pltpu.VMEM((5, (MIDDLE + 2 * EDGE) * PLANES, LAST), F32),
            pltpu.VMEM((2, PLANES, MIDDLE, LAST), F32),
            pltpu.VMEM((3, PLANES, MIDDLE, LAST), F32),
            pltpu.SemaphoreType.DMA((5,)),
        ],
        16,
    )(*arrays)
    got = lax.all_to_all(packed, "space", 0, 0, tiled=True)
    begin, mine = call(
        unpack_kernel, (shape(2, ROWS, NX, LAST), shape(3, PART, NX, LAST)), [VMEM], (VMEM, VMEM), [], 16
    )(got)
    other = swap(mine)

    field = pltpu.VMEM((2, ROWS, NX, LAST), F32)
    all_weights = pltpu.VMEM((ROWS, 2 * PAIR, NX, LAST), F32)
    weights, feed = call(
        weigh_kernel, (all_weights, shape(ROWS, 8, LAST)), [VMEM] * 2, (VMEM,) * 2, [], 16, 3
    )(mine, inlet)
    weights, base, give, g, beyond = call(
        relax_kernel,
        (all_weights, half, half, half, half),
        [VMEM] * 6,
        (VMEM,) * 5,
        [pltpu.VMEM((3, ROWS, NX, LAST), F32), pltpu.VMEM((ROWS, 8, LAST), F32), field, field, field],
        24,
        aliases={4: 0},
    )(begin, mine, other, inlet, weights, feed)
    u = base + swap(give)

    def leap(own, near, swapped, *rims, second=True, high=None):
        outs = (half,) * (1 + second) + rims
        operands = [own, near, swapped, weights] + ([] if high is None else [high])
        body = functools.partial(leap_kernel, high is not None)
        return call(body, outs, [VMEM] * len(operands), (VMEM,) * len(outs), [field, field], 20, 2 + 3 * second)(*operands)

    low, high = call(choose_kernel, (half, half), [VMEM] * 2, (VMEM,) * 2, [], 8)(u, sent(u, ACROSS, 0, 0))
    rim4, rim2 = shape(2, 4, NX, LAST), shape(2, 2, NX, LAST)
    a0 = along(low, 0)
    u1, u2 = leap(*exchanged(low, low, low))
    a1, a2, taken = along(u1, 1), along(u2, 2), swap(beyond)
    *operands, a0, taken = exchanged(u2, u2, u2, a0, taken)
    u3, u4 = leap(*operands, high=high)
    a4 = along(u4, 4)
    *operands, a1, a2 = exchanged(u4, u4, u4, a1, a2)
    u5, u6, inner, outer = leap(*operands, rim4, rim4)
    a5, a6 = along(u5, 5), along(u6, 6)
    *operands, a4 = exchanged(u6, inner, outer, a4)
    (u7,) = leap(*operands, second=False)
    c, inner, outer = call(share_kernel, (half, rim2, rim2), [VMEM] * 8, (VMEM,) * 3, [], 16)(
        a0, a1, a2, u3, a4, a5, a6, u7
    )
    parcel = shape(BRICKS, 2 * HALF * PLANES, LAST)
    keep, send = call(last_kernel, (parcel, parcel), [VMEM] * 6, (VMEM,) * 2, [field, field, field], 22)(
        c, beside(outer), swap(inner), g, taken, weights
    )
    back = lax.all_to_all(jnp.concatenate([keep, swap(send)], axis=1), "space", 0, 0, tiled=True)
    return call(restore_kernel, shape(1, 2, PLANES, MIDDLE, LAST), [VMEM], VMEM, [], 16)(back)


def solution(mesh):
    fine = Mesh(mesh.devices.reshape(SLABS // 2, 2, BRICKS), AXES)
    slabs = ("chip", "core")
    return jax.shard_map(
        shards,
        mesh=fine,
        in_specs=(
            P(None, "space", None, None),
            P(slabs, None, "space", None, None),
            P(None, "space", None, None),
            P("space", None, None),
            P(),
        ),
        out_specs=P(slabs, None, "space", None, None),
        check_vma=False,
    )
```

```python
import functools

import jax
import jax.numpy as jnp
from jax import lax
from jax.experimental import pallas as pl
from jax.experimental.pallas import tpu as pltpu
from jax.sharding import Mesh, PartitionSpec as P

SLABS = 16
BRICKS = 8
PLANES = 4
NX = 32
MIDDLE = 128
LAST = 128
STRIP = 16
CHIPS = SLABS // 2
RING = 4
HALF = 8
EDGE = 10
ROWS = STRIP + 2 * EDGE
LONGEST = 22
PART = ROWS // 2

RATE_ALONG = 4.0
RATE_ACROSS = 0.5
ADVECTION = 1.0
DAMPING = 0.8
COARSE_FACTOR = 4.0

ORDER = [0, 2, 4, 6, 7, 5, 3, 1]
AXES = ("chip", "core", "space")
MIB = 1 << 20

VMEM = pl.BlockSpec(memory_space=pltpu.VMEM)
HBM = pl.BlockSpec(memory_space=pltpu.HBM)
PAIR = 9
FINE, COARSE = 7, 8
F32 = jnp.float32


def shape(*dims):
    return jax.ShapeDtypeStruct(dims, F32)


def call(body, outs, in_specs, out_specs, scratch, limit, us=1, aliases={}):
    return pl.pallas_call(
        body,
        input_output_aliases=aliases,
        cost_estimate=pl.CostEstimate(flops=0, bytes_accessed=us * (3 << 20), transcendentals=0),
        out_shape=outs,
        in_specs=in_specs,
        out_specs=out_specs,
        scratch_shapes=scratch,
        compiler_params=pltpu.CompilerParams(vmem_limit_bytes=limit * MIB),
    )


def position():
    chip, core, space = (lax.axis_index(a) for a in AXES)
    y, odd = space // 2, space % 2
    return core, placed(jnp.where(odd == 0, y, BRICKS - 1 - y), chip), chip * 2 + core


def placed(place, chip):
    return jnp.where(chip < RING, place, BRICKS - 1 - place)


def pack_kernel(startup, guess, conduct, couple, out, padded, state, others, sems):
    core, _, slab = position()
    last = slab == SLABS - 1
    from_startup = [pltpu.make_async_copy(startup.at[i], state.at[i], sems.at[i]) for i in range(2)]
    from_guess = [pltpu.make_async_copy(guess.at[0, i], state.at[i], sems.at[i]) for i in range(2)]
    copies = [pltpu.make_async_copy(conduct.at[i], others.at[i], sems.at[2 + i]) for i in range(2)]
    copies.append(pltpu.make_async_copy(couple, others.at[2], sems.at[4]))

    @pl.when(last)
    def _():
        for copy in from_startup:
            copy.start()

    @pl.when(jnp.logical_not(last))
    def _():
        for copy in from_guess:
            copy.start()

    for copy in copies:
        copy.start()
    zero = jnp.zeros((EDGE * PLANES, LAST), F32)
    end = (EDGE + MIDDLE) * PLANES
    for i in range(5):
        padded[i, 0 : EDGE * PLANES] = zero
        padded[i, end : end + EDGE * PLANES] = zero
        (from_guess + copies)[i].wait()
        for plane in range(PLANES):
            for first in range(0, MIDDLE, 8):
                value = state[i, plane, first : first + 8] if i < 2 else others[i - 2, plane, first : first + 8]
                padded[i, pl.ds((EDGE + first) * PLANES + plane, 8, stride=PLANES), :] = value
    tall, part = (STRIP + 2 * EDGE) * PLANES, PART * PLANES
    for place in range(BRICKS):
        s = ORDER[place]
        start = pl.multiple_of(STRIP * PLANES * placed(place, slab // 2), 64)
        for i in range(2):
            out[s, i * tall : (i + 1) * tall] = padded[i, pl.ds(start, tall)]
        start = pl.multiple_of(start + part * core, 8)
        for i in range(3):
            at = 2 * tall + i * part
            out[s, at : at + part] = padded[2 + i, pl.ds(start, part)]


def unpack_kernel(got, state, coefficients):
    low = lax.broadcasted_iota(jnp.int32, (8, LAST), 0) < PLANES

    def widen(out, i, at, rows):
        for y in range(0, rows, 2):
            for t in range(NX // 8):
                a = got[2 * t, at + PLANES * y : at + PLANES * y + 8]
                b = got[2 * t + 1, at + PLANES * y : at + PLANES * y + 8]
                out[i, y, 8 * t : 8 * t + 8] = jnp.where(low, a, pltpu.roll(b, 4, 0))
                out[i, y + 1, 8 * t : 8 * t + 8] = jnp.where(low, pltpu.roll(a, 4, 0), b)

    tall, part = (STRIP + 2 * EDGE) * PLANES, PART * PLANES
    for i in range(2):
        widen(state, i, i * tall, STRIP + 2 * EDGE)
    for i in range(3):
        widen(coefficients, i, 2 * tall + i * part, PART)


def restore_kernel(got, out):
    core, _, slab = position()
    for part in range(2):
        half = core if part == 0 else 1 - core
        for place in range(BRICKS):
            first = pl.multiple_of(STRIP * placed(place, slab // 2) + HALF * half, HALF)
            for i in range(2):
                for plane in range(PLANES):
                    at = (part * 2 + i) * HALF * PLANES + plane
                    out[0, i, plane, pl.ds(first, HALF), :] = got[ORDER[place], pl.ds(at, HALF, stride=PLANES), :]


def sweep_rows(first, count, state, weights, earlier, into, step, source):
    centres = [[state[i, first - 1 + k] for k in range(count + 2)] for i in range(2)]
    for u in range(count):
        y = first + u
        for i in range(2):
            v = centres[i][u + 1]
            w = lambda k: weights[y, PAIR * i + k]
            along = w(0) * pltpu.roll(v, 1, 0) + w(1) * pltpu.roll(v, NX - 1, 0)
            middle = w(2) * centres[i][u] + w(3) * centres[i][u + 2]
            across = w(4) * pltpu.roll(v, 1, 1) + w(5) * pltpu.roll(v, LAST - 1, 1)
            begin = v if earlier is None else earlier[i, y]
            if step == COARSE:
                begin = (1.0 / COARSE_FACTOR) * begin
            gain = (along + middle) + (across + (w(6) * centres[1 - i][u + 1] + begin))
            if i == 1 and source is not None:
                gain = jnp.concatenate([gain[:8] + source[y], gain[8:]], axis=0)
            into[i, y] = (1.0 - DAMPING) * v + w(step) * gain


def sweep(state, weights, earlier, into, low, count, step, source=None):
    pieces = -(-count // LONGEST)
    size = -(-count // pieces)
    whole = count // size

    def piece(first, rows):
        sweep_rows(first, rows, state, weights, earlier, into, step, source)

    if whole > 1:

        def one(k, carry):
            piece(low + k * size, size)
            return carry

        lax.fori_loop(0, whole, one, 0)
    else:
        piece(low, size)
    if count > whole * size:
        piece(low + whole * size, count - whole * size)


def advances(many, e, v, weights, low, count, step, source=None):
    for m in range(many):
        sweep(e, weights, None, v, low + 2 * m + 1, count - 4 * m - 2, step, source)
        sweep(v, weights, e, e, low + 2 * m + 2, count - 4 * m - 4, step, source)


def weigh(first, count, c, offset, inlet, w, feed):
    _, strip, _ = position()
    plane = lax.broadcasted_iota(jnp.int32, (NX, LAST), 0)
    column = lax.broadcasted_iota(jnp.int32, (NX, LAST), 1)
    top = lax.broadcasted_iota(jnp.int32, (8, LAST), 0) == 0

    def row(r):
        at = r - offset
        y = strip * STRIP - EDGE + r
        lower = jnp.where(y == 0, 0.0, 1.0).astype(F32)
        upper = jnp.where(y == MIDDLE - 1, 0.0, 1.0).astype(F32)
        exchange = c[2, at]
        warmth = inlet[pl.ds(jnp.clip(y, 0, MIDDLE - 1), 1), :]
        for i in range(2):
            here = c[i, at]
            xm = jnp.where(plane == 0, 0.0, pltpu.roll(here, 1, 0))
            xp = jnp.where(plane == NX - 1, 0.0, pltpu.roll(here, NX - 1, 0))
            zm = jnp.where(column == 0, 0.0, pltpu.roll(here, 1, 1))
            zp = jnp.where(column == LAST - 1, 0.0, pltpu.roll(here, LAST - 1, 1))
            half_along, half_across = 0.5 * RATE_ALONG, 0.5 * RATE_ACROSS
            wxm = half_along * (here + xm)
            if i == 1:
                wxm = wxm + ADVECTION
            wxp = half_along * (here + xp)
            wym = half_across * (here + c[i, at - 1])
            wyp = half_across * (here + c[i, at + 1])
            wzm = half_across * (here + zm)
            wzp = half_across * (here + zp)
            outflow = wxm + wxp + wym + wyp + wzm + wzp + exchange
            inner = (
                jnp.where(plane == 0, 0.0, wxm),
                jnp.where(plane == NX - 1, 0.0, wxp),
                wym * lower,
                wyp * upper,
                jnp.where(column == 0, 0.0, wzm),
                jnp.where(column == LAST - 1, 0.0, wzp),
                exchange,
            )
            for k in range(7):
                w[r, PAIR * i + k] = inner[k]
            w[r, PAIR * i + FINE] = DAMPING / (1.0 + outflow)
            w[r, PAIR * i + COARSE] = (DAMPING * COARSE_FACTOR) / (1.0 + COARSE_FACTOR * outflow)
            if i == 1:
                feed[r] = jnp.where(top, wxm[:8] * warmth, 0.0)

    def two(k, carry):
        row(first + 2 * k)
        row(first + 2 * k + 1)
        return carry

    lax.fori_loop(0, count // 2, two, 0)


def weigh_kernel(mine, inlet, w, feed):
    core, _, _ = position()
    weigh(PART * core + 1, PART - 2, mine, PART * core, inlet, w, feed)


def relax_kernel(begin, mine, other, inlet, w_mine, feed_mine, w, base, give, own, beyond, c, feed, e, v, e0):
    core, _, slab = position()
    c[:, pl.ds(PART * core, PART)] = mine[...]
    c[:, pl.ds(PART - PART * core, PART)] = other[...]
    e[...] = begin[...]
    e0[...] = begin[...]
    ready = pl.ds(PART * core + 1, PART - 2)
    feed[ready] = feed_mine[ready]
    weigh(PART - 1 - (PART - 2) * core, PART, c, 0, inlet, w, feed)

    sweep(e0, w, None, v, EDGE - 3, STRIP + 6, COARSE)
    sweep(v, w, e0, e0, EDGE - 2, STRIP + 4, COARSE)
    advances(4, e, v, w, 0, ROWS, FINE, feed)
    keep = jnp.where(slab == SLABS - 1, 0.0, 1.0).astype(F32)
    rows = pl.ds(EDGE - 2, STRIP + 4)
    e[:, rows] = e[:, rows] - keep * e0[:, rows]
    sweep(e, w, None, v, EDGE - 1, STRIP + 2, COARSE)
    sweep(v, w, e, e0, EDGE, STRIP, COARSE)
    joined = jnp.where(slab == SLABS - 2, 0.0, 1.0).astype(F32)
    near, far = pl.ds(EDGE, HALF), pl.ds(EDGE + HALF, HALF)
    base[...] = jnp.where(core == 0, joined * e0[:, near], e[:, far])
    give[...] = jnp.where(core == 0, joined * e0[:, far], e[:, near])
    own[...] = e[:, near]
    beyond[...] = e[:, far]


def place(core, state, middle, inward, outward):
    many, rim = inward.shape[1], outward.shape[1]
    state[:, pl.ds(middle + HALF - (HALF + many) * core, many)] = inward[...]
    state[:, pl.ds(middle - rim + (HALF + rim) * core, rim)] = outward[...]


def leap_kernel(joined, own, near, swapped, w, *refs):
    high, (odd, *refs) = (refs[0], refs[1:]) if joined else (None, refs)
    core, _, _ = position()
    middle = EDGE + HALF * core
    rows = pl.ds(middle, HALF)
    *more, e, v = refs
    reach = HALF if more else HALF // 2
    e[:, rows] = own[...]
    place(core, e, middle, swapped, near)
    advances(2, e, v, w, middle - reach, HALF + 2 * reach, COARSE)
    odd[...] = e[:, rows]
    if more:
        (even,) = more
        advances(2, e, v, w, middle - 4, HALF + 8, COARSE)
        even[...] = e[:, rows] + high[...] if joined else e[:, rows]


def first_half_kernel(own, near, swapped, w, odd, state, e, v):
    core, _, _ = position()
    middle = EDGE + HALF * core
    e[:, pl.ds(middle, HALF)] = own[...]
    place(core, e, middle, swapped, near)
    advances(2, e, v, w, middle - HALF, 3 * HALF, COARSE)
    odd[...] = e[:, pl.ds(middle, HALF)]
    state[...] = e[:, pl.ds(middle - 4, HALF + 8)]


def second_half_kernel(state, w, even, inner, outer, e, v):
    core, _, _ = position()
    middle = EDGE + HALF * core
    e[:, pl.ds(middle - 4, HALF + 8)] = state[...]
    advances(2, e, v, w, middle - 4, HALF + 8, COARSE)
    even[...] = e[:, pl.ds(middle, HALF)]
    inner[...] = even[:, pl.ds(4 - 4 * core, 4)]
    outer[...] = even[:, pl.ds(4 * core, 4)]


def choose_kernel(ours, across, low, high):
    _, _, slab = position()
    chip = slab // 2
    stays = (chip < RING - 1) | (chip == CHIPS - 1)
    low[...] = jnp.where(stays, ours[...], across[...])
    high[...] = jnp.where(stays, across[...], ours[...])


def share_kernel(*refs):
    *arrived, out, inner, outer = refs
    core, _, slab = position()
    chip = slab // 2
    late = chip // RING
    total = 0.0
    for power, ref in enumerate(arrived):
        target = lax.rem(chip + 2 * RING - power, RING) + power
        total = total + jnp.where((target // RING == late) & (target < 2 * RING), ref[...], 0.0)
    out[...] = total
    inner[...] = out[:, pl.ds(6 - 6 * core, 2)]
    outer[...] = out[:, pl.ds(6 * core, 2)]


def last_kernel(own, near, swapped, g, taken, w, keep, send, r, v, e):
    core, _, _ = position()
    middle = EDGE + HALF * core
    rows = pl.ds(middle, HALF)
    r[:, rows] = own[...]
    place(core, r, middle, swapped, near)
    sweep(r, w, None, v, middle - 1, HALF + 2, COARSE)
    sweep(v, w, r, e, middle, HALF, COARSE)
    e[:, rows] = e[:, rows] + jnp.where(core == 0, g[...], taken[...])
    low = lax.broadcasted_iota(jnp.int32, (8, LAST), 0) < PLANES
    for out, other in ((keep, 0), (send, 1)):
        pick = lambda *at: jnp.where(core == other, r[at], e[at])
        for i in range(2):
            for y in range(0, HALF, 2):
                at = (i * HALF + y) * PLANES
                for t in range(NX // 8):
                    a = pick(i, middle + y, slice(8 * t, 8 * t + 8))
                    b = pick(i, middle + y + 1, slice(8 * t, 8 * t + 8))
                    out[2 * t, at : at + 8] = jnp.where(low, a, pltpu.roll(b, 4, 0))
                    out[2 * t + 1, at : at + 8] = jnp.where(low, pltpu.roll(a, 4, 0), b)


def index(chip, core, strip):
    return (chip * 2 + core) * BRICKS + ORDER[strip if chip < RING else BRICKS - 1 - strip]


def sent(value, chips, flip, shift):
    pairs = []
    for source, target in chips:
        for core in range(2):
            for strip in range(BRICKS):
                beside = (strip + shift * (1 if core == 0 else -1)) % BRICKS
                pairs.append((index(source, core ^ flip, strip), index(target, core, beside)))
    return lax.ppermute(value, AXES, pairs)


SAME = [(c, c) for c in range(CHIPS)]
ACROSS = [((c + RING) % CHIPS, c) for c in range(CHIPS)]


def along(value, power):
    pairs = [(c, c // RING * RING + (c + 1 + power) % RING) for c in range(CHIPS)]
    return sent(value, pairs, 0, 0)


def swap(value):
    return sent(value, SAME, 1, 0)


def beside(value):
    return sent(value, SAME, 1, 1)


def exchanged(own, inner, outer, *arrived):
    return lax.optimization_barrier((own, beside(outer), swap(inner)) + arrived)


def shards(startup, guess, conduct, couple, inlet):
    chunk = (2 * ROWS + 3 * PART) * PLANES
    half = shape(2, HALF, NX, LAST)
    arrays = [pltpu.with_memory_space_constraint(a, pltpu.HBM) for a in (startup, guess, conduct, couple)]
    packed = call(
        pack_kernel,
        shape(BRICKS, chunk, LAST),
        [HBM] * 4,
        VMEM,
        [
            pltpu.VMEM((5, (MIDDLE + 2 * EDGE) * PLANES, LAST), F32),
            pltpu.VMEM((2, PLANES, MIDDLE, LAST), F32),
            pltpu.VMEM((3, PLANES, MIDDLE, LAST), F32),
            pltpu.SemaphoreType.DMA((5,)),
        ],
        16,
    )(*arrays)
    got = lax.all_to_all(packed, "space", 0, 0, tiled=True)
    begin, mine = call(
        unpack_kernel, (shape(2, ROWS, NX, LAST), shape(3, PART, NX, LAST)), [VMEM], (VMEM, VMEM), [], 16
    )(got)
    other = swap(mine)

    field = pltpu.VMEM((2, ROWS, NX, LAST), F32)
    all_weights = pltpu.VMEM((ROWS, 2 * PAIR, NX, LAST), F32)
    weights, feed = call(
        weigh_kernel, (all_weights, shape(ROWS, 8, LAST)), [VMEM] * 2, (VMEM,) * 2, [], 16, 3
    )(mine, inlet)
    weights, base, give, g, beyond = call(
        relax_kernel,
        (all_weights, half, half, half, half),
        [VMEM] * 6,
        (VMEM,) * 5,
        [pltpu.VMEM((3, ROWS, NX, LAST), F32), pltpu.VMEM((ROWS, 8, LAST), F32), field, field, field],
        24,
        aliases={4: 0},
    )(begin, mine, other, inlet, weights, feed)
    u = base + swap(give)

    def leap(own, near, swapped, second=True, high=None):
        outs = (half,) * (1 + second)
        operands = [own, near, swapped, weights] + ([] if high is None else [high])
        body = functools.partial(leap_kernel, high is not None)
        return call(body, outs, [VMEM] * len(operands), (VMEM,) * len(outs), [field, field], 20, 2 + 3 * second)(*operands)

    low, high = call(choose_kernel, (half, half), [VMEM] * 2, (VMEM,) * 2, [], 8)(u, sent(u, ACROSS, 0, 0))
    rim4, rim2 = shape(2, 4, NX, LAST), shape(2, 2, NX, LAST)
    a0 = along(low, 0)
    u1, u2 = leap(*exchanged(low, low, low))
    a1, a2, taken = along(u1, 1), along(u2, 2), swap(beyond)
    *operands, a0, taken = exchanged(u2, u2, u2, a0, taken)
    u3, u4 = leap(*operands, high=high)
    a4 = along(u4, 4)
    *operands, a1, a2 = exchanged(u4, u4, u4, a1, a2)
    u5, state = call(
        first_half_kernel, (half, shape(2, 2 * HALF, NX, LAST)), [VMEM] * 4, (VMEM,) * 2, [field, field], 20, 2
    )(*operands, weights)
    a5 = along(u5, 5)
    u6, inner, outer = call(
        second_half_kernel, (half, rim4, rim4), [VMEM] * 2, (VMEM,) * 3, [field, field], 20, 2
    )(state, weights)
    a6 = along(u6, 6)
    *operands, a4, a5 = exchanged(u6, inner, outer, a4, a5)
    (u7,) = leap(*operands, second=False)
    c, inner, outer = call(share_kernel, (half, rim2, rim2), [VMEM] * 8, (VMEM,) * 3, [], 16)(
        a0, a1, a2, u3, a4, a5, a6, u7
    )
    parcel = shape(BRICKS, 2 * HALF * PLANES, LAST)
    keep, send = call(last_kernel, (parcel, parcel), [VMEM] * 6, (VMEM,) * 2, [field, field, field], 22)(
        c, beside(outer), swap(inner), g, taken, weights
    )
    back = lax.all_to_all(jnp.concatenate([keep, swap(send)], axis=1), "space", 0, 0, tiled=True)
    return call(restore_kernel, shape(1, 2, PLANES, MIDDLE, LAST), [VMEM], VMEM, [], 16)(back)


def solution(mesh):
    fine = Mesh(mesh.devices.reshape(SLABS // 2, 2, BRICKS), AXES)
    slabs = ("chip", "core")
    return jax.shard_map(
        shards,
        mesh=fine,
        in_specs=(
            P(None, "space", None, None),
            P(slabs, None, "space", None, None),
            P(None, "space", None, None),
            P("space", None, None),
            P(),
        ),
        out_specs=P(slabs, None, "space", None, None),
        check_vma=False,
    )
```

```python
import functools

import jax
import jax.numpy as jnp
from jax import lax
from jax.experimental import pallas as pl
from jax.experimental.pallas import tpu as pltpu
from jax.sharding import Mesh, PartitionSpec as P

SLABS = 16
BRICKS = 8
PLANES = 4
NX = 32
MIDDLE = 128
LAST = 128
STRIP = 16
CHIPS = SLABS // 2
RING = 4
HALF = 8
EDGE = 10
ROWS = STRIP + 2 * EDGE
LONGEST = 22
PART = ROWS // 2

RATE_ALONG = 4.0
RATE_ACROSS = 0.5
ADVECTION = 1.0
DAMPING = 0.8
COARSE_FACTOR = 4.0

ORDER = [0, 2, 4, 6, 7, 5, 3, 1]
AXES = ("chip", "core", "space")
MIB = 1 << 20

VMEM = pl.BlockSpec(memory_space=pltpu.VMEM)
HBM = pl.BlockSpec(memory_space=pltpu.HBM)
PAIR = 9
FINE, COARSE = 7, 8
F32 = jnp.float32


def shape(*dims):
    return jax.ShapeDtypeStruct(dims, F32)


def call(body, outs, in_specs, out_specs, scratch, limit, us=1, aliases={}):
    return pl.pallas_call(
        body,
        input_output_aliases=aliases,
        cost_estimate=pl.CostEstimate(flops=0, bytes_accessed=us * (3 << 20), transcendentals=0),
        out_shape=outs,
        in_specs=in_specs,
        out_specs=out_specs,
        scratch_shapes=scratch,
        compiler_params=pltpu.CompilerParams(vmem_limit_bytes=limit * MIB),
    )


def position():
    chip, core, space = (lax.axis_index(a) for a in AXES)
    y, odd = space // 2, space % 2
    return core, placed(jnp.where(odd == 0, y, BRICKS - 1 - y), chip), chip * 2 + core


def placed(place, chip):
    return jnp.where(chip < RING, place, BRICKS - 1 - place)


def pack_kernel(startup, guess, conduct, couple, out, padded, state, others, sems):
    core, _, slab = position()
    last = slab == SLABS - 1
    from_startup = [pltpu.make_async_copy(startup.at[i], state.at[i], sems.at[i]) for i in range(2)]
    from_guess = [pltpu.make_async_copy(guess.at[0, i], state.at[i], sems.at[i]) for i in range(2)]
    copies = [pltpu.make_async_copy(conduct.at[i], others.at[i], sems.at[2 + i]) for i in range(2)]
    copies.append(pltpu.make_async_copy(couple, others.at[2], sems.at[4]))

    @pl.when(last)
    def _():
        for copy in from_startup:
            copy.start()

    @pl.when(jnp.logical_not(last))
    def _():
        for copy in from_guess:
            copy.start()

    for copy in copies:
        copy.start()
    zero = jnp.zeros((EDGE * PLANES, LAST), F32)
    end = (EDGE + MIDDLE) * PLANES
    for i in range(5):
        padded[i, 0 : EDGE * PLANES] = zero
        padded[i, end : end + EDGE * PLANES] = zero
        (from_guess + copies)[i].wait()
        for plane in range(PLANES):
            for first in range(0, MIDDLE, 8):
                value = state[i, plane, first : first + 8] if i < 2 else others[i - 2, plane, first : first + 8]
                padded[i, pl.ds((EDGE + first) * PLANES + plane, 8, stride=PLANES), :] = value
    tall, part = (STRIP + 2 * EDGE) * PLANES, PART * PLANES
    for place in range(BRICKS):
        s = ORDER[place]
        start = pl.multiple_of(STRIP * PLANES * placed(place, slab // 2), 64)
        for i in range(2):
            out[s, i * tall : (i + 1) * tall] = padded[i, pl.ds(start, tall)]
        start = pl.multiple_of(start + part * core, 8)
        for i in range(3):
            at = 2 * tall + i * part
            out[s, at : at + part] = padded[2 + i, pl.ds(start, part)]


def unpack_kernel(got, state, coefficients):
    low = lax.broadcasted_iota(jnp.int32, (8, LAST), 0) < PLANES

    def widen(out, i, at, rows):
        for y in range(0, rows, 2):
            for t in range(NX // 8):
                a = got[2 * t, at + PLANES * y : at + PLANES * y + 8]
                b = got[2 * t + 1, at + PLANES * y : at + PLANES * y + 8]
                out[i, y, 8 * t : 8 * t + 8] = jnp.where(low, a, pltpu.roll(b, 4, 0))
                out[i, y + 1, 8 * t : 8 * t + 8] = jnp.where(low, pltpu.roll(a, 4, 0), b)

    tall, part = (STRIP + 2 * EDGE) * PLANES, PART * PLANES
    for i in range(2):
        widen(state, i, i * tall, STRIP + 2 * EDGE)
    for i in range(3):
        widen(coefficients, i, 2 * tall + i * part, PART)


def restore_kernel(got, out):
    core, _, slab = position()
    for part in range(2):
        half = core if part == 0 else 1 - core
        for place in range(BRICKS):
            first = pl.multiple_of(STRIP * placed(place, slab // 2) + HALF * half, HALF)
            for i in range(2):
                for plane in range(PLANES):
                    at = (part * 2 + i) * HALF * PLANES + plane
                    out[0, i, plane, pl.ds(first, HALF), :] = got[ORDER[place], pl.ds(at, HALF, stride=PLANES), :]


def sweep_rows(first, count, state, weights, earlier, into, step, source):
    centres = [[state[i, first - 1 + k] for k in range(count + 2)] for i in range(2)]
    for u in range(count):
        y = first + u
        for i in range(2):
            v = centres[i][u + 1]
            w = lambda k: weights[y, PAIR * i + k]
            along = w(0) * pltpu.roll(v, 1, 0) + w(1) * pltpu.roll(v, NX - 1, 0)
            middle = w(2) * centres[i][u] + w(3) * centres[i][u + 2]
            across = w(4) * pltpu.roll(v, 1, 1) + w(5) * pltpu.roll(v, LAST - 1, 1)
            begin = v if earlier is None else earlier[i, y]
            if step == COARSE:
                begin = (1.0 / COARSE_FACTOR) * begin
            gain = (along + middle) + (across + (w(6) * centres[1 - i][u + 1] + begin))
            if i == 1 and source is not None:
                gain = jnp.concatenate([gain[:8] + source[y], gain[8:]], axis=0)
            into[i, y] = (1.0 - DAMPING) * v + w(step) * gain


def sweep(state, weights, earlier, into, low, count, step, source=None):
    pieces = -(-count // LONGEST)
    size = -(-count // pieces)
    whole = count // size

    def piece(first, rows):
        sweep_rows(first, rows, state, weights, earlier, into, step, source)

    if whole > 1:

        def one(k, carry):
            piece(low + k * size, size)
            return carry

        lax.fori_loop(0, whole, one, 0)
    else:
        piece(low, size)
    if count > whole * size:
        piece(low + whole * size, count - whole * size)


def advances(many, e, v, weights, low, count, step, source=None):
    for m in range(many):
        sweep(e, weights, None, v, low + 2 * m + 1, count - 4 * m - 2, step, source)
        sweep(v, weights, e, e, low + 2 * m + 2, count - 4 * m - 4, step, source)


def weigh(first, count, c, offset, inlet, w, feed):
    _, strip, _ = position()
    plane = lax.broadcasted_iota(jnp.int32, (NX, LAST), 0)
    column = lax.broadcasted_iota(jnp.int32, (NX, LAST), 1)
    top = lax.broadcasted_iota(jnp.int32, (8, LAST), 0) == 0

    def row(r):
        at = r - offset
        y = strip * STRIP - EDGE + r
        lower = jnp.where(y == 0, 0.0, 1.0).astype(F32)
        upper = jnp.where(y == MIDDLE - 1, 0.0, 1.0).astype(F32)
        exchange = c[2, at]
        warmth = inlet[pl.ds(jnp.clip(y, 0, MIDDLE - 1), 1), :]
        for i in range(2):
            here = c[i, at]
            xm = jnp.where(plane == 0, 0.0, pltpu.roll(here, 1, 0))
            xp = jnp.where(plane == NX - 1, 0.0, pltpu.roll(here, NX - 1, 0))
            zm = jnp.where(column == 0, 0.0, pltpu.roll(here, 1, 1))
            zp = jnp.where(column == LAST - 1, 0.0, pltpu.roll(here, LAST - 1, 1))
            half_along, half_across = 0.5 * RATE_ALONG, 0.5 * RATE_ACROSS
            wxm = half_along * (here + xm)
            if i == 1:
                wxm = wxm + ADVECTION
            wxp = half_along * (here + xp)
            wym = half_across * (here + c[i, at - 1])
            wyp = half_across * (here + c[i, at + 1])
            wzm = half_across * (here + zm)
            wzp = half_across * (here + zp)
            outflow = wxm + wxp + wym + wyp + wzm + wzp + exchange
            inner = (
                jnp.where(plane == 0, 0.0, wxm),
                jnp.where(plane == NX - 1, 0.0, wxp),
                wym * lower,
                wyp * upper,
                jnp.where(column == 0, 0.0, wzm),
                jnp.where(column == LAST - 1, 0.0, wzp),
                exchange,
            )
            for k in range(7):
                w[r, PAIR * i + k] = inner[k]
            w[r, PAIR * i + FINE] = DAMPING / (1.0 + outflow)
            w[r, PAIR * i + COARSE] = (DAMPING * COARSE_FACTOR) / (1.0 + COARSE_FACTOR * outflow)
            if i == 1:
                feed[r] = jnp.where(top, wxm[:8] * warmth, 0.0)

    def two(k, carry):
        row(first + 2 * k)
        row(first + 2 * k + 1)
        return carry

    lax.fori_loop(0, count // 2, two, 0)


def weigh_kernel(mine, inlet, w, feed):
    core, _, _ = position()
    weigh(PART * core + 1, PART - 2, mine, PART * core, inlet, w, feed)


def relax_kernel(begin, mine, other, inlet, w_mine, feed_mine, w, base, give, own, beyond, c, feed, e, v, e0):
    core, _, slab = position()
    c[:, pl.ds(PART * core, PART)] = mine[...]
    c[:, pl.ds(PART - PART * core, PART)] = other[...]
    e[...] = begin[...]
    e0[...] = begin[...]
    ready = pl.ds(PART * core + 1, PART - 2)
    feed[ready] = feed_mine[ready]
    weigh(PART - 1 - (PART - 2) * core, PART, c, 0, inlet, w, feed)

    sweep(e0, w, None, v, EDGE - 3, STRIP + 6, COARSE)
    sweep(v, w, e0, e0, EDGE - 2, STRIP + 4, COARSE)
    advances(4, e, v, w, 0, ROWS, FINE, feed)
    keep = jnp.where(slab == SLABS - 1, 0.0, 1.0).astype(F32)
    rows = pl.ds(EDGE - 2, STRIP + 4)
    e[:, rows] = e[:, rows] - keep * e0[:, rows]
    sweep(e, w, None, v, EDGE - 1, STRIP + 2, COARSE)
    sweep(v, w, e, e0, EDGE, STRIP, COARSE)
    joined = jnp.where(slab == SLABS - 2, 0.0, 1.0).astype(F32)
    near, far = pl.ds(EDGE, HALF), pl.ds(EDGE + HALF, HALF)
    base[...] = jnp.where(core == 0, joined * e0[:, near], e[:, far])
    give[...] = jnp.where(core == 0, joined * e0[:, far], e[:, near])
    own[...] = e[:, near]
    beyond[...] = e[:, far]


def place(core, state, middle, inward, outward):
    many, rim = inward.shape[1], outward.shape[1]
    state[:, pl.ds(middle + HALF - (HALF + many) * core, many)] = inward[...]
    state[:, pl.ds(middle - rim + (HALF + rim) * core, rim)] = outward[...]


def leap_kernel(joined, own, near, swapped, w, *refs):
    high, (odd, *refs) = (refs[0], refs[1:]) if joined else (None, refs)
    core, _, _ = position()
    middle = EDGE + HALF * core
    rows = pl.ds(middle, HALF)
    *more, e, v = refs
    reach = HALF if more else HALF // 2
    e[:, rows] = own[...]
    place(core, e, middle, swapped, near)
    advances(2, e, v, w, middle - reach, HALF + 2 * reach, COARSE)
    odd[...] = e[:, rows]
    if more:
        (even,) = more
        advances(2, e, v, w, middle - 4, HALF + 8, COARSE)
        even[...] = e[:, rows] + high[...] if joined else e[:, rows]


def first_half_kernel(own, near, swapped, w, odd, state, e, v):
    core, _, _ = position()
    middle = EDGE + HALF * core
    e[:, pl.ds(middle, HALF)] = own[...]
    place(core, e, middle, swapped, near)
    advances(2, e, v, w, middle - HALF, 3 * HALF, COARSE)
    odd[...] = e[:, pl.ds(middle, HALF)]
    state[...] = e[:, pl.ds(middle - 4, HALF + 8)]


def second_half_kernel(state, w, even, inner, outer, e, v):
    core, _, _ = position()
    middle = EDGE + HALF * core
    e[:, pl.ds(middle - 4, HALF + 8)] = state[...]
    advances(2, e, v, w, middle - 4, HALF + 8, COARSE)
    even[...] = e[:, pl.ds(middle, HALF)]
    inner[...] = even[:, pl.ds(4 - 4 * core, 4)]
    outer[...] = even[:, pl.ds(4 * core, 4)]


def choose_kernel(ours, across, low, high):
    _, _, slab = position()
    chip = slab // 2
    stays = (chip < RING - 1) | (chip == CHIPS - 1)
    low[...] = jnp.where(stays, ours[...], across[...])
    high[...] = jnp.where(stays, across[...], ours[...])


def share_kernel(*refs):
    *arrived, out, inner, outer = refs
    core, _, slab = position()
    chip = slab // 2
    late = chip // RING
    total = 0.0
    for power, ref in enumerate(arrived):
        target = lax.rem(chip + 2 * RING - power, RING) + power
        total = total + jnp.where((target // RING == late) & (target < 2 * RING), ref[...], 0.0)
    out[...] = total
    inner[...] = out[:, pl.ds(6 - 6 * core, 2)]
    outer[...] = out[:, pl.ds(6 * core, 2)]


def last_kernel(own, near, swapped, g, taken, w, keep, send, r, v, e):
    core, _, _ = position()
    middle = EDGE + HALF * core
    rows = pl.ds(middle, HALF)
    r[:, rows] = own[...]
    place(core, r, middle, swapped, near)
    sweep(r, w, None, v, middle - 1, HALF + 2, COARSE)
    sweep(v, w, r, e, middle, HALF, COARSE)
    e[:, rows] = e[:, rows] + jnp.where(core == 0, g[...], taken[...])
    low = lax.broadcasted_iota(jnp.int32, (8, LAST), 0) < PLANES
    for out, other in ((keep, 0), (send, 1)):
        pick = lambda *at: jnp.where(core == other, r[at], e[at])
        for i in range(2):
            for y in range(0, HALF, 2):
                at = (i * HALF + y) * PLANES
                for t in range(NX // 8):
                    a = pick(i, middle + y, slice(8 * t, 8 * t + 8))
                    b = pick(i, middle + y + 1, slice(8 * t, 8 * t + 8))
                    out[2 * t, at : at + 8] = jnp.where(low, a, pltpu.roll(b, 4, 0))
                    out[2 * t + 1, at : at + 8] = jnp.where(low, pltpu.roll(a, 4, 0), b)


def index(chip, core, strip):
    return (chip * 2 + core) * BRICKS + ORDER[strip if chip < RING else BRICKS - 1 - strip]


def sent(value, chips, flip, shift):
    pairs = []
    for source, target in chips:
        for core in range(2):
            for strip in range(BRICKS):
                beside = (strip + shift * (1 if core == 0 else -1)) % BRICKS
                pairs.append((index(source, core ^ flip, strip), index(target, core, beside)))
    return lax.ppermute(value, AXES, pairs)


SAME = [(c, c) for c in range(CHIPS)]
ACROSS = [((c + RING) % CHIPS, c) for c in range(CHIPS)]


def along(value, power):
    pairs = [(c, c // RING * RING + (c + 1 + power) % RING) for c in range(CHIPS)]
    return sent(value, pairs, 0, 0)


def swap(value):
    return sent(value, SAME, 1, 0)


def beside(value):
    return sent(value, SAME, 1, 1)


def exchanged(own, inner, outer, *arrived):
    return lax.optimization_barrier((own, beside(outer), swap(inner)) + arrived)


def shards(startup, guess, conduct, couple, inlet):
    chunk = (2 * ROWS + 3 * PART) * PLANES
    half = shape(2, HALF, NX, LAST)
    arrays = [pltpu.with_memory_space_constraint(a, pltpu.HBM) for a in (startup, guess, conduct, couple)]
    packed = call(
        pack_kernel,
        shape(BRICKS, chunk, LAST),
        [HBM] * 4,
        VMEM,
        [
            pltpu.VMEM((5, (MIDDLE + 2 * EDGE) * PLANES, LAST), F32),
            pltpu.VMEM((2, PLANES, MIDDLE, LAST), F32),
            pltpu.VMEM((3, PLANES, MIDDLE, LAST), F32),
            pltpu.SemaphoreType.DMA((5,)),
        ],
        16,
    )(*arrays)
    got = lax.all_to_all(packed, "space", 0, 0, tiled=True)
    begin, mine = call(
        unpack_kernel, (shape(2, ROWS, NX, LAST), shape(3, PART, NX, LAST)), [VMEM], (VMEM, VMEM), [], 16
    )(got)
    other = swap(mine)

    field = pltpu.VMEM((2, ROWS, NX, LAST), F32)
    all_weights = pltpu.VMEM((ROWS, 2 * PAIR, NX, LAST), F32)
    weights, feed = call(
        weigh_kernel, (all_weights, shape(ROWS, 8, LAST)), [VMEM] * 2, (VMEM,) * 2, [], 16, 3
    )(mine, inlet)
    weights, base, give, g, beyond = call(
        relax_kernel,
        (all_weights, half, half, half, half),
        [VMEM] * 6,
        (VMEM,) * 5,
        [pltpu.VMEM((3, ROWS, NX, LAST), F32), pltpu.VMEM((ROWS, 8, LAST), F32), field, field, field],
        24,
        aliases={4: 0},
    )(begin, mine, other, inlet, weights, feed)
    u = base + swap(give)

    def leap(own, near, swapped, second=True, high=None):
        outs = (half,) * (1 + second)
        operands = [own, near, swapped, weights] + ([] if high is None else [high])
        body = functools.partial(leap_kernel, high is not None)
        return call(body, outs, [VMEM] * len(operands), (VMEM,) * len(outs), [field, field], 20, 2 + 3 * second)(*operands)

    low, high = call(choose_kernel, (half, half), [VMEM] * 2, (VMEM,) * 2, [], 8)(u, sent(u, ACROSS, 0, 0))
    rim4, rim2 = shape(2, 4, NX, LAST), shape(2, 2, NX, LAST)
    a0 = along(low, 0)
    u1, u2 = leap(*exchanged(low, low, low))
    a1, a2, taken = along(u1, 1), along(u2, 2), swap(beyond)
    *operands, a0, taken = exchanged(u2, u2, u2, a0, taken)
    u3, u4 = leap(*operands, high=high)
    a4 = along(u4, 4)
    *operands, a1 = exchanged(u4, u4, u4, a1)
    u5, state = call(
        first_half_kernel, (half, shape(2, 2 * HALF, NX, LAST)), [VMEM] * 4, (VMEM,) * 2, [field, field], 20, 2
    )(*operands, weights)
    a5 = along(u5, 5)
    u6, inner, outer = call(
        second_half_kernel, (half, rim4, rim4), [VMEM] * 2, (VMEM,) * 3, [field, field], 20, 2
    )(state, weights)
    a6 = along(u6, 6)
    *operands, a2, a4, a5 = exchanged(u6, inner, outer, a2, a4, a5)
    (u7,) = leap(*operands, second=False)
    c, inner, outer = call(share_kernel, (half, rim2, rim2), [VMEM] * 8, (VMEM,) * 3, [], 16)(
        a0, a1, a2, u3, a4, a5, a6, u7
    )
    parcel = shape(BRICKS, 2 * HALF * PLANES, LAST)
    keep, send = call(last_kernel, (parcel, parcel), [VMEM] * 6, (VMEM,) * 2, [field, field, field], 22)(
        c, beside(outer), swap(inner), g, taken, weights
    )
    back = lax.all_to_all(jnp.concatenate([keep, swap(send)], axis=1), "space", 0, 0, tiled=True)
    return call(restore_kernel, shape(1, 2, PLANES, MIDDLE, LAST), [VMEM], VMEM, [], 16)(back)


def solution(mesh):
    fine = Mesh(mesh.devices.reshape(SLABS // 2, 2, BRICKS), AXES)
    slabs = ("chip", "core")
    return jax.shard_map(
        shards,
        mesh=fine,
        in_specs=(
            P(None, "space", None, None),
            P(slabs, None, "space", None, None),
            P(None, "space", None, None),
            P("space", None, None),
            P(),
        ),
        out_specs=P(slabs, None, "space", None, None),
        check_vma=False,
    )
```
